256 devices in a mesh: dp: 4 (over z_lo), space: 8 (over x, z_hi), tensor: 8 (over y, core).
Axes of the slice: x: 4, y: 4, z: 8 (z_hi: 2, z_lo: 4; z = z_hi * 4 + z_lo), core: 2. Of those that a mesh axis runs over, the one named last changes fastest.
Arguments:
- features: bfloat16 [4, 128, 64, 1024], P('dp', ('space', 'tensor')), may hold values from -6 to 6
- kernel: bfloat16 [3, 3, 1024, 1024], P(None, None, 'tensor'), may hold values from -0.0625 to 0.0625
- embedding: float32 [1000, 1024], P(None, 'tensor'), may hold values from -6 to 6
- labels: int32 [4], P('dp'), may hold values from 0 to 999
Outputs:
- weight_grad: float32 [3, 3, 1024, 1024], P(None, None, 'tensor')
- embed_grad: float32 [1000, 1024], P(None, 'tensor')
The draws below stay inside these ranges and needn't reach their ends.
All inputs are finite; a program needn't handle non-finite values.
Results may differ from the reference program's by a relative error of at most 0.00033.
Values may be sent and summed in bfloat16 or wider, within the bound.
No kernel may reach another device: no remote copies, remote signals or barrier semaphores. Data moves between devices by JAX's collectives and lax.ppermute only.
A program may use at most 64 MiB of HBM per device.

```python
import jax
import jax.numpy as jnp
from jax import lax

C = 1024
CLASSES = 1000
COLS = 64
IMAGES = 4
HEIGHT = 128


def with_ends(entries, own_key, smallest, largest):
    place = [jax.random.randint(jax.random.fold_in(own_key, axis), (), 0, length) for axis, length in enumerate(entries.shape)]
    main_axis = entries.shape.index(max(entries.shape))
    beside = place[:main_axis] + [(place[main_axis] + 1) % entries.shape[main_axis]] + place[main_axis + 1:]
    return entries.at[tuple(place)].set(smallest).at[tuple(beside)].set(largest)


def levels(own_key, shape, shards, least, high):
    loudness, own = 1.0, jax.random.fold_in(own_key, 6)
    for axis_at, blocks in shards:
        steps = jnp.exp(jax.random.uniform(jax.random.fold_in(own, axis_at), (blocks,), jnp.float32, least / len(shards), high / len(shards)))
        loudness = loudness * jnp.repeat(steps, shape[axis_at] // blocks).reshape([-1 if axis == axis_at else 1 for axis in range(len(shape))])
    return loudness


def gaussian(own_key, shape, spread, most, split=(), dtype=jnp.bfloat16):
    entries = jax.random.normal(own_key, shape, jnp.float32) * spread
    if len(split) > 0:
        entries = levels(own_key, shape, split, -0.22, 0.18) * entries
    return jnp.clip(entries, min=-most, max=most).astype(dtype)


def setup_inputs(seed: int = 0) -> dict:
    key_of = jax.random.split(jax.random.key(seed), 5)
    return {
        "features": gaussian(key_of[0], (IMAGES, HEIGHT, COLS, C), 1.0, 6.0, ((0, 4), (1, 64))),
        "kernel": gaussian(key_of[1], (3, 3, C, C), (9 * C) ** -0.5, 0.0625, ((2, 8),)),
        "embedding": gaussian(key_of[2], (CLASSES, C), 1.0, 6.0, ((1, 8),), jnp.float32),
        "labels": with_ends(jax.random.randint(key_of[3], (IMAGES,), 0, CLASSES), jax.random.fold_in(key_of[3], 1), 0, CLASSES - 1).astype(jnp.int32),
    }


r1_factor = 1000.0

def conv_valid(padded, kern):
    return lax.conv_general_dilated(padded, kern, (1, 1), 'VALID', dimension_numbers=('NHWC', 'HWIO', 'NHWC'), preferred_element_type=jnp.float32)

def pad_both(field):
    return jnp.pad(field, ((0, 0), (1, 1), (1, 1), (0, 0)))

def taps_of(padded, grad):
    row_count = grad.shape[1]
    col_count = grad.shape[2]
    flat_grad = grad.reshape(-1, grad.shape[3])
    outer = []
    for tap_row in range(3):
        inner = []
        for tap_col in range(3):
            window = padded[:, tap_row:tap_row + row_count, tap_col:tap_col + col_count, :].reshape(-1, padded.shape[3])
            inner.append(lax.dot_general(window, flat_grad, (((0,), (0,)), ((), ())), preferred_element_type=jnp.float32))
        outer.append(jnp.stack(inner))
    return jnp.stack(outer)

def reference(features, kernel, embedding, labels):
    scale = 1.0 / jnp.sqrt(jnp.float32(HEIGHT * COLS * C))
    gweight = r1_factor / IMAGES
    flipped = jnp.transpose(kernel[::-1, ::-1], (0, 1, 3, 2))

    def one_image(carry, inputs):
        wsum, esum = carry
        image, label = inputs
        x_pad = pad_both(image[None])
        hidden = conv_valid(x_pad, kernel)
        sig = jax.nn.sigmoid(hidden)
        act = hidden * sig
        slope = sig * (1.0 + hidden * (1.0 - sig))
        curve = sig * (1.0 - sig) * (2.0 + hidden * (1.0 - 2.0 * sig))
        embed_row = embedding[label]
        score = scale * jnp.sum(act * embed_row)
        coeff = -jax.nn.sigmoid(-score) / IMAGES
        grad_hidden = (embed_row * slope * scale).astype(jnp.bfloat16)
        grad_input = conv_valid(pad_both(grad_hidden), flipped).astype(jnp.bfloat16)
        gx_pad = pad_both(grad_input)
        second = conv_valid(gx_pad, kernel)
        pre = (coeff * embed_row * slope * scale + gweight * second * embed_row * curve * scale).astype(jnp.bfloat16)
        wgrad = taps_of(x_pad, pre) + gweight * taps_of(gx_pad, grad_hidden)
        vec = coeff * scale * lax.optimization_barrier(jnp.sum(act, axis=(0, 1, 2))) + gweight * scale * lax.optimization_barrier(jnp.sum(second * slope, axis=(0, 1, 2)))
        esum = esum.at[label].add(vec)
        return ((wsum + wgrad, esum), None)
    init = (jnp.zeros((3, 3, C, C), jnp.float32), jnp.zeros((CLASSES, C), jnp.float32))
    (wsum, esum), _ = lax.scan(one_image, init, (features, labels.astype(jnp.int32)))
    return (wsum, esum)
```

```python
import math

import jax
import jax.numpy as jnp
from jax import lax
from jax.experimental import pallas as pl
from jax.experimental.pallas import tpu as pltpu
from jax.sharding import PartitionSpec as P

r1_factor = 1000.0
BF = jnp.bfloat16
F32 = jnp.float32

IMAGES, HEIGHT, COLS, CHANS = 4, 128, 64, 1024
SCALE = 1.0 / math.sqrt(HEIGHT * COLS * CHANS)
GWEIGHT = r1_factor / IMAGES

CORE_SWAP = [(t, t ^ 1) for t in range(8)]
HI_SWAP = [(s, s ^ 1) for s in range(8)]
ORDER = (2, 1, 3)
Z_ORDER = (4, 3, 5, 2, 6, 1, 7)


def y_perm(d):
    return [(2 * y + c, 2 * ((y + d) % 4) + c) for y in range(4) for c in range(2)]


def x_perm(d):
    return [(2 * x + h, 2 * ((x + d) % 4) + h) for x in range(4) for h in range(2)]


def z_perm(d):
    pairs = []
    for z in range(8):
        w = (z + d) % 8
        for x in range(4):
            pairs.append(((z % 4) * 8 + 2 * x + z // 4, (w % 4) * 8 + 2 * x + w // 4))
    return pairs


def core_swap(v):
    return lax.ppermute(v, "tensor", CORE_SWAP)


def y_send(v, d):
    return lax.ppermute(v, "tensor", y_perm(d))


def x_send(v, d):
    return lax.ppermute(v, "space", x_perm(d))


def z_send(v, d):
    return lax.ppermute(v, ("dp", "space"), z_perm(d))


def place_of():
    t = lax.axis_index("tensor")
    s = lax.axis_index("space")
    lo = lax.axis_index("dp")
    return t // 2, lax.rem(t, 2), s, s // 2, 4 * lax.rem(s, 2) + lo, lo


def call(kernel, outs, scratch, *args, flops=0):
    vm = pl.BlockSpec(memory_space=pltpu.VMEM)
    total = sum(math.prod(a.shape) * a.dtype.itemsize for a in args)
    total += sum(math.prod(o.shape) * o.dtype.itemsize for o in outs)
    return pl.pallas_call(
        kernel,
        out_shape=tuple(outs),
        in_specs=[vm] * len(args),
        out_specs=tuple([vm] * len(outs)),
        scratch_shapes=scratch,
        compiler_params=pltpu.CompilerParams(vmem_limit_bytes=48 << 20),
        cost_estimate=pl.CostEstimate(flops=flops, bytes_accessed=total, transcendentals=0),
    )(*args)


def out(shape, dtype):
    return jax.ShapeDtypeStruct(shape, dtype)


def conv_rows(acc, source, rows, weight, contract):
    flat = source.reshape(source.shape[0] * COLS, CHANS)
    for b in range(3):
        total = None
        for a in range(3):
            part = lax.dot_general(
                flat[a * COLS : (a + rows) * COLS],
                weight(a, b),
                (((1,), (contract,)), ((), ())),
                preferred_element_type=F32,
            )
            total = part if total is None else total + part
        acc[b] = total.reshape(rows, COLS, 256)
    edge = jnp.zeros((rows, 1, 256), F32)
    left, right = acc[0], acc[2]
    return (
        acc[1]
        + jnp.concatenate([edge, left[:, : COLS - 1]], 1)
        + jnp.concatenate([right[:, 1:], edge], 1)
    )


def inside_rows(start, rows):
    row = start + lax.broadcasted_iota(jnp.int32, (rows, COLS, 256), 0)
    return (row >= 0) & (row < HEIGHT)


def hidden_kernel(*refs):
    mine, other = refs[0:4], refs[4:8]
    halo, r1, r2, r3, crossed = refs[8:13]
    kern, k1, k2, k3 = refs[13:17]
    kother = refs[17:21]
    e_ref = refs[21]
    gh_ref, hid_ref, stat_ref, x_ref, w_ref, acc = refs[22:28]
    y, c, s, _, _, _ = place_of()
    for d in range(4):
        at = lax.rem(y + 4 - d, 4)
        x_ref[pl.ds(3 + 4 * at + 2 * c, 2)] = mine[d][...]
        x_ref[pl.ds(3 + 4 * at + 2 * (1 - c), 2)] = other[d][...]
        for core, piece in ((c, (kern, k1, k2, k3)[d]), (1 - c, kother[d])):
            if piece is kern:
                block = kern[:, :, pl.ds(pl.multiple_of(y * 256, 256), 256)]
            else:
                block = piece[...]
            w_ref[:, pl.ds(pl.multiple_of((2 * at + core) * 128, 128), 128), :] = block
    for source, up, down in ((halo, 3, 0), (r1, 0, 1), (r2, 1, 2), (r3, 2, 3)):

        @pl.when((y == up) & (c == 0))
        def _():
            x_ref[0:1] = source[1:2]

        @pl.when((y == up) & (c == 1))
        def _():
            x_ref[2:3] = source[1:2]

        @pl.when((y == down) & (c == 0))
        def _():
            x_ref[19:20] = source[0:1]

        @pl.when((y == down) & (c == 1))
        def _():
            x_ref[21:22] = source[0:1]

    @pl.when(c == 0)
    def _():
        x_ref[1:3] = crossed[...]

    @pl.when(c == 1)
    def _():
        x_ref[19:21] = crossed[...]

    hidden = conv_rows(acc, x_ref[pl.ds(10 * c, 12)], 10, lambda a, b: w_ref[3 * a + b], 0)
    acc[0] = hidden
    sig = jax.nn.sigmoid(hidden)
    slope = sig * (1.0 + hidden * (1.0 - sig))
    e = e_ref[0:1, :].reshape(1, 1, 256)
    gh = jnp.where(inside_rows(16 * s - 2 + 10 * c, 10), e * slope * SCALE, 0.0)
    gh_ref[...] = gh.astype(BF)
    own = acc[0, pl.ds(2 - 2 * c, 8)]
    hid_ref[...] = own
    act = own * jax.nn.sigmoid(own)
    act_sum = jnp.sum(jnp.sum(act, axis=0), axis=0, keepdims=True)
    part = SCALE * jnp.sum(act_sum * e_ref[0:1, :])
    stat_ref[0:8] = jnp.broadcast_to(act_sum, (8, 256))
    stat_ref[8:16] = jnp.full((8, 256), part, F32)


def fill_rows(scratch, pieces, swapped, rows, y, c):
    for d in range(4):
        at = pl.multiple_of(lax.rem(y + 4 - d, 4) * 256, 256)
        scratch[pl.ds(c, rows), :, pl.ds(at, 256)] = pieces[d][...]
        scratch[pl.ds(rows * (1 - c), 1), :, pl.ds(at, 256)] = swapped[d : d + 1]


def input_kernel(p0, p1, p2, p3, swapped, kern, kother, gi_ref, full, acc):
    y, c, s, _, _, _ = place_of()
    fill_rows(full, (p0, p1, p2, p3), swapped, 10, y, c)

    def weight(a, b):
        tap = 3 * (2 - a) + 2 - b
        return jnp.concatenate([kern[tap], kother[tap]], 0)

    grad = conv_rows(acc, full[...], 9, weight, 1)
    turned = jnp.concatenate([grad[:, :, 128:], grad[:, :, :128]], 2)
    grad = jnp.where(c == 0, grad, turned)
    gi_ref[...] = jnp.where(inside_rows(16 * s - 1 + 9 * c, 9), grad, 0.0).astype(BF)


def second_kernel(
    p0, p1, p2, p3, swapped, w_ref, hid_ref, stat_ref, score, e_ref, pre_ref, vec_ref, full, acc
):
    y, c, _, _, _, _ = place_of()
    fill_rows(full, (p0, p1, p2, p3), swapped, 9, y, c)
    second = conv_rows(acc, full[...], 8, lambda a, b: w_ref[3 * a + b], 0)
    hidden = hid_ref[...]
    sig = jax.nn.sigmoid(hidden)
    slope = sig * (1.0 + hidden * (1.0 - sig))
    curve = sig * (1.0 - sig) * (2.0 + hidden * (1.0 - 2.0 * sig))
    e = e_ref[0:1, :].reshape(1, 1, 256)
    coeff = -jax.nn.sigmoid(-score[0:1, 0:1]) / IMAGES
    c3 = coeff.reshape(1, 1, 1)
    pre = c3 * e * slope * SCALE + GWEIGHT * second * e * curve * SCALE
    pre_ref[...] = pre.astype(BF)
    part = jnp.sum(jnp.sum(second * slope, axis=0), axis=0, keepdims=True)
    vec = coeff * SCALE * stat_ref[0:1] + GWEIGHT * SCALE * part
    vec_ref[...] = jnp.broadcast_to(vec, (8, 256))


def power_of(top):
    power = 7.0 - jnp.ceil(jnp.log2(jnp.maximum(top, 1e-30)) + 0.01)
    return jnp.clip(power, -100.0, 100.0)


def encode(v, power):
    u = v * jnp.exp2(power)
    q = u * u
    q = q * q
    q = q * q
    q = q * q
    return jnp.where(u < 0, -q, q).astype(BF)


def decode(code, power):
    f = code.astype(F32)
    mag = jnp.exp2(jnp.log2(jnp.abs(f)) * (1.0 / 16.0) - power)
    return jnp.where(f < 0, -mag, mag)


def tail_rows(power, vec, width):
    hi = vec.astype(BF).astype(F32)
    mid = (vec - hi).astype(BF).astype(F32)
    lo = vec - hi - mid
    rows = [power, hi, mid, lo]
    if width > 128:
        rows = [power] + [jnp.concatenate([r, r], 1) for r in rows[1:]]
    row = lax.broadcasted_iota(jnp.int32, (16, width), 0)
    tail = jnp.zeros((16, width), F32)
    for k in range(4):
        tail = jnp.where(row == k, rows[k], tail)
    return tail.astype(BF)


def tail_vec(tail):
    t = tail[1:4, :128].astype(F32)
    return t[0:1] + t[1:2] + t[2:3]


def shifted(v, target):
    edge = jnp.zeros((16, 1, 256), F32)
    f = v.astype(F32)
    target[:, 0:256] = jnp.concatenate([f[:, 1:], edge], 1).astype(BF).reshape(1024, 256)
    target[:, 256:512] = v.reshape(1024, 256)
    target[:, 512:768] = jnp.concatenate([edge, f[:, : COLS - 1]], 1).astype(BF).reshape(1024, 256)


def corr_kernel(
    x_ref, p0, p1, p2, p3, take, gh, gho, pre, preo, vec, veco,
    own_ref, m1, m2, m3, evec_ref, xh, gih, both, g_gh, g_pre, wsum,
):
    y, c, _, x, _, _ = place_of()
    for k in range(4):
        at = pl.multiple_of((2 * k + c) * 128, 128)
        xh[:, :, k * 128 : (k + 1) * 128] = x_ref[2:20, :, pl.ds(at, 128)]
    for d, piece in enumerate((p0, p1, p2, p3)):
        at = pl.multiple_of(lax.rem(y + 4 - d, 4) * 128, 128)
        half = pl.multiple_of(c * 128, 128)
        gih[pl.ds(9 * c, 9), :, pl.ds(at, 128)] = piece[:, :, pl.ds(half, 128)]
        gih[pl.ds(9 * (1 - c), 9), :, pl.ds(at, 128)] = take[d]
    both[pl.ds(8 * c, 8)] = gh[...]
    both[pl.ds(8 * (1 - c), 8)] = gho[...]
    shifted(both[...], g_gh)
    both[pl.ds(8 * c, 8)] = pre[...]
    both[pl.ds(8 * (1 - c), 8)] = preo[...]
    shifted(both[...], g_pre)
    for a in range(3):
        adv = lax.dot_general(
            xh[a : a + 16].reshape(1024, 512), g_pre[...], (((0,), (0,)), ((), ())),
            preferred_element_type=F32,
        )
        direct = lax.dot_general(
            gih[a : a + 16].reshape(1024, 512), g_gh[...], (((0,), (0,)), ((), ())),
            preferred_element_type=F32,
        )
        total = adv + GWEIGHT * direct
        for b in range(3):
            wsum[3 * a + b] = total[:, b * 256 : (b + 1) * 256].reshape(4, 4, 32, 256)
    half = pl.multiple_of(c * 128, 128)
    evec = vec[0:1, pl.ds(half, 128)] + veco[0:1, pl.ds(half, 128)]
    evec_ref[...] = jnp.broadcast_to(evec, (8, 128))
    own_ref[...] = wsum[:, :, pl.ds(x, 1)].reshape(1152, 256)
    for d, m in ((1, m1), (2, m2), (3, m3)):
        part = wsum[:, :, pl.ds(lax.rem(x + d, 4), 1)].reshape(1152, 256)
        power = power_of(jnp.max(jnp.abs(part), axis=0, keepdims=True))
        m[0:1152] = encode(part, power)
        m[1152:1168] = tail_rows(power, evec, 256)


def xsum_kernel(own, evec_in, m1, m2, m3, own_ref, evec_ref, *rest):
    zmsgs, total = rest[:7], rest[7]
    _, _, _, _, z, _ = place_of()
    evec = evec_in[0:1]
    powers = []
    for m in (m1, m2, m3):
        tail = m[1152:1168]
        powers.append(tail[0:1].astype(F32))
        evec = evec + tail_vec(tail)
    t = own[...]
    for m, power in zip((m1, m2, m3), powers):
        t = t + decode(m[0:1152], power)
    t = t.reshape(36, 4, 8, 256)
    for h in range(2):
        for q in range(4):
            total[2 * q + h] = t[:, q, :, h * 128 : (h + 1) * 128]
    evec_ref[...] = jnp.broadcast_to(evec, (8, 128))
    own_ref[...] = total[pl.ds(z, 1)].reshape(288, 128)
    for d in range(1, 8):
        part = total[pl.ds(lax.rem(z + d, 8), 1)].reshape(288, 128)
        power = power_of(jnp.max(jnp.abs(part), axis=0, keepdims=True))
        zmsgs[d - 1][0:288] = encode(part, power)
        zmsgs[d - 1][288:304] = tail_rows(power, evec, 128)


def zsum_kernel(own, evec_in, m1, m2, m3, m4, m5, m6, m7, y0, y1, y2, y3, e_out, total):
    y, _, _, _, z, lo = place_of()
    t = own[...]
    slot = lax.broadcasted_iota(jnp.int32, (8, 128), 0)
    e = jnp.where(slot == lo, evec_in[...], 0.0)
    for d, m in enumerate((m1, m2, m3, m4, m5, m6, m7), 1):
        tail = m[288:304]
        t = t + decode(m[0:288], tail[0:1].astype(F32))
        e = e + jnp.where(slot == lax.rem(z + 8 - d, 4), tail_vec(tail), 0.0)
    e_out[...] = e
    total[...] = t.reshape(9, 4, 8, 128)
    for d, target in enumerate((y0, y1, y2, y3)):
        target[...] = total[:, pl.ds(lax.rem(y + d, 4), 1)].reshape(72, 128)


def code_kernel(y0, y1, y2, y3, m_ref, tail):
    y, _, _, _, _, _ = place_of()
    tail[...] = jnp.zeros((16, 128), F32)
    for d, piece in enumerate((y0, y1, y2, y3)):
        at = lax.rem(y + 4 - d, 4)
        v = piece[...]
        power = power_of(jnp.max(jnp.abs(v), axis=0, keepdims=True))
        m_ref[pl.ds(at, 1)] = encode(v, power).reshape(1, 9, 8, 128)
        row = lax.broadcasted_iota(jnp.int32, (16, 128), 0)
        tail[...] = jnp.where(row == at, power, tail[...])
    m_ref[4:5] = jnp.zeros((1, 9, 8, 128), BF)
    m_ref[4, 0:2] = tail[...].astype(BF).reshape(2, 8, 128)


def final_kernel(b0, b1, b2, b3, out_ref):
    _, _, _, x, z, _ = place_of()
    for d, block in enumerate((b0, b1, b2, b3)):
        u_base = 32 * lax.rem(x + 4 - d, 4)
        for k in range(8):
            zz = lax.rem(z + 8 - k, 8)
            rows = pl.ds(pl.multiple_of(u_base + 8 * (zz // 2), 8), 8)
            shift = 128 * lax.rem(zz, 2)
            powers = block[k, 4, 0].astype(F32)
            for yy in range(4):
                lanes = pl.ds(pl.multiple_of(yy * 256 + shift, 128), 128)
                values = decode(block[k, yy], powers[yy : yy + 1].reshape(1, 1, 128))
                out_ref[:, rows, lanes] = values


def body(features, kernel, embedding, labels):
    t = lax.axis_index("tensor")
    y, c = t // 2, lax.rem(t, 2)
    lo = lax.axis_index("dp")
    first = c == 0

    def by_core(zero, one):
        return jnp.where(first, zero, one)

    own = features[0]
    kern = kernel.reshape(9, 128, CHANS)
    halo_pairs = []
    for q in range(7):
        for k in range(2):
            halo_pairs.append((q * 8 + 6 + k, (q + 1) * 8 + 6 + k))
            halo_pairs.append(((q + 1) * 8 + k, q * 8 + k))
    halo = lax.ppermute(own, ("space", "tensor"), halo_pairs)
    mine = {d: y_send(own, d) for d in ORDER}
    mine[0] = own
    cols = {
        d: y_send(lax.dynamic_slice_in_dim(kern, lax.rem(y + d, 4) * 256, 256, 2), d)
        for d in ORDER
    }
    kown = lax.dynamic_slice_in_dim(kern, y * 256, 256, 2)
    other = [core_swap(mine[d]) for d in range(4)]
    kother = core_swap(kern)
    cother = [core_swap(kown)] + [core_swap(cols[d]) for d in (1, 2, 3)]

    def halo_pairs_y(d):
        return [(6 + k, 2 * ((3 + d) % 4) + k) for k in range(2)] + [
            (k, 2 * d + k) for k in range(2)
        ]

    r1, r2, r3 = (lax.ppermute(halo, "tensor", halo_pairs_y(d)) for d in (1, 2, 3))
    top = jnp.where(y == 0, r1, jnp.where(y == 1, r2, jnp.where(y == 2, r3, halo)))
    bottom = jnp.where(y == 0, halo, jnp.where(y == 1, r1, jnp.where(y == 2, r2, r3)))
    crossed = core_swap(by_core(bottom, top))

    e_own = jnp.broadcast_to(lax.dynamic_slice_in_dim(embedding, labels[0], 1, 0), (8, 128))
    e_other = core_swap(e_own)
    e = by_core(
        jnp.concatenate([e_own, e_other], 1), jnp.concatenate([e_other, e_own], 1)
    )

    gh, hidden, stat, x_rows, w = call(
        hidden_kernel,
        [
            out((10, COLS, 256), BF),
            out((8, COLS, 256), F32),
            out((16, 256), F32),
            out((22, COLS, CHANS), BF),
            out((9, CHANS, 256), BF),
        ],
        [pltpu.VMEM((3, 10, COLS, 256), F32)],
        *[mine[d] for d in range(4)],
        *other,
        halo, r1, r2, r3, crossed,
        kern, cols[1], cols[2], cols[3],
        *cother,
        e,
        flops=2 * 640 * 9 * 1024 * 256,
    )

    def spread(v, last):
        got = {d: y_send(v, d) for d in ORDER}
        got[0] = v
        edge = jnp.stack([by_core(got[d][last], got[d][0]) for d in range(4)])
        return [got[d] for d in range(4)], core_swap(edge)

    gh_pieces, gh_edge = spread(gh, 9)
    part = stat[8:16, :128]
    part = part + core_swap(part)
    part = part + y_send(part, 1) + y_send(part, 2) + y_send(part, 3)
    part = part + x_send(part, 1) + x_send(part, 2) + x_send(part, 3)
    score = part + lax.ppermute(part, "space", HI_SWAP)
    gh8 = by_core(gh[2:10], gh[0:8])
    gh8_other = core_swap(gh8)

    (gi,) = call(
        input_kernel,
        [out((9, COLS, 256), BF)],
        [pltpu.VMEM((11, COLS, CHANS), BF), pltpu.VMEM((3, 9, COLS, 256), F32)],
        *gh_pieces, gh_edge, kern, kother,
        flops=2 * 576 * 9 * 1024 * 256,
    )
    gi_pieces, gi_edge = spread(gi, 8)
    take = core_swap(jnp.stack([by_core(p[:, :, 128:], p[:, :, :128]) for p in gi_pieces]))
    pre, vec = call(
        second_kernel,
        [out((8, COLS, 256), BF), out((8, 256), F32)],
        [pltpu.VMEM((10, COLS, CHANS), BF), pltpu.VMEM((3, 8, COLS, 256), F32)],
        *gi_pieces, gi_edge, w, hidden, stat, score, e,
        flops=2 * 512 * 9 * 1024 * 256,
    )
    pre_other = core_swap(pre)
    vec_other = core_swap(vec)
    own_x, evec, m1, m2, m3 = corr_call(
        x_rows, *gi_pieces, take, gh8, gh8_other, pre, pre_other, vec, vec_other
    )
    sent = {1: m1, 2: m2, 3: m3}
    got = {d: x_send(sent[d], d) for d in ORDER}
    own_z, evec, *zmsgs = call(
        xsum_kernel,
        [out((288, 128), F32), out((8, 128), F32)] + [out((304, 128), BF)] * 7,
        [pltpu.VMEM((8, 36, 8, 128), F32)],
        own_x, evec, got[1], got[2], got[3],
    )
    got = {d: z_send(zmsgs[d - 1], d) for d in Z_ORDER}
    y0, y1, y2, y3, e_all = call(
        zsum_kernel,
        [out((72, 128), F32)] * 4 + [out((8, 128), F32)],
        [pltpu.VMEM((9, 4, 8, 128), F32)],
        own_z, evec, *[got[d] for d in range(1, 8)],
    )
    sent = {1: y1, 2: y2, 3: y3}
    got = {d: y_send(sent[d], d) for d in ORDER}
    (message,) = call(
        code_kernel,
        [out((5, 9, 8, 128), BF)],
        [pltpu.VMEM((16, 128), F32)],
        y0, got[1], got[2], got[3],
    )
    got = {d: z_send(message, d) for d in Z_ORDER}
    by_z = jnp.stack([message] + [got[d] for d in range(1, 8)])
    got = {d: x_send(by_z, d) for d in ORDER}
    (wtotal,) = call(
        final_kernel, [out((9, 128, CHANS), F32)], [], by_z, got[1], got[2], got[3]
    )

    tags = jnp.broadcast_to(labels, (1,))
    owners = [(lo, tags)] + [
        (lax.rem(lo + 4 - d, 4), lax.ppermute(tags, "dp", [(i, (i + d) % 4) for i in range(4)]))
        for d in (1, 2, 3)
    ]
    class_ids = jnp.arange(embedding.shape[0], dtype=jnp.int32)[:, None]
    egrad = jnp.zeros(embedding.shape, F32)
    for at, tag in owners:
        row = lax.dynamic_slice_in_dim(e_all, at, 1, 0)
        egrad = egrad + jnp.where(class_ids == tag[0], row, 0.0)
    return (wtotal.reshape(3, 3, 128, CHANS), egrad)


def corr_call(*args):
    own_x, m1, m2, m3, evec = call(
        corr_kernel,
        [out((1152, 256), F32)] + [out((1168, 256), BF)] * 3 + [out((8, 128), F32)],
        [
            pltpu.VMEM((18, COLS, 512), BF),
            pltpu.VMEM((18, COLS, 512), BF),
            pltpu.VMEM((16, COLS, 256), BF),
            pltpu.VMEM((1024, 768), BF),
            pltpu.VMEM((1024, 768), BF),
            pltpu.VMEM((9, 4, 4, 32, 256), F32),
        ],
        *args,
        flops=4 * 1024 * 9 * 512 * 256,
    )
    return own_x, evec, m1, m2, m3


def solution(mesh):
    placed = (
        P("dp", ("space", "tensor"), None, None),
        P(None, None, "tensor", None),
        P(None, "tensor"),
        P("dp"),
    )
    return jax.shard_map(
        body,
        mesh=mesh,
        in_specs=placed,
        out_specs=(P(None, None, "tensor", None), P(None, "tensor")),
        check_vma=False,
    )
```

```python
import math

import jax
import jax.numpy as jnp
from jax import lax
from jax.experimental import pallas as pl
from jax.experimental.pallas import tpu as pltpu
from jax.sharding import PartitionSpec as P

r1_factor = 1000.0
BF = jnp.bfloat16
F32 = jnp.float32

IMAGES, HEIGHT, COLS, CHANS = 4, 128, 64, 1024
SCALE = 1.0 / math.sqrt(HEIGHT * COLS * CHANS)
GWEIGHT = r1_factor / IMAGES

CORE_SWAP = [(t, t ^ 1) for t in range(8)]
HI_SWAP = [(s, s ^ 1) for s in range(8)]
X_PAIRS = [(s, s ^ 2) for s in range(8)]
X_FAR = [(s, s ^ 4) for s in range(8)]
ORDER = (2, 1, 3)
Z_STEP = {1: 1, 2: 2, 3: 7}


def y_perm(d):
    return [(2 * y + c, 2 * ((y + d) % 4) + c) for y in range(4) for c in range(2)]


def x_perm(d):
    return [(2 * x + h, 2 * ((x + d) % 4) + h) for x in range(4) for h in range(2)]


def z_perm(d):
    pairs = []
    for z in range(8):
        w = (z + d) % 8
        for x in range(4):
            pairs.append(((z % 4) * 8 + 2 * x + z // 4, (w % 4) * 8 + 2 * x + w // 4))
    return pairs


def core_swap(v):
    return lax.ppermute(v, "tensor", CORE_SWAP)


def y_send(v, d):
    return lax.ppermute(v, "tensor", y_perm(d))


def x_send(v, d):
    return lax.ppermute(v, "space", x_perm(d))


def z_send(v, d):
    return lax.ppermute(v, ("dp", "space"), z_perm(d))


def place_of():
    t = lax.axis_index("tensor")
    s = lax.axis_index("space")
    lo = lax.axis_index("dp")
    return t // 2, lax.rem(t, 2), s, s // 2, 4 * lax.rem(s, 2) + lo, lo


def call(kernel, outs, scratch, *args, flops=0, far=(), far_out=()):
    vm = pl.BlockSpec(memory_space=pltpu.VMEM)
    anywhere = pl.BlockSpec(memory_space=pl.ANY)
    total = sum(math.prod(a.shape) * a.dtype.itemsize for a in args)
    total += sum(math.prod(o.shape) * o.dtype.itemsize for o in outs)
    return pl.pallas_call(
        kernel,
        out_shape=tuple(outs),
        in_specs=[anywhere if k in far else vm for k in range(len(args))],
        out_specs=tuple(anywhere if k in far_out else vm for k in range(len(outs))),
        scratch_shapes=scratch,
        compiler_params=pltpu.CompilerParams(vmem_limit_bytes=48 << 20),
        cost_estimate=pl.CostEstimate(flops=flops, bytes_accessed=total, transcendentals=0),
    )(*args)


def out(shape, dtype):
    return jax.ShapeDtypeStruct(shape, dtype)


def conv_rows(acc, source, rows, weight, contract):
    flat = source.reshape(source.shape[0] * COLS, CHANS)
    for b in range(3):
        total = None
        for a in range(3):
            part = lax.dot_general(
                flat[a * COLS : (a + rows) * COLS],
                weight(a, b),
                (((1,), (contract,)), ((), ())),
                preferred_element_type=F32,
            )
            total = part if total is None else total + part
        acc[b] = total.reshape(rows, COLS, 256)
    edge = jnp.zeros((rows, 1, 256), F32)
    left, right = acc[0], acc[2]
    return (
        acc[1]
        + jnp.concatenate([edge, left[:, : COLS - 1]], 1)
        + jnp.concatenate([right[:, 1:], edge], 1)
    )


def inside_rows(start, rows):
    row = start + lax.broadcasted_iota(jnp.int32, (rows, COLS, 256), 0)
    return (row >= 0) & (row < HEIGHT)


def split_rows(row):
    hi = row.astype(BF).astype(F32)
    mid = (row - hi).astype(BF).astype(F32)
    return [hi, mid, row - hi - mid]


def rows_block(rows, height, width):
    at = lax.broadcasted_iota(jnp.int32, (height, width), 0)
    block = jnp.zeros((height, width), F32)
    for k, row in enumerate(rows):
        block = jnp.where(at == k, row, block)
    return block.astype(BF)


def hidden_kernel(*refs):
    mine, other = refs[0:4], refs[4]
    kern, k1, k2, k3, kother, c1, c2, c3 = refs[5:13]
    halo, r1, r2, r3, crossed, e_ref = refs[13:19]
    gh_ref, hid_ref, stat_ref, x_out, w_out = refs[19:24]
    x_ref, w_ref, acc, sems = refs[24:28]
    y, c, s, _, _, _ = place_of()
    columns = pl.ds(pl.multiple_of(y * 256, 256), 256)
    copies = []

    def copy(source, target):
        job = pltpu.make_async_copy(source, target, sems.at[len(copies)])
        job.start()
        copies.append(job)

    for d in range(4):
        at = lax.rem(y + 4 - d, 4)
        copy(mine[d], x_ref.at[pl.ds(3 + 4 * at + 2 * c, 2)])
        copy(other.at[d], x_ref.at[pl.ds(3 + 4 * at + 2 * (1 - c), 2)])
    for d in range(4):
        at = lax.rem(y + 4 - d, 4)
        for core, piece, whole in ((c, (k1, k2, k3)[d - 1], kern), (1 - c, (c1, c2, c3)[d - 1], kother)):
            source = piece if d else whole.at[:, :, columns]
            block = pl.ds(pl.multiple_of((2 * at + core) * 128, 128), 128)
            copy(source, w_ref.at[:, block, :])
    for source, up, down in ((halo, 3, 0), (r1, 0, 1), (r2, 1, 2), (r3, 2, 3)):

        @pl.when((y == up) & (c == 0))
        def _():
            x_ref[0:1] = source[1:2]

        @pl.when((y == up) & (c == 1))
        def _():
            x_ref[2:3] = source[1:2]

        @pl.when((y == down) & (c == 0))
        def _():
            x_ref[19:20] = source[0:1]

        @pl.when((y == down) & (c == 1))
        def _():
            x_ref[21:22] = source[0:1]

    @pl.when(c == 0)
    def _():
        x_ref[1:3] = crossed[...]

    @pl.when(c == 1)
    def _():
        x_ref[19:21] = crossed[...]

    for job in copies:
        job.wait()
    jobs = [
        pltpu.make_async_copy(x_ref.at[pl.ds(2, 18)], x_out, sems.at[16]),
        pltpu.make_async_copy(w_ref, w_out, sems.at[17]),
    ]
    for job in jobs:
        job.start()
    hidden = conv_rows(acc, x_ref[pl.ds(10 * c, 12)], 10, lambda a, b: w_ref[3 * a + b], 0)
    acc[0] = hidden
    sig = jax.nn.sigmoid(hidden)
    slope = sig * (1.0 + hidden * (1.0 - sig))
    e = e_ref[0:1, :].reshape(1, 1, 256)
    gh = jnp.where(inside_rows(16 * s - 2 + 10 * c, 10), e * slope * SCALE, 0.0)
    gh_ref[0:640] = gh.astype(BF).reshape(640, 256)
    own = acc[0, pl.ds(2 - 2 * c, 8)]
    hid_ref[...] = own
    act = own * jax.nn.sigmoid(own)
    act_sum = jnp.sum(jnp.sum(act, axis=0), axis=0, keepdims=True)
    part = SCALE * jnp.sum(act_sum * e_ref[0:1, :])
    stat_ref[...] = jnp.broadcast_to(act_sum, (8, 256))
    gh_ref[640:656] = rows_block(split_rows(jnp.full((1, 256), part, F32)), 16, 256)
    for job in jobs:
        job.wait()


def sum_rows(tail):
    t = tail.astype(F32)
    return t[0:1] + t[1:2] + t[2:3]


def input_kernel(p0, p1, p2, p3, swapped, kern, kother, gi_ref, part_ref, full, acc):
    y, c, s, _, _, _ = place_of()
    part = jnp.zeros((1, 256), F32)
    for d, piece in enumerate((p0, p1, p2, p3)):
        at = pl.multiple_of(lax.rem(y + 4 - d, 4) * 256, 256)
        full[pl.ds(c, 10), :, pl.ds(at, 256)] = piece[0:640].reshape(10, COLS, 256)
        full[pl.ds(10 * (1 - c), 1), :, pl.ds(at, 256)] = swapped[d * 64 : d * 64 + 64].reshape(
            1, COLS, 256
        )
        part = part + sum_rows(piece[640:656]) + sum_rows(swapped[768 + 16 * d : 784 + 16 * d])
    part_ref[...] = jnp.broadcast_to(part[:, :128], (8, 128))

    def weight(a, b):
        tap = 3 * (2 - a) + 2 - b
        return jnp.concatenate([kern[tap], kother[tap]], 0)

    grad = conv_rows(acc, full[...], 9, weight, 1)
    turned = jnp.concatenate([grad[:, :, 128:], grad[:, :, :128]], 2)
    grad = jnp.where(c == 0, grad, turned)
    gi_ref[...] = jnp.where(inside_rows(16 * s - 1 + 9 * c, 9), grad, 0.0).astype(BF)


def second_kernel(
    p0, p1, p2, p3, swapped, w_ref, hid_ref, stat_ref, score, e_ref, pre_ref, vec_ref, full, acc
):
    y, c, _, _, _, _ = place_of()
    for d, piece in enumerate((p0, p1, p2, p3)):
        at = pl.multiple_of(lax.rem(y + 4 - d, 4) * 256, 256)
        near = pl.multiple_of(at + 128 * c, 128)
        away = pl.multiple_of(at + 128 * (1 - c), 128)
        full[pl.ds(c, 9), :, pl.ds(at, 256)] = piece[...]
        full[pl.ds(9 * (1 - c), 1), :, pl.ds(near, 128)] = swapped[d, pl.ds(8 * c, 1)]
        full[pl.ds(9 * (1 - c), 1), :, pl.ds(away, 128)] = swapped[d, 9:10]
    second = conv_rows(acc, full[...], 8, lambda a, b: w_ref[3 * a + b], 0)
    hidden = hid_ref[...]
    sig = jax.nn.sigmoid(hidden)
    slope = sig * (1.0 + hidden * (1.0 - sig))
    curve = sig * (1.0 - sig) * (2.0 + hidden * (1.0 - 2.0 * sig))
    e = e_ref[0:1, :].reshape(1, 1, 256)
    coeff = -jax.nn.sigmoid(-score[0:1, 0:1]) / IMAGES
    c3 = coeff.reshape(1, 1, 1)
    pre = c3 * e * slope * SCALE + GWEIGHT * second * e * curve * SCALE
    pre_ref[0:512] = pre.astype(BF).reshape(512, 256)
    part = jnp.sum(jnp.sum(second * slope, axis=0), axis=0, keepdims=True)
    vec = coeff * SCALE * stat_ref[0:1] + GWEIGHT * SCALE * part
    pre_ref[512:528] = rows_block(split_rows(vec), 16, 256)
    vec_ref[...] = jnp.broadcast_to(vec, (8, 256))


def power_of(top):
    power = 7.0 - jnp.ceil(jnp.log2(jnp.maximum(top, 1e-30)) + 0.01)
    return jnp.clip(power, -100.0, 100.0)


def encode(v, power):
    u = v * jnp.exp2(power)
    q = u * u
    q = q * q
    q = q * q
    q = q * q
    return jnp.where(u < 0, -q, q).astype(BF)


def decode(code, power):
    f = code.astype(F32)
    mag = jnp.exp2(jnp.log2(jnp.abs(f)) * (1.0 / 16.0) - power)
    return jnp.where(f < 0, -mag, mag)


def shifted(v, target):
    edge = jnp.zeros((16, 1, 256), F32)
    f = v.astype(F32)
    target[:, 0:256] = jnp.concatenate([f[:, 1:], edge], 1).astype(BF).reshape(1024, 256)
    target[:, 256:512] = v.reshape(1024, 256)
    target[:, 512:768] = jnp.concatenate([edge, f[:, : COLS - 1]], 1).astype(BF).reshape(1024, 256)


def lane_top(v):
    return power_of(jnp.max(jnp.abs(v), axis=0, keepdims=True))


def corr_kernel(
    x_ref, p0, p1, p2, p3, take, gh, gho, pre, preo, vec,
    own_a, own_b, a1, a2, a3, b1, b2, b3, evec_ref, xh, gih, both, g_gh, g_pre, wsum,
):
    y, c, _, x, _, lo = place_of()
    for k in range(4):
        at = pl.multiple_of((2 * k + c) * 128, 128)
        xh[:, :, k * 128 : (k + 1) * 128] = x_ref[:, :, pl.ds(at, 128)]
    half = pl.multiple_of(c * 128, 128)
    for d, piece in enumerate((p0, p1, p2, p3)):
        at = pl.multiple_of(lax.rem(y + 4 - d, 4) * 128, 128)
        gih[pl.ds(9 * c, 9), :, pl.ds(at, 128)] = piece[:, :, pl.ds(half, 128)]
        gih[pl.ds(9 * (1 - c), 9), :, pl.ds(at, 128)] = take[d, 0:9]
    own_rows = pl.ds(pl.multiple_of(128 - 128 * c, 128), 512)
    both[pl.ds(8 * c, 8)] = gh[own_rows].reshape(8, COLS, 256)
    both[pl.ds(8 * (1 - c), 8)] = gho[256:768].reshape(8, COLS, 256)
    shifted(both[...], g_gh)
    both[pl.ds(8 * c, 8)] = pre[0:512].reshape(8, COLS, 256)
    both[pl.ds(8 * (1 - c), 8)] = preo[0:512].reshape(8, COLS, 256)
    shifted(both[...], g_pre)
    for a in range(3):
        adv = lax.dot_general(
            xh[a : a + 16].reshape(1024, 512), g_pre[...], (((0,), (0,)), ((), ())),
            preferred_element_type=F32,
        )
        direct = lax.dot_general(
            gih[a : a + 16].reshape(1024, 512), g_gh[...], (((0,), (0,)), ((), ())),
            preferred_element_type=F32,
        )
        total = adv + GWEIGHT * direct
        for b in range(3):
            for h in range(2):
                lanes = total[:, b * 256 + h * 128 : b * 256 + h * 128 + 128]
                wsum[h, 3 * a + b] = lanes.reshape(4, 4, 32, 128)
    evec = vec[0:1, pl.ds(half, 128)] + sum_rows(preo[512:528, pl.ds(half, 128)])
    evec_ref[...] = jnp.broadcast_to(evec, (8, 128))
    extra = split_rows(evec)
    for h, at, own, targets in ((0, x, own_a, (a1, a2, a3)), (1, lo, own_b, (b1, b2, b3))):
        own[...] = wsum[h, :, :, pl.ds(at, 1)].reshape(1152, 128)
        for d, m in enumerate(targets, 1):
            part = wsum[h, :, :, pl.ds(lax.rem(at + d, 4), 1)].reshape(1152, 128)
            power = lane_top(part)
            m[0:1152] = encode(part, power)
            m[1152:1168] = rows_block([power] + extra, 16, 128)


def added(own, messages, size):
    t = own[...]
    for m in messages:
        t = t + decode(m[0:size], m[size : size + 16][0:1].astype(F32))
    return t


def first_sum_kernel(
    own_a, own_b, evec_in, label, a1, a2, a3, b1, b2, b3,
    out_a, out_b, c1, c2, c3, d1, d2, d3, evec_ref, total,
):
    _, _, _, x, _, lo = place_of()
    evec = evec_in[0:1]
    for m in (a1, a2, a3):
        evec = evec + sum_rows(m[1152:1168][1:4])
    evec_ref[...] = jnp.broadcast_to(evec, (8, 128))
    tag = jnp.broadcast_to(label[...], (1, 128)).astype(F32)
    high = jnp.floor(tag * (1.0 / 32.0))
    extra = split_rows(evec) + [high, tag - 32.0 * high]
    for own, got, at, mine, targets in (
        (own_a, (a1, a2, a3), lo, out_a, (c1, c2, c3)),
        (own_b, (b1, b2, b3), x, out_b, (d1, d2, d3)),
    ):
        total[...] = added(own, got, 1152).reshape(36, 4, 8, 128)
        mine[...] = total[:, pl.ds(at, 1)].reshape(288, 128)
        for d, m in enumerate(targets, 1):
            part = total[:, pl.ds(lax.rem(at + d, 4), 1)].reshape(288, 128)
            power = lane_top(part)
            m[0:288] = encode(part, power)
            m[288:304] = rows_block([power] + extra, 16, 128)


def second_sum_kernel(own_a, own_b, evec_in, label, a1, a2, a3, b1, b2, b3, m_ref):
    _, _, _, _, _, lo = place_of()
    ta = added(own_a, (a1, a2, a3), 288)
    tb = added(own_b, (b1, b2, b3), 288)
    pa, pb = lane_top(ta), lane_top(tb)
    m_ref[0:288] = encode(ta, pa)
    m_ref[288:576] = encode(tb, pb)
    lane = lax.broadcasted_iota(jnp.int32, (1, 128), 1)
    tag = jnp.broadcast_to(label[...], (1, 128)).astype(F32)
    high = jnp.floor(tag * (1.0 / 32.0))
    found = [(lo, split_rows(evec_in[0:1]) + [high, tag - 32.0 * high])]
    for d, m in enumerate((a1, a2, a3), 1):
        t = m[288:304].astype(F32)
        found.append((lax.rem(lo + 4 - d, 4), [t[k : k + 1] for k in range(1, 6)]))
    rows = [pa, pb]
    zero = jnp.zeros((1, 128), F32)
    for slot in range(4):
        for k in range(3):
            row = zero
            for at, parts in found:
                row = jnp.where(at == slot, parts[k], row)
            rows.append(row)
    for k in (3, 4):
        row = zero
        for at, parts in found:
            row = jnp.where(lane == at, parts[k], row)
        rows.append(row)
    m_ref[576:592] = rows_block(rows, 16, 128)


def pair_kernel(mine, theirs, y0, y1, y2, y3, egrad_ref, total):
    y, _, _, _, _, _ = place_of()
    t1 = mine[576:592].astype(F32)
    t2 = theirs[576:592].astype(F32)
    for h in range(2):
        rows = pl.ds(288 * h, 288)
        value = decode(mine[rows], t1[h : h + 1]) + decode(theirs[rows], t2[h : h + 1])
        total[h] = value.reshape(9, 4, 8, 128)
    for d, target in enumerate((y0, y1, y2, y3)):
        target[...] = total[:, :, pl.ds(lax.rem(y + d, 4), 1)].reshape(2, 72, 128)
    row = lax.broadcasted_iota(jnp.int32, (1000, 128), 0)
    egrad = jnp.zeros((1000, 128), F32)
    for slot in range(4):
        at = 2 + 3 * slot
        vec = (t1[at : at + 1] + t1[at + 1 : at + 2] + t1[at + 2 : at + 3]) + (
            t2[at : at + 1] + t2[at + 1 : at + 2] + t2[at + 2 : at + 3]
        )
        tag = (32.0 * t1[14:15, slot : slot + 1] + t1[15:16, slot : slot + 1]).astype(jnp.int32)
        egrad = egrad + jnp.where(row == tag, vec, 0.0)
    egrad_ref[...] = egrad


def code_kernel(y0, y1, y2, y3, ma_ref, mb_ref):
    y, _, _, _, _, _ = place_of()
    for h, m_ref in enumerate((ma_ref, mb_ref)):
        row = lax.broadcasted_iota(jnp.int32, (8, 128), 0)
        tail = jnp.zeros((8, 128), F32)
        for d, piece in enumerate((y0, y1, y2, y3)):
            at = lax.rem(y + 4 - d, 4)
            v = piece[h]
            power = lane_top(v)
            m_ref[pl.ds(9 * at, 9)] = encode(v, power).reshape(9, 8, 128)
            tail = jnp.where(row == at, power, tail)
        m_ref[36] = tail.astype(BF)


def final_kernel(a0, a1, a2, a3, b0, b1, b2, b3, out_ref):
    _, _, _, x, _, lo = place_of()
    for h, blocks in enumerate(((a0, a1, a2, a3), (b0, b1, b2, b3))):
        for d, block in enumerate(blocks):
            for k in range(4):
                if h == 0:
                    u = 32 * lax.rem(x + 4 - d, 4) + 8 * lax.rem(lo + 4 - k, 4)
                else:
                    u = 32 * lax.rem(lo + 4 - d, 4) + 8 * lax.rem(x + 4 - k, 4)
                rows = pl.ds(pl.multiple_of(u, 8), 8)
                powers = block[k, 36].astype(F32)
                for yy in range(4):
                    lanes = slice(yy * 256 + h * 128, yy * 256 + h * 128 + 128)
                    values = decode(
                        block[k, 9 * yy : 9 * yy + 9], powers[yy : yy + 1].reshape(1, 1, 128)
                    )
                    out_ref[:, rows, lanes] = values


def body(features, kernel, embedding, labels):
    t = lax.axis_index("tensor")
    y, c = t // 2, lax.rem(t, 2)
    first = c == 0

    def by_core(zero, one):
        return jnp.where(first, zero, one)

    def y_all(v):
        got = {d: y_send(v, d) for d in ORDER}
        return [v, got[1], got[2], got[3]]

    def x_all(values):
        got = {d: x_send(values[d - 1], d) for d in ORDER}
        return [got[d] for d in (1, 2, 3)]

    def z_all(values):
        got = {d: z_send(values[d - 1], Z_STEP[d]) for d in ORDER}
        return [got[d] for d in (1, 2, 3)]

    own = features[0]
    kern = kernel.reshape(9, 128, CHANS)
    slices = [
        lax.dynamic_slice_in_dim(kern, lax.rem(y + d, 4) * 256, 256, 2) for d in (1, 2, 3)
    ]
    own, *slices = lax.optimization_barrier((own, *slices))
    cols = {d: y_send(slices[d - 1], d) for d in ORDER}
    halo_pairs = []
    for q in range(7):
        for k in range(2):
            halo_pairs.append((q * 8 + 6 + k, (q + 1) * 8 + 6 + k))
            halo_pairs.append(((q + 1) * 8 + k, q * 8 + k))
    halo = lax.ppermute(own, ("space", "tensor"), halo_pairs)
    mine = y_all(own)
    kother = core_swap(kern)
    other = core_swap(jnp.stack(mine))
    cother = [core_swap(cols[d]) for d in (1, 2, 3)]

    def halo_pairs_y(d):
        return [(6 + k, 2 * ((3 + d) % 4) + k) for k in range(2)] + [
            (k, 2 * d + k) for k in range(2)
        ]

    r1, r2, r3 = (lax.ppermute(halo, "tensor", halo_pairs_y(d)) for d in (1, 2, 3))
    top = jnp.where(y == 0, r1, jnp.where(y == 1, r2, jnp.where(y == 2, r3, halo)))
    bottom = jnp.where(y == 0, halo, jnp.where(y == 1, r1, jnp.where(y == 2, r2, r3)))
    crossed = core_swap(by_core(bottom, top))

    e_own = jnp.broadcast_to(lax.dynamic_slice_in_dim(embedding, labels[0], 1, 0), (8, 128))
    e_other = core_swap(e_own)
    e = by_core(
        jnp.concatenate([e_own, e_other], 1), jnp.concatenate([e_other, e_own], 1)
    )

    gh, hidden, stat, x_rows, w = call(
        hidden_kernel,
        [
            out((656, 256), BF),
            out((8, COLS, 256), F32),
            out((8, 256), F32),
            out((18, COLS, CHANS), BF),
            out((9, CHANS, 256), BF),
        ],
        [
            pltpu.VMEM((22, COLS, CHANS), BF),
            pltpu.VMEM((9, CHANS, 256), BF),
            pltpu.VMEM((3, 10, COLS, 256), F32),
            pltpu.SemaphoreType.DMA((18,)),
        ],
        *mine, other,
        kern, cols[1], cols[2], cols[3], kother, *cother,
        halo, r1, r2, r3, crossed, e,
        flops=2 * 640 * 9 * 1024 * 256,
        far=range(13),
        far_out=(3, 4),
    )

    gh_pieces = y_all(gh)
    rows = [by_core(p[576:640], p[0:64]) for p in gh_pieces]
    rows.append(by_core(gh[128:640], gh[0:512]))
    rows.extend(p[640:656] for p in gh_pieces)
    gh_other = core_swap(jnp.concatenate(rows, 0))
    gi, part = call(
        input_kernel,
        [out((9, COLS, 256), BF), out((8, 128), F32)],
        [pltpu.VMEM((11, COLS, CHANS), BF), pltpu.VMEM((3, 9, COLS, 256), F32)],
        *gh_pieces, gh_other, kern, kother,
        flops=2 * 576 * 9 * 1024 * 256,
    )

    gi_pieces = y_all(gi)
    for pairs in (X_PAIRS, X_FAR, HI_SWAP):
        part = part + lax.ppermute(part, "space", pairs)
    rows = []
    for p in gi_pieces:
        low, high = p[:, :, :128], p[:, :, 128:]
        rows.append(
            jnp.concatenate([by_core(high, low), by_core(low[8:9], high[0:1])], 0)
        )
    take = core_swap(jnp.stack(rows))
    pre, vec = call(
        second_kernel,
        [out((528, 256), BF), out((8, 256), F32)],
        [pltpu.VMEM((10, COLS, CHANS), BF), pltpu.VMEM((3, 8, COLS, 256), F32)],
        *gi_pieces, take, w, hidden, stat, part, e,
        flops=2 * 512 * 9 * 1024 * 256,
    )
    pre_other = core_swap(pre)
    quarter, eighth = out((1168, 128), BF), out((304, 128), BF)
    own_a, own_b, a1, a2, a3, b1, b2, b3, evec = call(
        corr_kernel,
        [out((1152, 128), F32)] * 2 + [quarter] * 6 + [out((8, 128), F32)],
        [
            pltpu.VMEM((18, COLS, 512), BF),
            pltpu.VMEM((18, COLS, 512), BF),
            pltpu.VMEM((16, COLS, 256), BF),
            pltpu.VMEM((1024, 768), BF),
            pltpu.VMEM((1024, 768), BF),
            pltpu.VMEM((2, 9, 4, 4, 32, 128), F32),
        ],
        x_rows, *gi_pieces, take, gh, gh_other, pre, pre_other, vec,
        flops=4 * 1024 * 9 * 512 * 256,
    )

    label = labels.reshape(1, 1)
    got_a = x_all([a1, a2, a3])
    got_b = z_all([b1, b2, b3])
    own_a, own_b, a1, a2, a3, b1, b2, b3, evec = call(
        first_sum_kernel,
        [out((288, 128), F32)] * 2 + [eighth] * 6 + [out((8, 128), F32)],
        [pltpu.VMEM((36, 4, 8, 128), F32)],
        own_a, own_b, evec, label, *got_a, *got_b,
    )
    got_a = z_all([a1, a2, a3])
    got_b = x_all([b1, b2, b3])
    (message,) = call(
        second_sum_kernel,
        [out((592, 128), BF)],
        [],
        own_a, own_b, evec, label, *got_a, *got_b,
    )
    theirs = z_send(message, 4)
    y0, y1, y2, y3, egrad = call(
        pair_kernel,
        [out((2, 72, 128), F32)] * 4 + [out((1000, 128), F32)],
        [pltpu.VMEM((2, 9, 4, 8, 128), F32)],
        message, theirs,
    )
    sent = {1: y1, 2: y2, 3: y3}
    got = {d: y_send(sent[d], d) for d in ORDER}
    code_a, code_b = call(
        code_kernel, [out((37, 8, 128), BF)] * 2, [], y0, got[1], got[2], got[3]
    )
    got_a = z_all([code_a] * 3)
    got_b = x_all([code_b] * 3)
    code_a = jnp.stack([code_a] + got_a)
    code_b = jnp.stack([code_b] + got_b)
    got_a = x_all([code_a] * 3)
    got_b = z_all([code_b] * 3)
    (wtotal,) = call(
        final_kernel,
        [out((9, 128, CHANS), F32)],
        [],
        code_a, *got_a, code_b, *got_b,
    )
    return (wtotal.reshape(3, 3, 128, CHANS), egrad)


def solution(mesh):
    placed = (
        P("dp", ("space", "tensor"), None, None),
        P(None, None, "tensor", None),
        P(None, "tensor"),
        P("dp"),
    )
    return jax.shard_map(
        body,
        mesh=mesh,
        in_specs=placed,
        out_specs=(P(None, None, "tensor", None), P(None, "tensor")),
        check_vma=False,
    )
```

```python
import functools
import math

import jax
import jax.numpy as jnp
from jax import lax
from jax.experimental import pallas as pl
from jax.experimental.pallas import tpu as pltpu
from jax.sharding import PartitionSpec as P

r1_factor = 1000.0
BF = jnp.bfloat16
F32 = jnp.float32

IMAGES, HEIGHT, COLS, CHANS = 4, 128, 64, 1024
SCALE = 1.0 / math.sqrt(HEIGHT * COLS * CHANS)
GWEIGHT = r1_factor / IMAGES

CORE_SWAP = [(t, t ^ 1) for t in range(8)]
HI_SWAP = [(s, s ^ 1) for s in range(8)]
X_PAIRS = [(s, s ^ 2) for s in range(8)]
X_FAR = [(s, s ^ 4) for s in range(8)]
ORDER = (2, 1, 3)
Z_STEP = {1: 1, 2: 2, 3: 7}


def y_perm(d):
    return [(2 * y + c, 2 * ((y + d) % 4) + c) for y in range(4) for c in range(2)]


def x_perm(d):
    return [(2 * x + h, 2 * ((x + d) % 4) + h) for x in range(4) for h in range(2)]


def z_perm(d):
    pairs = []
    for z in range(8):
        w = (z + d) % 8
        for x in range(4):
            pairs.append(((z % 4) * 8 + 2 * x + z // 4, (w % 4) * 8 + 2 * x + w // 4))
    return pairs


def core_swap(v):
    return lax.ppermute(v, "tensor", CORE_SWAP)


def y_send(v, d):
    return lax.ppermute(v, "tensor", y_perm(d))


def x_send(v, d):
    return lax.ppermute(v, "space", x_perm(d))


def z_send(v, d):
    return lax.ppermute(v, ("dp", "space"), z_perm(d))


def place_of():
    t = lax.axis_index("tensor")
    s = lax.axis_index("space")
    lo = lax.axis_index("dp")
    return t // 2, lax.rem(t, 2), s, s // 2, 4 * lax.rem(s, 2) + lo, lo


def call(kernel, outs, scratch, *args, flops=0, far=(), far_out=()):
    vm = pl.BlockSpec(memory_space=pltpu.VMEM)
    anywhere = pl.BlockSpec(memory_space=pl.ANY)
    total = sum(math.prod(a.shape) * a.dtype.itemsize for a in args)
    total += sum(math.prod(o.shape) * o.dtype.itemsize for o in outs)
    return pl.pallas_call(
        kernel,
        out_shape=tuple(outs),
        in_specs=[anywhere if k in far else vm for k in range(len(args))],
        out_specs=tuple(anywhere if k in far_out else vm for k in range(len(outs))),
        scratch_shapes=scratch,
        compiler_params=pltpu.CompilerParams(vmem_limit_bytes=48 << 20),
        cost_estimate=pl.CostEstimate(flops=flops, bytes_accessed=total, transcendentals=0),
    )(*args)


def out(shape, dtype):
    return jax.ShapeDtypeStruct(shape, dtype)


def conv_rows(acc, source, rows, weight, contract):
    flat = source.reshape(-1, CHANS)
    for b in range(3):
        total = None
        for a in range(3):
            part = lax.dot_general(
                flat[a * COLS : (a + rows) * COLS],
                weight(a, b),
                (((1,), (contract,)), ((), ())),
                preferred_element_type=F32,
            )
            total = part if total is None else total + part
        acc[b] = total.reshape(rows, COLS, 256)
    edge = jnp.zeros((rows, 1, 256), F32)
    left, right = acc[0], acc[2]
    return (
        acc[1]
        + jnp.concatenate([edge, left[:, : COLS - 1]], 1)
        + jnp.concatenate([right[:, 1:], edge], 1)
    )


def inside_rows(start, rows):
    row = start + lax.broadcasted_iota(jnp.int32, (rows, COLS, 256), 0)
    return (row >= 0) & (row < HEIGHT)


def split_rows(row):
    hi = row.astype(BF).astype(F32)
    mid = (row - hi).astype(BF).astype(F32)
    return [hi, mid, row - hi - mid]


def rows_block(rows, height, width):
    at = lax.broadcasted_iota(jnp.int32, (height, width), 0)
    block = jnp.zeros((height, width), F32)
    for k, row in enumerate(rows):
        block = jnp.where(at == k, row, block)
    return block.astype(BF)


def pack_kernel(kern, own, m1, m2, m3, sems):
    y, _, _, _, _, _ = place_of()
    jobs = []
    for d, m in enumerate((m1, m2, m3), 1):
        columns = pl.ds(pl.multiple_of(lax.rem(y + d, 4) * 256, 256), 256)
        pairs = [(kern.at[:, :, columns], m.at[0:9])]
        for k in range(4):
            pairs.append((own.at[:, k * 256 : (k + 1) * 256], m.at[9 + k]))
        for source, target in pairs:
            job = pltpu.make_async_copy(source, target, sems.at[len(jobs)])
            job.start()
            jobs.append(job)
    for job in jobs:
        job.wait()


def hidden_kernel(*refs):
    own, own_other, kern, kother = refs[0:4]
    mine, other = refs[4:7], refs[7:10]
    halo, r1, r2, r3, crossed, e_ref = refs[10:16]
    gh_ref, hid_ref, stat_ref, part_ref, x_out, w_out = refs[16:22]
    x_ref, w_ref, acc, sems = refs[22:26]
    y, c, s, _, _, _ = place_of()
    columns = pl.ds(pl.multiple_of(y * 256, 256), 256)
    copies = []

    def copy(source, target):
        job = pltpu.make_async_copy(source, target, sems.at[len(copies)])
        job.start()
        copies.append(job)

    for d in range(4):
        at = lax.rem(y + 4 - d, 4)
        for core, whole, weights, pieces in ((c, own, kern, mine), (1 - c, own_other, kother, other)):
            rows = pl.ds(pl.multiple_of((3 + 4 * at + 2 * core) * COLS, COLS), 2 * COLS)
            block = pl.ds(pl.multiple_of((2 * at + core) * 128, 128), 128)
            if d == 0:
                copy(whole, x_ref.at[rows, :])
                copy(weights.at[:, :, columns], w_ref.at[:, block, :])
            else:
                piece = pieces[d - 1]
                copy(piece.at[0:9], w_ref.at[:, block, :])
                for k in range(4):
                    copy(piece.at[9 + k], x_ref.at[rows, k * 256 : (k + 1) * 256])
    def row(k, count=1):
        return slice(k * COLS, (k + count) * COLS)

    for source, up, down in ((halo, 3, 0), (r1, 0, 1), (r2, 1, 2), (r3, 2, 3)):

        @pl.when((y == up) & (c == 0))
        def _():
            x_ref[row(0)] = source[row(1)]

        @pl.when((y == up) & (c == 1))
        def _():
            x_ref[row(2)] = source[row(1)]

        @pl.when((y == down) & (c == 0))
        def _():
            x_ref[row(19)] = source[row(0)]

        @pl.when((y == down) & (c == 1))
        def _():
            x_ref[row(21)] = source[row(0)]

    @pl.when(c == 0)
    def _():
        x_ref[row(1, 2)] = crossed[...]

    @pl.when(c == 1)
    def _():
        x_ref[row(19, 2)] = crossed[...]

    for job in copies:
        job.wait()
    jobs = [
        pltpu.make_async_copy(x_ref.at[row(2, 18)], x_out, sems.at[34]),
        pltpu.make_async_copy(w_ref, w_out, sems.at[35]),
    ]
    for job in jobs:
        job.start()
    hidden = conv_rows(acc, x_ref[pl.ds(pl.multiple_of(640 * c, 128), 768)], 10, lambda a, b: w_ref[3 * a + b], 0)
    acc[0] = hidden
    sig = jax.nn.sigmoid(hidden)
    slope = sig * (1.0 + hidden * (1.0 - sig))
    e = e_ref[0:1, :].reshape(1, 1, 256)
    gh = jnp.where(inside_rows(16 * s - 2 + 10 * c, 10), e * slope * SCALE, 0.0)
    gh_ref[...] = gh.astype(BF).reshape(640, 256)
    own = acc[0, pl.ds(2 - 2 * c, 8)]
    hid_ref[...] = own
    act = own * jax.nn.sigmoid(own)
    act_sum = jnp.sum(jnp.sum(act, axis=0), axis=0, keepdims=True)
    part = SCALE * jnp.sum(act_sum * e_ref[0:1, :])
    stat_ref[...] = jnp.broadcast_to(act_sum, (8, 256))
    part_ref[...] = jnp.full((8, 128), part, F32)
    for job in jobs:
        job.wait()


def sum_rows(tail):
    t = tail.astype(F32)
    return t[0:1] + t[1:2] + t[2:3]


def input_kernel(p0, p1, p2, p3, swapped, kern, kother, part, gi_ref, full, acc):
    y, c, s, _, _, _ = place_of()
    for d, piece in enumerate((p0, p1, p2, p3)):
        at = pl.multiple_of(lax.rem(y + 4 - d, 4) * 256, 256)
        full[pl.ds(c, 10), :, pl.ds(at, 256)] = piece[...].reshape(10, COLS, 256)
        full[pl.ds(10 * (1 - c), 1), :, pl.ds(at, 256)] = swapped[d * 64 : d * 64 + 64].reshape(
            1, COLS, 256
        )

    def weight(a, b):
        tap = 3 * (2 - a) + 2 - b
        return jnp.concatenate([kern[tap], kother[tap]], 0)

    grad = conv_rows(acc, full[...], 9, weight, 1)
    turned = jnp.concatenate([grad[:, :, 128:], grad[:, :, :128]], 2)
    grad = jnp.where(c == 0, grad, turned)
    grad = jnp.where(inside_rows(16 * s - 1 + 9 * c, 9), grad, 0.0)
    gi_ref[0:576] = grad.astype(BF).reshape(576, 256)
    row = jnp.concatenate([part[0:1], part[0:1]], 1)
    gi_ref[576:592] = rows_block(split_rows(row), 16, 256)


def second_kernel(
    p0, p1, p2, p3, swapped, w_ref, hid_ref, stat_ref, e_ref, pre_ref, vec_ref, full, acc
):
    y, c, _, _, _, _ = place_of()
    score = jnp.zeros((1, 128), F32)
    for d, piece in enumerate((p0, p1, p2, p3)):
        score = score + sum_rows(piece[576:592])[:, :128]
        at = pl.multiple_of(lax.rem(y + 4 - d, 4) * 256, 256)
        near = pl.multiple_of(at + 128 * c, 128)
        away = pl.multiple_of(at + 128 * (1 - c), 128)
        full[pl.ds(c, 9), :, pl.ds(at, 256)] = piece[0:576].reshape(9, COLS, 256)
        full[pl.ds(9 * (1 - c), 1), :, pl.ds(near, 128)] = swapped[d, pl.ds(8 * c, 1)]
        full[pl.ds(9 * (1 - c), 1), :, pl.ds(away, 128)] = swapped[d, 9:10]
    second = conv_rows(acc, full[...], 8, lambda a, b: w_ref[3 * a + b], 0)
    hidden = hid_ref[...]
    sig = jax.nn.sigmoid(hidden)
    slope = sig * (1.0 + hidden * (1.0 - sig))
    curve = sig * (1.0 - sig) * (2.0 + hidden * (1.0 - 2.0 * sig))
    e = e_ref[0:1, :].reshape(1, 1, 256)
    coeff = -jax.nn.sigmoid(-score[0:1, 0:1]) / IMAGES
    c3 = coeff.reshape(1, 1, 1)
    pre = c3 * e * slope * SCALE + GWEIGHT * second * e * curve * SCALE
    pre_ref[0:512] = pre.astype(BF).reshape(512, 256)
    part = jnp.sum(jnp.sum(second * slope, axis=0), axis=0, keepdims=True)
    vec = coeff * SCALE * stat_ref[0:1] + GWEIGHT * SCALE * part
    pre_ref[512:528] = rows_block(split_rows(vec), 16, 256)
    vec_ref[...] = jnp.broadcast_to(vec, (8, 256))


def power_of(top):
    power = 7.0 - jnp.ceil(jnp.log2(jnp.maximum(top, 1e-30)) + 0.01)
    return jnp.clip(power, -100.0, 100.0)


def encode(v, power):
    u = v * jnp.exp2(power)
    q = u * u
    q = q * q
    q = q * q
    q = q * q
    return jnp.where(u < 0, -q, q).astype(BF)


def decode(code, power):
    f = code.astype(F32)
    mag = jnp.exp2(jnp.log2(jnp.abs(f)) * (1.0 / 16.0) - power)
    return jnp.where(f < 0, -mag, mag)


def shifted(v, target):
    edge = jnp.zeros((16, 1, 128), F32)
    f = v.astype(F32)
    target[:, 0:128] = jnp.concatenate([f[:, 1:], edge], 1).astype(BF).reshape(1024, 128)
    target[:, 128:256] = v.reshape(1024, 128)
    target[:, 256:384] = jnp.concatenate([edge, f[:, : COLS - 1]], 1).astype(BF).reshape(1024, 128)


def lane_top(v):
    return power_of(jnp.max(jnp.abs(v), axis=0, keepdims=True))


def corr_kernel(
    h, x_ref, p0, p1, p2, p3, take, gh, gho, pre, preo, vec,
    own, m1, m2, m3, evec_ref, xh, gih, both, g_gh, g_pre, wsum,
):
    y, c, _, x, _, lo = place_of()
    lanes = slice(128 * h, 128 * h + 128)
    for k in range(4):
        at = pl.multiple_of((2 * k + c) * 128, 128)
        xh[:, k * 128 : (k + 1) * 128] = x_ref[:, pl.ds(at, 128)]
    half = pl.multiple_of(c * 128, 128)
    for d, piece in enumerate((p0, p1, p2, p3)):
        at = pl.multiple_of(lax.rem(y + 4 - d, 4) * 128, 128)
        here = pl.ds(pl.multiple_of(576 * c, 64), 576)
        there = pl.ds(pl.multiple_of(576 * (1 - c), 64), 576)
        gih[here, pl.ds(at, 128)] = piece[0:576, pl.ds(half, 128)]
        gih[there, pl.ds(at, 128)] = take[d, 0:9].reshape(576, 128)
    own_rows = pl.ds(pl.multiple_of(128 - 128 * c, 128), 512)
    both[pl.ds(8 * c, 8)] = gh[own_rows, lanes].reshape(8, COLS, 128)
    both[pl.ds(8 * (1 - c), 8)] = gho[256:768, lanes].reshape(8, COLS, 128)
    shifted(both[...], g_gh)
    both[pl.ds(8 * c, 8)] = pre[0:512, lanes].reshape(8, COLS, 128)
    both[pl.ds(8 * (1 - c), 8)] = preo[0:512, lanes].reshape(8, COLS, 128)
    shifted(both[...], g_pre)
    for a in range(3):
        adv = lax.dot_general(
            xh[a * COLS : a * COLS + 1024], g_pre[...], (((0,), (0,)), ((), ())),
            preferred_element_type=F32,
        )
        direct = lax.dot_general(
            gih[a * COLS : a * COLS + 1024], g_gh[...], (((0,), (0,)), ((), ())),
            preferred_element_type=F32,
        )
        total = adv + GWEIGHT * direct
        for b in range(3):
            wsum[3 * a + b] = total[:, b * 128 : b * 128 + 128].reshape(4, 4, 32, 128)
    evec = vec[0:1, pl.ds(half, 128)] + sum_rows(preo[512:528, pl.ds(half, 128)])
    evec_ref[...] = jnp.broadcast_to(evec, (8, 128))
    extra = split_rows(evec)
    at = (x, lo)[h]
    own[...] = wsum[:, :, pl.ds(at, 1)].reshape(1152, 128)
    for d, m in enumerate((m1, m2, m3), 1):
        part = wsum[:, :, pl.ds(lax.rem(at + d, 4), 1)].reshape(1152, 128)
        power = lane_top(part)
        m[0:1152] = encode(part, power)
        m[1152:1168] = rows_block([power] + extra, 16, 128)


def added(own, messages, size):
    t = own[...]
    for m in messages:
        t = t + decode(m[0:size], m[size : size + 16][0:1].astype(F32))
    return t


def label_rows(label):
    tag = jnp.broadcast_to(label[...], (1, 128)).astype(F32)
    high = jnp.floor(tag * (1.0 / 32.0))
    return [high, tag - 32.0 * high]


def first_sum_kernel(h, own, evec_in, label, m1, m2, m3, mine, c1, c2, c3, evec_ref, total):
    _, _, _, x, _, lo = place_of()
    evec = evec_in[0:1]
    for m in (m1, m2, m3):
        evec = evec + sum_rows(m[1152:1168][1:4])
    evec_ref[...] = jnp.broadcast_to(evec, (8, 128))
    extra = split_rows(evec) + label_rows(label)
    at = (lo, x)[h]
    total[...] = added(own, (m1, m2, m3), 1152).reshape(36, 4, 8, 128)
    mine[...] = total[:, pl.ds(at, 1)].reshape(288, 128)
    for d, m in enumerate((c1, c2, c3), 1):
        part = total[:, pl.ds(lax.rem(at + d, 4), 1)].reshape(288, 128)
        power = lane_top(part)
        m[0:288] = encode(part, power)
        m[288:304] = rows_block([power] + extra, 16, 128)


def second_sum_kernel(h, own, evec_in, label, m1, m2, m3, m_ref):
    _, _, _, _, _, lo = place_of()
    t = added(own, (m1, m2, m3), 288)
    power = lane_top(t)
    m_ref[0:288] = encode(t, power)
    rows = [power]
    if h == 0:
        lane = lax.broadcasted_iota(jnp.int32, (1, 128), 1)
        found = [(lo, split_rows(evec_in[0:1]) + label_rows(label))]
        for d, m in enumerate((m1, m2, m3), 1):
            t = m[288:304].astype(F32)
            found.append((lax.rem(lo + 4 - d, 4), [t[k : k + 1] for k in range(1, 6)]))
        zero = jnp.zeros((1, 128), F32)
        for slot in range(4):
            for k in range(3):
                row = zero
                for at, parts in found:
                    row = jnp.where(at == slot, parts[k], row)
                rows.append(row)
        for k in (3, 4):
            row = zero
            for at, parts in found:
                row = jnp.where(lane == at, parts[k], row)
            rows.append(row)
    m_ref[288:304] = rows_block(rows, 16, 128)


def pair_kernel(h, mine, theirs, y0, y1, y2, y3, *rest):
    y, _, _, _, _, _ = place_of()
    total = rest[-1]
    t1 = mine[288:304].astype(F32)
    t2 = theirs[288:304].astype(F32)
    value = decode(mine[0:288], t1[0:1]) + decode(theirs[0:288], t2[0:1])
    total[...] = value.reshape(9, 4, 8, 128)
    for d, target in enumerate((y0, y1, y2, y3)):
        target[...] = total[:, pl.ds(lax.rem(y + d, 4), 1)].reshape(72, 128)
    if h == 0:
        row = lax.broadcasted_iota(jnp.int32, (1000, 128), 0)
        egrad = jnp.zeros((1000, 128), F32)
        for slot in range(4):
            at = 1 + 3 * slot
            vec = sum_rows(t1[at : at + 3]) + sum_rows(t2[at : at + 3])
            tag = 32.0 * t1[13:14, slot : slot + 1] + t1[14:15, slot : slot + 1]
            egrad = egrad + jnp.where(row == tag.astype(jnp.int32), vec, 0.0)
        rest[0][...] = egrad


def code_kernel(y0, y1, y2, y3, m_ref):
    y, _, _, _, _, _ = place_of()
    row = lax.broadcasted_iota(jnp.int32, (8, 128), 0)
    tail = jnp.zeros((8, 128), F32)
    for d, piece in enumerate((y0, y1, y2, y3)):
        at = lax.rem(y + 4 - d, 4)
        v = piece[...]
        power = lane_top(v)
        m_ref[pl.ds(9 * at, 9)] = encode(v, power).reshape(9, 8, 128)
        tail = jnp.where(row == at, power, tail)
    m_ref[36] = tail.astype(BF)


def final_kernel(a0, a1, a2, a3, b0, b1, b2, b3, out_ref):
    _, _, _, x, _, lo = place_of()
    for h, blocks in enumerate(((a0, a1, a2, a3), (b0, b1, b2, b3))):
        for d, block in enumerate(blocks):
            for k in range(4):
                if h == 0:
                    u = 32 * lax.rem(x + 4 - d, 4) + 8 * lax.rem(lo + 4 - k, 4)
                else:
                    u = 32 * lax.rem(lo + 4 - d, 4) + 8 * lax.rem(x + 4 - k, 4)
                rows = pl.ds(pl.multiple_of(u, 8), 8)
                powers = block[k, 36].astype(F32)
                for yy in range(4):
                    lanes = slice(yy * 256 + h * 128, yy * 256 + h * 128 + 128)
                    values = decode(
                        block[k, 9 * yy : 9 * yy + 9], powers[yy : yy + 1].reshape(1, 1, 128)
                    )
                    out_ref[:, rows, lanes] = values


def body(features, kernel, embedding, labels):
    t = lax.axis_index("tensor")
    y, c = t // 2, lax.rem(t, 2)
    first = c == 0

    def by_core(zero, one):
        return jnp.where(first, zero, one)

    def y_all(v):
        got = {d: y_send(v, d) for d in ORDER}
        return [v, got[1], got[2], got[3]]

    def x_all(values):
        got = {d: x_send(values[d - 1], d) for d in ORDER}
        return [got[d] for d in (1, 2, 3)]

    def z_all(values):
        got = {d: z_send(values[d - 1], Z_STEP[d]) for d in ORDER}
        return [got[d] for d in (1, 2, 3)]

    own = features.reshape(2 * COLS, CHANS)
    kern = kernel.reshape(9, 128, CHANS)
    packed = call(
        pack_kernel,
        [out((13, 128, 256), BF)] * 3,
        [pltpu.SemaphoreType.DMA((15,))],
        kern, own,
        far=range(2),
        far_out=range(3),
    )
    halo_pairs = []
    for q in range(7):
        for k in range(2):
            halo_pairs.append((q * 8 + 6 + k, (q + 1) * 8 + 6 + k))
            halo_pairs.append(((q + 1) * 8 + k, q * 8 + k))
    halo = lax.ppermute(own, ("space", "tensor"), halo_pairs)
    mine = {d: y_send(packed[d - 1], d) for d in ORDER}
    kother = core_swap(kern)
    own_other = core_swap(own)

    def halo_pairs_y(d):
        return [(6 + k, 2 * ((3 + d) % 4) + k) for k in range(2)] + [
            (k, 2 * d + k) for k in range(2)
        ]

    r1, r2, r3 = (lax.ppermute(halo, "tensor", halo_pairs_y(d)) for d in (1, 2, 3))
    top = jnp.where(y == 0, r1, jnp.where(y == 1, r2, jnp.where(y == 2, r3, halo)))
    bottom = jnp.where(y == 0, halo, jnp.where(y == 1, r1, jnp.where(y == 2, r2, r3)))
    crossed = core_swap(by_core(bottom, top))
    other = [core_swap(mine[d]) for d in (1, 2, 3)]

    e_own = jnp.broadcast_to(lax.dynamic_slice_in_dim(embedding, labels[0], 1, 0), (8, 128))
    e_other = core_swap(e_own)
    e = by_core(
        jnp.concatenate([e_own, e_other], 1), jnp.concatenate([e_other, e_own], 1)
    )

    gh, hidden, stat, part, x_rows, w = call(
        hidden_kernel,
        [
            out((640, 256), BF),
            out((8, COLS, 256), F32),
            out((8, 256), F32),
            out((8, 128), F32),
            out((18 * COLS, CHANS), BF),
            out((9, CHANS, 256), BF),
        ],
        [
            pltpu.VMEM((22 * COLS, CHANS), BF),
            pltpu.VMEM((9, CHANS, 256), BF),
            pltpu.VMEM((3, 10, COLS, 256), F32),
            pltpu.SemaphoreType.DMA((36,)),
        ],
        own, own_other, kern, kother, mine[1], mine[2], mine[3], *other,
        halo, r1, r2, r3, crossed, e,
        flops=2 * 640 * 9 * 1024 * 256,
        far=range(10),
        far_out=(4, 5),
    )

    got = {1: y_send(gh, 1), 3: y_send(gh, 3)}
    part = part + core_swap(part)
    part = part + x_send(part, 1) + x_send(part, 2) + x_send(part, 3)
    part, late = lax.optimization_barrier((part, gh))
    got[2] = y_send(late, 2)
    part = part + lax.ppermute(part, "space", HI_SWAP)
    gh_pieces = [gh, got[1], got[2], got[3]]
    rows = [by_core(p[576:640], p[0:64]) for p in gh_pieces]
    rows.append(by_core(gh[128:640], gh[0:512]))
    gh_other = core_swap(jnp.concatenate(rows, 0))
    (gi,) = call(
        input_kernel,
        [out((592, 256), BF)],
        [pltpu.VMEM((11, COLS, CHANS), BF), pltpu.VMEM((3, 9, COLS, 256), F32)],
        *gh_pieces, gh_other, kern, kother, part,
        flops=2 * 576 * 9 * 1024 * 256,
    )

    gi_pieces = y_all(gi)
    rows = []
    for p in gi_pieces:
        low, high = p[0:576, :128], p[0:576, 128:]
        edge = by_core(low[512:576], high[0:64])
        rows.append(jnp.concatenate([by_core(high, low), edge], 0))
    take = core_swap(jnp.stack(rows).reshape(4, 10, COLS, 128))
    pre, vec = call(
        second_kernel,
        [out((528, 256), BF), out((8, 256), F32)],
        [pltpu.VMEM((10, COLS, CHANS), BF), pltpu.VMEM((3, 8, COLS, 256), F32)],
        *gi_pieces, take, w, hidden, stat, e,
        flops=2 * 512 * 9 * 1024 * 256,
    )
    pre_other = core_swap(pre)

    def correlate(h):
        own_h, m1, m2, m3, evec = call(
            functools.partial(corr_kernel, h),
            [out((1152, 128), F32)] + [out((1168, 128), BF)] * 3 + [out((8, 128), F32)],
            [
                pltpu.VMEM((18 * COLS, 512), BF),
                pltpu.VMEM((18 * COLS, 512), BF),
                pltpu.VMEM((16, COLS, 128), BF),
                pltpu.VMEM((1024, 384), BF),
                pltpu.VMEM((1024, 384), BF),
                pltpu.VMEM((9, 4, 4, 32, 128), F32),
            ],
            x_rows, *gi_pieces, take, gh, gh_other, pre, pre_other, vec,
            flops=2 * 1024 * 9 * 512 * 256,
        )
        return own_h, evec, (m1, m2, m3)

    label = labels.reshape(1, 1)

    def reduced(h, own_h, evec, sent):
        send_first, send_then = ((x_all, z_all), (z_all, x_all))[h]
        got = send_first(sent)
        mine_h, c1, c2, c3, evec = call(
            functools.partial(first_sum_kernel, h),
            [out((288, 128), F32)] + [out((304, 128), BF)] * 3 + [out((8, 128), F32)],
            [pltpu.VMEM((36, 4, 8, 128), F32)],
            own_h, evec, label, *got,
        )
        got = send_then((c1, c2, c3))
        (message,) = call(
            functools.partial(second_sum_kernel, h),
            [out((304, 128), BF)],
            [],
            mine_h, evec, label, *got,
        )
        theirs = z_send(message, 4)
        y0, y1, y2, y3, *egrad = call(
            functools.partial(pair_kernel, h),
            [out((72, 128), F32)] * 4 + [out((1000, 128), F32)] * (1 - h),
            [pltpu.VMEM((9, 4, 8, 128), F32)],
            message, theirs,
        )
        sent = {1: y1, 2: y2, 3: y3}
        got = {d: y_send(sent[d], d) for d in ORDER}
        (code,) = call(code_kernel, [out((37, 8, 128), BF)], [], y0, got[1], got[2], got[3])
        code = jnp.stack([code] + send_then([code] * 3))
        return [code] + send_first([code] * 3), egrad

    first_half = correlate(0)
    second_half = correlate(1)
    codes_a, egrad = reduced(0, *first_half)
    codes_b, _ = reduced(1, *second_half)
    (wtotal,) = call(
        final_kernel,
        [out((9, 128, CHANS), F32)],
        [],
        *codes_a, *codes_b,
    )
    return (wtotal.reshape(3, 3, 128, CHANS), egrad[0])


def solution(mesh):
    placed = (
        P("dp", ("space", "tensor"), None, None),
        P(None, None, "tensor", None),
        P(None, "tensor"),
        P("dp"),
    )
    return jax.shard_map(
        body,
        mesh=mesh,
        in_specs=placed,
        out_specs=(P(None, None, "tensor", None), P(None, "tensor")),
        check_vma=False,
    )
```

```python
import functools
import math

import jax
import jax.numpy as jnp
from jax import lax
from jax.experimental import pallas as pl
from jax.experimental.pallas import tpu as pltpu
from jax.sharding import PartitionSpec as P

r1_factor = 1000.0
BF = jnp.bfloat16
F32 = jnp.float32

IMAGES, HEIGHT, COLS, CHANS = 4, 128, 64, 1024
SCALE = 1.0 / math.sqrt(HEIGHT * COLS * CHANS)
GWEIGHT = r1_factor / IMAGES

CORE_SWAP = [(t, t ^ 1) for t in range(8)]
HI_SWAP = [(s, s ^ 1) for s in range(8)]
X_PAIRS = [(s, s ^ 2) for s in range(8)]
X_FAR = [(s, s ^ 4) for s in range(8)]
ORDER = (2, 1, 3)
Z_STEP = {1: 1, 2: 2, 3: 7}


def y_perm(d):
    return [(2 * y + c, 2 * ((y + d) % 4) + c) for y in range(4) for c in range(2)]


def x_perm(d):
    return [(2 * x + h, 2 * ((x + d) % 4) + h) for x in range(4) for h in range(2)]


def z_perm(d):
    pairs = []
    for z in range(8):
        w = (z + d) % 8
        for x in range(4):
            pairs.append(((z % 4) * 8 + 2 * x + z // 4, (w % 4) * 8 + 2 * x + w // 4))
    return pairs


def core_swap(v):
    return lax.ppermute(v, "tensor", CORE_SWAP)


def y_send(v, d):
    return lax.ppermute(v, "tensor", y_perm(d))


def x_send(v, d):
    return lax.ppermute(v, "space", x_perm(d))


def z_send(v, d):
    return lax.ppermute(v, ("dp", "space"), z_perm(d))


def place_of():
    t = lax.axis_index("tensor")
    s = lax.axis_index("space")
    lo = lax.axis_index("dp")
    return t // 2, lax.rem(t, 2), s, s // 2, 4 * lax.rem(s, 2) + lo, lo


def call(kernel, outs, scratch, *args, flops=0, far=(), far_out=()):
    vm = pl.BlockSpec(memory_space=pltpu.VMEM)
    anywhere = pl.BlockSpec(memory_space=pl.ANY)
    total = sum(math.prod(a.shape) * a.dtype.itemsize for a in args)
    total += sum(math.prod(o.shape) * o.dtype.itemsize for o in outs)
    return pl.pallas_call(
        kernel,
        out_shape=tuple(outs),
        in_specs=[anywhere if k in far else vm for k in range(len(args))],
        out_specs=tuple(anywhere if k in far_out else vm for k in range(len(outs))),
        scratch_shapes=scratch,
        compiler_params=pltpu.CompilerParams(vmem_limit_bytes=48 << 20),
        cost_estimate=pl.CostEstimate(flops=flops, bytes_accessed=total, transcendentals=0),
    )(*args)


def out(shape, dtype):
    return jax.ShapeDtypeStruct(shape, dtype)


def conv_rows(acc, source, rows, weight, contract):
    flat = source.reshape(-1, CHANS)
    for b in range(3):
        total = None
        for a in range(3):
            part = lax.dot_general(
                flat[a * COLS : (a + rows) * COLS],
                weight(a, b),
                (((1,), (contract,)), ((), ())),
                preferred_element_type=F32,
            )
            total = part if total is None else total + part
        acc[b] = total.reshape(rows, COLS, 256)
    edge = jnp.zeros((rows, 1, 256), F32)
    left, right = acc[0], acc[2]
    return (
        acc[1]
        + jnp.concatenate([edge, left[:, : COLS - 1]], 1)
        + jnp.concatenate([right[:, 1:], edge], 1)
    )


def inside_rows(start, rows):
    row = start + lax.broadcasted_iota(jnp.int32, (rows, COLS, 256), 0)
    return (row >= 0) & (row < HEIGHT)


def split_rows(row):
    hi = row.astype(BF).astype(F32)
    mid = (row - hi).astype(BF).astype(F32)
    return [hi, mid, row - hi - mid]


def rows_block(rows, height, width):
    at = lax.broadcasted_iota(jnp.int32, (height, width), 0)
    block = jnp.zeros((height, width), F32)
    for k, row in enumerate(rows):
        block = jnp.where(at == k, row, block)
    return block.astype(BF)


def pack_kernel(kern, m1, m2, m3, sems):
    y, _, _, _, _, _ = place_of()
    jobs = []
    for d, m in enumerate((m1, m2, m3), 1):
        columns = pl.ds(pl.multiple_of(lax.rem(y + d, 4) * 256, 256), 256)
        job = pltpu.make_async_copy(kern.at[:, :, columns], m, sems.at[d - 1])
        job.start()
        jobs.append(job)
    for job in jobs:
        job.wait()


def hidden_kernel(*refs):
    mine, other, halo, kern, kother = refs[0:4], *refs[4:8]
    cols, cols_other, e_ref = refs[8:11], refs[11:14], refs[14]
    gh_ref, hid_ref, stat_ref, part_ref, x_out, w_out = refs[15:21]
    x_ref, w_ref, acc, sems = refs[21:25]
    y, c, s, _, _, _ = place_of()
    columns = pl.ds(pl.multiple_of(y * 256, 256), 256)
    copies = []

    def copy(source, target):
        job = pltpu.make_async_copy(source, target, sems.at[len(copies)])
        job.start()
        copies.append(job)

    for d in range(4):
        at = lax.rem(y + 4 - d, 4)
        rows = pl.ds(pl.multiple_of((3 + 4 * at + 2 * c) * COLS, COLS), 2 * COLS)
        copy(mine[d], x_ref.at[rows, :])
        rows = pl.ds(pl.multiple_of((5 + 4 * at - 2 * c) * COLS, COLS), 2 * COLS)
        copy(other.at[d], x_ref.at[rows, :])
        for core, whole, pieces in ((c, kern, cols), (1 - c, kother, cols_other)):
            block = pl.ds(pl.multiple_of((2 * at + core) * 128, 128), 128)
            source = pieces[d - 1] if d else whole.at[:, :, columns]
            copy(source, w_ref.at[:, block, :])
    copy(halo, x_ref.at[pl.ds(pl.multiple_of(19 * COLS * c, COLS), 3 * COLS), :])
    for job in copies:
        job.wait()
    jobs = [
        pltpu.make_async_copy(x_ref.at[2 * COLS : 20 * COLS], x_out, sems.at[17]),
        pltpu.make_async_copy(w_ref, w_out, sems.at[18]),
    ]
    for job in jobs:
        job.start()
    hidden = conv_rows(acc, x_ref[pl.ds(pl.multiple_of(640 * c, 128), 768)], 10, lambda a, b: w_ref[3 * a + b], 0)
    acc[0] = hidden
    sig = jax.nn.sigmoid(hidden)
    slope = sig * (1.0 + hidden * (1.0 - sig))
    e = e_ref[0:1, :].reshape(1, 1, 256)
    gh = jnp.where(inside_rows(16 * s - 2 + 10 * c, 10), e * slope * SCALE, 0.0)
    gh_ref[...] = gh.astype(BF).reshape(640, 256)
    own = acc[0, pl.ds(2 - 2 * c, 8)]
    hid_ref[...] = own
    act = own * jax.nn.sigmoid(own)
    act_sum = jnp.sum(jnp.sum(act, axis=0), axis=0, keepdims=True)
    part = SCALE * jnp.sum(act_sum * e_ref[0:1, :])
    stat_ref[...] = jnp.broadcast_to(act_sum, (8, 256))
    part_ref[...] = jnp.full((8, 128), part, F32)
    for job in jobs:
        job.wait()


def sum_rows(tail):
    t = tail.astype(F32)
    return t[0:1] + t[1:2] + t[2:3]


def input_kernel(p0, p1, p2a, p2b, p3, swapped, kern, kother, part, gi_ref, full, acc):
    y, c, s, _, _, _ = place_of()
    for d in range(4):
        at = pl.multiple_of(lax.rem(y + 4 - d, 4) * 256, 256)
        if d == 2:
            full[pl.ds(c, 5), :, pl.ds(at, 256)] = p2a[...].reshape(5, COLS, 256)
            full[pl.ds(c + 5, 5), :, pl.ds(at, 256)] = p2b[...].reshape(5, COLS, 256)
        else:
            full[pl.ds(c, 10), :, pl.ds(at, 256)] = (p0, p1, p2a, p3)[d][...].reshape(10, COLS, 256)
        full[pl.ds(10 * (1 - c), 1), :, pl.ds(at, 256)] = swapped[d * 64 : d * 64 + 64].reshape(
            1, COLS, 256
        )

    def weight(a, b):
        tap = 3 * (2 - a) + 2 - b
        return jnp.concatenate([kern[tap], kother[tap]], 0)

    grad = conv_rows(acc, full[...], 9, weight, 1)
    turned = jnp.concatenate([grad[:, :, 128:], grad[:, :, :128]], 2)
    grad = jnp.where(c == 0, grad, turned)
    grad = jnp.where(inside_rows(16 * s - 1 + 9 * c, 9), grad, 0.0)
    gi_ref[0:576] = grad.astype(BF).reshape(576, 256)
    row = jnp.concatenate([part[0:1], part[0:1]], 1)
    gi_ref[576:592] = rows_block(split_rows(row), 16, 256)


def second_kernel(
    p0, p1, p2, p3, swapped, w_ref, hid_ref, stat_ref, e_ref, pre_ref, vec_ref, full, acc
):
    y, c, _, _, _, _ = place_of()
    score = jnp.zeros((1, 128), F32)
    for d, piece in enumerate((p0, p1, p2, p3)):
        score = score + sum_rows(piece[576:592])[:, :128] + sum_rows(swapped[d, 640:656])
        at = pl.multiple_of(lax.rem(y + 4 - d, 4) * 256, 256)
        near = pl.multiple_of(at + 128 * c, 128)
        away = pl.multiple_of(at + 128 * (1 - c), 128)
        full[pl.ds(c, 9), :, pl.ds(at, 256)] = piece[0:576].reshape(9, COLS, 256)
        full[pl.ds(9 * (1 - c), 1), :, pl.ds(near, 128)] = swapped[
            d, pl.ds(pl.multiple_of(8 * COLS * c, COLS), COLS)
        ].reshape(1, COLS, 128)
        full[pl.ds(9 * (1 - c), 1), :, pl.ds(away, 128)] = swapped[d, 576:640].reshape(1, COLS, 128)
    second = conv_rows(acc, full[...], 8, lambda a, b: w_ref[3 * a + b], 0)
    hidden = hid_ref[...]
    sig = jax.nn.sigmoid(hidden)
    slope = sig * (1.0 + hidden * (1.0 - sig))
    curve = sig * (1.0 - sig) * (2.0 + hidden * (1.0 - 2.0 * sig))
    e = e_ref[0:1, :].reshape(1, 1, 256)
    coeff = -jax.nn.sigmoid(-score[0:1, 0:1]) / IMAGES
    c3 = coeff.reshape(1, 1, 1)
    pre = c3 * e * slope * SCALE + GWEIGHT * second * e * curve * SCALE
    pre_ref[0:512] = pre.astype(BF).reshape(512, 256)
    part = jnp.sum(jnp.sum(second * slope, axis=0), axis=0, keepdims=True)
    vec = coeff * SCALE * stat_ref[0:1] + GWEIGHT * SCALE * part
    pre_ref[512:528] = rows_block(split_rows(vec), 16, 256)
    vec_ref[...] = jnp.broadcast_to(vec, (8, 256))


def power_of(top):
    power = 7.0 - jnp.ceil(jnp.log2(jnp.maximum(top, 1e-30)) + 0.01)
    return jnp.clip(power, -100.0, 100.0)


def encode(v, power):
    u = v * jnp.exp2(power)
    q = u * u
    q = q * q
    q = q * q
    q = q * q
    return jnp.where(u < 0, -q, q).astype(BF)


def decode(code, power):
    f = code.astype(F32)
    mag = jnp.exp2(jnp.log2(jnp.abs(f)) * (1.0 / 16.0) - power)
    return jnp.where(f < 0, -mag, mag)


def shifted(v, target):
    edge = jnp.zeros((16, 1, 128), F32)
    f = v.astype(F32)
    target[:, 0:128] = jnp.concatenate([f[:, 1:], edge], 1).astype(BF).reshape(1024, 128)
    target[:, 128:256] = v.reshape(1024, 128)
    target[:, 256:384] = jnp.concatenate([edge, f[:, : COLS - 1]], 1).astype(BF).reshape(1024, 128)


def lane_top(v):
    return power_of(jnp.max(jnp.abs(v), axis=0, keepdims=True))


def corr_kernel(
    h, x_ref, x_edge, p0, p1, p2, p3, take, gh, gho, pre, preo, vec,
    own, m1, m2, m3, evec_ref, xh, gih, both, g_gh, g_pre, wsum,
):
    y, c, _, x, _, lo = place_of()
    lanes = slice(128 * h, 128 * h + 128)
    for k in range(4):
        at = pl.multiple_of((2 * k + c) * 128, 128)
        xh[:, k * 128 : (k + 1) * 128] = x_ref[:, pl.ds(at, 128)]
        edge = pl.ds(pl.multiple_of(17 * COLS * (1 - c), COLS), COLS)
        xh[edge, k * 128 : (k + 1) * 128] = x_edge[:, k * 128 : (k + 1) * 128]
    half = pl.multiple_of(c * 128, 128)
    for d, piece in enumerate((p0, p1, p2, p3)):
        at = pl.multiple_of(lax.rem(y + 4 - d, 4) * 128, 128)
        here = pl.ds(pl.multiple_of(576 * c, 64), 576)
        there = pl.ds(pl.multiple_of(576 * (1 - c), 64), 576)
        gih[here, pl.ds(at, 128)] = piece[0:576, pl.ds(half, 128)]
        gih[there, pl.ds(at, 128)] = take[d, 0:576]
    own_rows = pl.ds(pl.multiple_of(128 - 128 * c, 128), 512)
    both[pl.ds(8 * c, 8)] = gh[own_rows, lanes].reshape(8, COLS, 128)
    both[pl.ds(8 * (1 - c), 8)] = gho[256:768, lanes].reshape(8, COLS, 128)
    shifted(both[...], g_gh)
    both[pl.ds(8 * c, 8)] = pre[0:512, lanes].reshape(8, COLS, 128)
    both[pl.ds(8 * (1 - c), 8)] = preo[0:512, lanes].reshape(8, COLS, 128)
    shifted(both[...], g_pre)
    for a in range(3):
        adv = lax.dot_general(
            xh[a * COLS : a * COLS + 1024], g_pre[...], (((0,), (0,)), ((), ())),
            preferred_element_type=F32,
        )
        direct = lax.dot_general(
            gih[a * COLS : a * COLS + 1024], g_gh[...], (((0,), (0,)), ((), ())),
            preferred_element_type=F32,
        )
        total = adv + GWEIGHT * direct
        for b in range(3):
            wsum[3 * a + b] = total[:, b * 128 : b * 128 + 128].reshape(4, 4, 32, 128)
    evec = vec[0:1, pl.ds(half, 128)] + sum_rows(preo[512:528, pl.ds(half, 128)])
    evec_ref[...] = jnp.broadcast_to(evec, (8, 128))
    extra = split_rows(evec)
    at = (x, lo)[h]
    own[...] = wsum[:, :, pl.ds(at, 1)].reshape(1152, 128)
    for d, m in enumerate((m1, m2, m3), 1):
        part = wsum[:, :, pl.ds(lax.rem(at + d, 4), 1)].reshape(1152, 128)
        power = lane_top(part)
        m[0:1152] = encode(part, power)
        m[1152:1168] = rows_block([power] + extra, 16, 128)


def added(own, messages, size):
    t = own[...]
    for m in messages:
        t = t + decode(m[0:size], m[size : size + 16][0:1].astype(F32))
    return t


def label_rows(label):
    tag = jnp.broadcast_to(label[...], (1, 128)).astype(F32)
    high = jnp.floor(tag * (1.0 / 32.0))
    return [high, tag - 32.0 * high]


def first_sum_kernel(h, own, evec_in, label, m1, m2, m3, mine, c1, c2, c3, evec_ref, total):
    _, _, _, x, _, lo = place_of()
    evec = evec_in[0:1]
    for m in (m1, m2, m3):
        evec = evec + sum_rows(m[1152:1168][1:4])
    evec_ref[...] = jnp.broadcast_to(evec, (8, 128))
    extra = split_rows(evec) + label_rows(label)
    at = (lo, x)[h]
    total[...] = added(own, (m1, m2, m3), 1152).reshape(36, 4, 8, 128)
    mine[...] = total[:, pl.ds(at, 1)].reshape(288, 128)
    for d, m in enumerate((c1, c2, c3), 1):
        part = total[:, pl.ds(lax.rem(at + d, 4), 1)].reshape(288, 128)
        power = lane_top(part)
        m[0:288] = encode(part, power)
        m[288:304] = rows_block([power] + extra, 16, 128)


def second_sum_kernel(h, own, evec_in, label, m1, m2, m3, m_ref):
    _, _, _, _, _, lo = place_of()
    t = added(own, (m1, m2, m3), 288)
    power = lane_top(t)
    m_ref[0:288] = encode(t, power)
    rows = [power]
    if h == 0:
        lane = lax.broadcasted_iota(jnp.int32, (1, 128), 1)
        found = [(lo, split_rows(evec_in[0:1]) + label_rows(label))]
        for d, m in enumerate((m1, m2, m3), 1):
            t = m[288:304].astype(F32)
            found.append((lax.rem(lo + 4 - d, 4), [t[k : k + 1] for k in range(1, 6)]))
        zero = jnp.zeros((1, 128), F32)
        for slot in range(4):
            for k in range(3):
                row = zero
                for at, parts in found:
                    row = jnp.where(at == slot, parts[k], row)
                rows.append(row)
        for k in (3, 4):
            row = zero
            for at, parts in found:
                row = jnp.where(lane == at, parts[k], row)
            rows.append(row)
    m_ref[288:304] = rows_block(rows, 16, 128)


def pair_kernel(h, mine, theirs, y0, y1, y2, y3, *rest):
    y, _, _, _, _, _ = place_of()
    total = rest[-1]
    t1 = mine[288:304].astype(F32)
    t2 = theirs[288:304].astype(F32)
    value = decode(mine[0:288], t1[0:1]) + decode(theirs[0:288], t2[0:1])
    total[...] = value.reshape(9, 4, 8, 128)
    for d, target in enumerate((y0, y1, y2, y3)):
        target[...] = total[:, pl.ds(lax.rem(y + d, 4), 1)].reshape(72, 128)
    if h == 0:
        row = lax.broadcasted_iota(jnp.int32, (1000, 128), 0)
        egrad = jnp.zeros((1000, 128), F32)
        for slot in range(4):
            at = 1 + 3 * slot
            vec = sum_rows(t1[at : at + 3]) + sum_rows(t2[at : at + 3])
            tag = 32.0 * t1[13:14, slot : slot + 1] + t1[14:15, slot : slot + 1]
            egrad = egrad + jnp.where(row == tag.astype(jnp.int32), vec, 0.0)
        rest[0][...] = egrad


def code_kernel(y0, y1, y2, y3, m_ref):
    y, _, _, _, _, _ = place_of()
    row = lax.broadcasted_iota(jnp.int32, (8, 128), 0)
    tail = jnp.zeros((8, 128), F32)
    for d, piece in enumerate((y0, y1, y2, y3)):
        at = lax.rem(y + 4 - d, 4)
        v = piece[...]
        power = lane_top(v)
        m_ref[pl.ds(9 * at, 9)] = encode(v, power).reshape(9, 8, 128)
        tail = jnp.where(row == at, power, tail)
    m_ref[36] = tail.astype(BF)


def final_kernel(a0, a1, a2, a3, b0, b1, b2, b3, out_ref):
    _, _, _, x, _, lo = place_of()
    for h, blocks in enumerate(((a0, a1, a2, a3), (b0, b1, b2, b3))):
        for d, block in enumerate(blocks):
            for k in range(4):
                if h == 0:
                    u = 32 * lax.rem(x + 4 - d, 4) + 8 * lax.rem(lo + 4 - k, 4)
                else:
                    u = 32 * lax.rem(lo + 4 - d, 4) + 8 * lax.rem(x + 4 - k, 4)
                rows = pl.ds(pl.multiple_of(u, 8), 8)
                powers = block[k, 36].astype(F32)
                for yy in range(4):
                    lanes = slice(yy * 256 + h * 128, yy * 256 + h * 128 + 128)
                    values = decode(
                        block[k, 9 * yy : 9 * yy + 9], powers[yy : yy + 1].reshape(1, 1, 128)
                    )
                    out_ref[:, rows, lanes] = values


def body(features, kernel, embedding, labels):
    t = lax.axis_index("tensor")
    y, c = t // 2, lax.rem(t, 2)
    first = c == 0

    def by_core(zero, one):
        return jnp.where(first, zero, one)

    def y_all(v):
        got = {d: y_send(v, d) for d in ORDER}
        return [v, got[1], got[2], got[3]]

    def x_all(values):
        got = {d: x_send(values[d - 1], d) for d in ORDER}
        return [got[d] for d in (1, 2, 3)]

    def y_all_of(values):
        got = {d: y_send(values[d - 1], d) for d in ORDER}
        return [got[d] for d in (1, 2, 3)]

    def mine_at(pieces, at, y):
        where = lax.rem(y + 4 - at, 4)
        return jnp.where(
            where == 0,
            pieces[0],
            jnp.where(where == 1, pieces[1], jnp.where(where == 2, pieces[2], pieces[3])),
        )

    def other_at(pieces, at, y):
        return mine_at([pieces[d] for d in range(4)], at, y)

    def z_all(values):
        got = {d: z_send(values[d - 1], Z_STEP[d]) for d in ORDER}
        return [got[d] for d in (1, 2, 3)]

    own = features.reshape(2 * COLS, CHANS)
    kern = kernel.reshape(9, 128, CHANS)
    slices = call(
        pack_kernel,
        [out((9, 128, 256), BF)] * 3,
        [pltpu.SemaphoreType.DMA((3,))],
        kern,
        far=range(1),
        far_out=range(3),
    )
    e_own = jnp.broadcast_to(lax.dynamic_slice_in_dim(embedding, labels[0], 1, 0), (8, 128))
    e_other = core_swap(e_own)
    e = by_core(
        jnp.concatenate([e_own, e_other], 1), jnp.concatenate([e_other, e_own], 1)
    )
    mine = y_all(own)
    kother = core_swap(kern)
    *mine, e, kother = lax.optimization_barrier((*mine, e, kother))
    other = core_swap(jnp.stack(mine))
    *slices, other = lax.optimization_barrier((*slices, other))
    cols = y_all_of(slices)
    first_rows = jnp.concatenate([mine_at(mine, 0, y), other_at(other, 0, y)[:COLS]], 0)
    last_rows = jnp.concatenate([other_at(other, 3, y)[COLS:], mine_at(mine, 3, y)], 0)
    halo_pairs = []
    for q in range(7):
        for k in range(4):
            halo_pairs.append((q * 8 + 2 * k + 1, (q + 1) * 8 + 2 * k))
            halo_pairs.append(((q + 1) * 8 + 2 * k, q * 8 + 2 * k + 1))
    halo = lax.ppermute(by_core(first_rows, last_rows), ("space", "tensor"), halo_pairs)
    *cols, halo = lax.optimization_barrier((*cols, halo))
    cols_other = [core_swap(v) for v in cols]

    gh, hidden, stat, part, x_rows, w = call(
        hidden_kernel,
        [
            out((640, 256), BF),
            out((8, COLS, 256), F32),
            out((8, 256), F32),
            out((8, 128), F32),
            out((18 * COLS, CHANS), BF),
            out((9, CHANS, 256), BF),
        ],
        [
            pltpu.VMEM((22 * COLS, CHANS), BF),
            pltpu.VMEM((9, CHANS, 256), BF),
            pltpu.VMEM((3, 10, COLS, 256), F32),
            pltpu.SemaphoreType.DMA((19,)),
        ],
        *mine, other, halo, kern, kother, *cols, *cols_other, e,
        flops=2 * 640 * 9 * 1024 * 256,
        far=range(14),
        far_out=(4, 5),
    )

    p1, p3 = y_send(gh, 1), y_send(gh, 3)
    part = part + lax.ppermute(part, "space", HI_SWAP)
    part, late = lax.optimization_barrier((part, gh[0:320]))
    p2a = y_send(late, 2)
    part = part + x_send(part, 1) + x_send(part, 2) + x_send(part, 3)
    part, late = lax.optimization_barrier((part, gh[320:640]))
    p2b = y_send(late, 2)
    rows = [
        by_core(gh[576:640], gh[0:64]),
        by_core(p1[576:640], p1[0:64]),
        by_core(p2b[256:320], p2a[0:64]),
        by_core(p3[576:640], p3[0:64]),
        by_core(gh[128:640], gh[0:512]),
    ]
    gh_other = core_swap(jnp.concatenate(rows, 0))
    (gi,) = call(
        input_kernel,
        [out((592, 256), BF)],
        [pltpu.VMEM((11, COLS, CHANS), BF), pltpu.VMEM((3, 9, COLS, 256), F32)],
        gh, p1, p2a, p2b, p3, gh_other, kern, kother, part,
        flops=2 * 576 * 9 * 1024 * 256,
    )

    gi_pieces = y_all(gi)
    edge = by_core(x_rows[0:COLS], x_rows[17 * COLS :]).reshape(COLS, 4, 2, 128)
    give_edge = by_core(edge[:, :, 1], edge[:, :, 0]).reshape(COLS, 512)
    rows = []
    for p in gi_pieces:
        low, high = p[0:576, :128], p[0:576, 128:]
        edge = by_core(low[512:576], high[0:64])
        rows.append(jnp.concatenate([by_core(high, low), edge, p[576:592, :128]], 0))
    take = core_swap(jnp.stack(rows))
    x_edge = core_swap(give_edge)
    pre, vec = call(
        second_kernel,
        [out((528, 256), BF), out((8, 256), F32)],
        [pltpu.VMEM((10, COLS, CHANS), BF), pltpu.VMEM((3, 8, COLS, 256), F32)],
        *gi_pieces, take, w, hidden, stat, e,
        flops=2 * 512 * 9 * 1024 * 256,
    )
    pre_other = core_swap(pre)

    def correlate(h):
        own_h, m1, m2, m3, evec = call(
            functools.partial(corr_kernel, h),
            [out((1152, 128), F32)] + [out((1168, 128), BF)] * 3 + [out((8, 128), F32)],
            [
                pltpu.VMEM((18 * COLS, 512), BF),
                pltpu.VMEM((18 * COLS, 512), BF),
                pltpu.VMEM((16, COLS, 128), BF),
                pltpu.VMEM((1024, 384), BF),
                pltpu.VMEM((1024, 384), BF),
                pltpu.VMEM((9, 4, 4, 32, 128), F32),
            ],
            x_rows, x_edge, *gi_pieces, take, gh, gh_other, pre, pre_other, vec,
            flops=2 * 1024 * 9 * 512 * 256,
        )
        return own_h, evec, (m1, m2, m3)

    label = labels.reshape(1, 1)

    def reduced(h, own_h, evec, sent):
        send_first, send_then = ((x_all, z_all), (z_all, x_all))[h]
        got = send_first(sent)
        mine_h, c1, c2, c3, evec = call(
            functools.partial(first_sum_kernel, h),
            [out((288, 128), F32)] + [out((304, 128), BF)] * 3 + [out((8, 128), F32)],
            [pltpu.VMEM((36, 4, 8, 128), F32)],
            own_h, evec, label, *got,
        )
        got = send_then((c1, c2, c3))
        (message,) = call(
            functools.partial(second_sum_kernel, h),
            [out((304, 128), BF)],
            [],
            mine_h, evec, label, *got,
        )
        theirs = z_send(message, 4)
        y0, y1, y2, y3, *egrad = call(
            functools.partial(pair_kernel, h),
            [out((72, 128), F32)] * 4 + [out((1000, 128), F32)] * (1 - h),
            [pltpu.VMEM((9, 4, 8, 128), F32)],
            message, theirs,
        )
        sent = {1: y1, 2: y2, 3: y3}
        got = {d: y_send(sent[d], d) for d in ORDER}
        (code,) = call(code_kernel, [out((37, 8, 128), BF)], [], y0, got[1], got[2], got[3])
        code = jnp.stack([code] + send_then([code] * 3))
        return [code] + send_first([code] * 3), egrad

    first_half = correlate(0)
    second_half = correlate(1)
    codes_a, egrad = reduced(0, *first_half)
    codes_b, _ = reduced(1, *second_half)
    (wtotal,) = call(
        final_kernel,
        [out((9, 128, CHANS), F32)],
        [],
        *codes_a, *codes_b,
    )
    return (wtotal.reshape(3, 3, 128, CHANS), egrad[0])


def solution(mesh):
    placed = (
        P("dp", ("space", "tensor"), None, None),
        P(None, None, "tensor", None),
        P(None, "tensor"),
        P("dp"),
    )
    return jax.shard_map(
        body,
        mesh=mesh,
        in_specs=placed,
        out_specs=(P(None, None, "tensor", None), P(None, "tensor")),
        check_vma=False,
    )
```

```python
import functools
import math

import jax
import jax.numpy as jnp
from jax import lax
from jax.experimental import pallas as pl
from jax.experimental.pallas import tpu as pltpu
from jax.sharding import PartitionSpec as P

r1_factor = 1000.0
BF = jnp.bfloat16
F32 = jnp.float32

IMAGES, HEIGHT, COLS, CHANS = 4, 128, 64, 1024
SCALE = 1.0 / math.sqrt(HEIGHT * COLS * CHANS)
GWEIGHT = r1_factor / IMAGES

CORE_SWAP = [(t, t ^ 1) for t in range(8)]
HI_SWAP = [(s, s ^ 1) for s in range(8)]
X_PAIRS = [(s, s ^ 2) for s in range(8)]
X_FAR = [(s, s ^ 4) for s in range(8)]
ORDER = (2, 1, 3)
Z_STEP = {1: 1, 2: 2, 3: 7}


def y_perm(d):
    return [(2 * y + c, 2 * ((y + d) % 4) + c) for y in range(4) for c in range(2)]


def x_perm(d):
    return [(2 * x + h, 2 * ((x + d) % 4) + h) for x in range(4) for h in range(2)]


def z_perm(d):
    pairs = []
    for z in range(8):
        w = (z + d) % 8
        for x in range(4):
            pairs.append(((z % 4) * 8 + 2 * x + z // 4, (w % 4) * 8 + 2 * x + w // 4))
    return pairs


def core_swap(v):
    return lax.ppermute(v, "tensor", CORE_SWAP)


def y_send(v, d):
    return lax.ppermute(v, "tensor", y_perm(d))


def x_send(v, d):
    return lax.ppermute(v, "space", x_perm(d))


def z_send(v, d):
    return lax.ppermute(v, ("dp", "space"), z_perm(d))


def place_of():
    t = lax.axis_index("tensor")
    s = lax.axis_index("space")
    lo = lax.axis_index("dp")
    return t // 2, lax.rem(t, 2), s, s // 2, 4 * lax.rem(s, 2) + lo, lo


def call(kernel, outs, scratch, *args, flops=0, far=(), far_out=()):
    vm = pl.BlockSpec(memory_space=pltpu.VMEM)
    anywhere = pl.BlockSpec(memory_space=pl.ANY)
    total = sum(math.prod(a.shape) * a.dtype.itemsize for a in args)
    total += sum(math.prod(o.shape) * o.dtype.itemsize for o in outs)
    return pl.pallas_call(
        kernel,
        out_shape=tuple(outs),
        in_specs=[anywhere if k in far else vm for k in range(len(args))],
        out_specs=tuple(anywhere if k in far_out else vm for k in range(len(outs))),
        scratch_shapes=scratch,
        compiler_params=pltpu.CompilerParams(vmem_limit_bytes=48 << 20),
        cost_estimate=pl.CostEstimate(flops=flops, bytes_accessed=total, transcendentals=0),
    )(*args)


def out(shape, dtype):
    return jax.ShapeDtypeStruct(shape, dtype)


def conv_rows(acc, source, rows, weight, contract):
    flat = source.reshape(-1, CHANS)
    for b in range(3):
        total = None
        for a in range(3):
            part = lax.dot_general(
                flat[a * COLS : (a + rows) * COLS],
                weight(a, b),
                (((1,), (contract,)), ((), ())),
                preferred_element_type=F32,
            )
            total = part if total is None else total + part
        acc[b] = total.reshape(rows, COLS, 256)
    edge = jnp.zeros((rows, 1, 256), F32)
    left, right = acc[0], acc[2]
    return (
        acc[1]
        + jnp.concatenate([edge, left[:, : COLS - 1]], 1)
        + jnp.concatenate([right[:, 1:], edge], 1)
    )


def inside_rows(start, rows):
    row = start + lax.broadcasted_iota(jnp.int32, (rows, COLS, 256), 0)
    return (row >= 0) & (row < HEIGHT)


def split_rows(row):
    hi = row.astype(BF).astype(F32)
    mid = (row - hi).astype(BF).astype(F32)
    return [hi, mid, row - hi - mid]


def rows_block(rows, height, width):
    at = lax.broadcasted_iota(jnp.int32, (height, width), 0)
    block = jnp.zeros((height, width), F32)
    for k, row in enumerate(rows):
        block = jnp.where(at == k, row, block)
    return block.astype(BF)


def pack_kernel(kern, own, m1, m2, m3, sems):
    y, _, _, x, _, _ = place_of()
    jobs = []

    def copy(source, target):
        job = pltpu.make_async_copy(source, target, sems.at[len(jobs)])
        job.start()
        jobs.append(job)

    for d, m in ((2, m2), (1, m1), (3, m3)):
        columns = pl.ds(pl.multiple_of(lax.rem(y + d, 4) * 256, 256), 256)
        if d == 2:
            quarter = pl.ds(pl.multiple_of(32 * x, 32), 32)
            for tap in range(9):
                copy(kern.at[tap, quarter, columns], m.at[tap * 32 : tap * 32 + 32])
            for k in range(4):
                copy(own.at[:, k * 256 : (k + 1) * 256], m.at[288 + 128 * k : 416 + 128 * k])
        else:
            copy(kern.at[:, :, columns], m.at[0:9])
            for k in range(4):
                copy(own.at[:, k * 256 : (k + 1) * 256], m.at[9 + k])
    for job in jobs:
        job.wait()


def hidden_kernel(*refs):
    own, own_other, kern, kother = refs[0:4]
    near, near_other = refs[4:6], refs[6:8]
    far, far_other, quarters = refs[8], refs[9], refs[10:14]
    halo, r1, r2, r3, crossed, e_ref = refs[14:20]
    gh_ref, hid_ref, stat_ref, part_ref, x_out, w_out = refs[20:26]
    x_ref, w_ref, acc, sems = refs[26:30]
    y, c, s, x, _, _ = place_of()
    columns = pl.ds(pl.multiple_of(y * 256, 256), 256)
    copies = []

    def copy(source, target):
        job = pltpu.make_async_copy(source, target, sems.at[len(copies)])
        job.start()
        copies.append(job)

    for core, whole, weights, pieces in ((c, own, kern, near), (1 - c, own_other, kother, near_other)):
        for d in range(4):
            at = lax.rem(y + 4 - d, 4)
            rows = pl.ds(pl.multiple_of((3 + 4 * at + 2 * core) * COLS, COLS), 2 * COLS)
            base = (2 * at + core) * 128
            block = pl.ds(pl.multiple_of(base, 128), 128)
            if d == 0:
                copy(whole, x_ref.at[rows, :])
                copy(weights.at[:, :, columns], w_ref.at[:, block, :])
            elif d != 2:
                piece = pieces[d // 2]
                copy(piece.at[0:9], w_ref.at[:, block, :])
                for k in range(4):
                    copy(piece.at[9 + k], x_ref.at[rows, k * 256 : (k + 1) * 256])
            else:
                mine = pieces is near
                for q in range(4):
                    share = pl.ds(pl.multiple_of(base + 32 * lax.rem(x + 4 - q, 4), 32), 32)
                    source = quarters[q] if mine else far_other.at[9 * q : 9 * q + 9]
                    copy(source, w_ref.at[:, share, :])
                for k in range(4):
                    if mine:
                        source = far.at[288 + 128 * k : 416 + 128 * k]
                        copy(source, x_ref.at[rows, k * 256 : (k + 1) * 256])
                    else:
                        for b in range(4):
                            part = pl.ds(
                                pl.multiple_of((3 + 4 * at + 2 * core) * COLS + 32 * b, 32), 32
                            )
                            copy(
                                far_other.at[36 + 4 * k + b],
                                x_ref.at[part, k * 256 : (k + 1) * 256],
                            )
    def row(k, count=1):
        return slice(k * COLS, (k + count) * COLS)

    for source, up, down in ((halo, 3, 0), (r1, 0, 1), (r2, 1, 2), (r3, 2, 3)):

        @pl.when((y == up) & (c == 0))
        def _():
            x_ref[row(0)] = source[row(1)]

        @pl.when((y == up) & (c == 1))
        def _():
            x_ref[row(2)] = source[row(1)]

        @pl.when((y == down) & (c == 0))
        def _():
            x_ref[row(19)] = source[row(0)]

        @pl.when((y == down) & (c == 1))
        def _():
            x_ref[row(21)] = source[row(0)]

    @pl.when(c == 0)
    def _():
        x_ref[row(1, 2)] = crossed[...]

    @pl.when(c == 1)
    def _():
        x_ref[row(19, 2)] = crossed[...]

    for job in copies:
        job.wait()
    jobs = [
        pltpu.make_async_copy(x_ref.at[2 * COLS : 20 * COLS], x_out, sems.at[len(copies)]),
        pltpu.make_async_copy(w_ref, w_out, sems.at[len(copies) + 1]),
    ]
    for job in jobs:
        job.start()
    hidden = conv_rows(acc, x_ref[pl.ds(pl.multiple_of(640 * c, 128), 768)], 10, lambda a, b: w_ref[3 * a + b], 0)
    acc[0] = hidden
    sig = jax.nn.sigmoid(hidden)
    slope = sig * (1.0 + hidden * (1.0 - sig))
    e = e_ref[0:1, :].reshape(1, 1, 256)
    gh = jnp.where(inside_rows(16 * s - 2 + 10 * c, 10), e * slope * SCALE, 0.0)
    gh_ref[...] = gh.astype(BF).reshape(640, 256)
    own = acc[0, pl.ds(2 - 2 * c, 8)]
    hid_ref[...] = own
    act = own * jax.nn.sigmoid(own)
    act_sum = jnp.sum(jnp.sum(act, axis=0), axis=0, keepdims=True)
    part = SCALE * jnp.sum(act_sum * e_ref[0:1, :])
    stat_ref[...] = jnp.broadcast_to(act_sum, (8, 256))
    part_ref[...] = jnp.full((8, 128), part, F32)
    for job in jobs:
        job.wait()


def sum_rows(tail):
    t = tail.astype(F32)
    return t[0:1] + t[1:2] + t[2:3]


def input_kernel(p0, p1, p2a, p2b, p3, swapped, kern, kother, part, gi_ref, full, acc):
    y, c, s, _, _, _ = place_of()
    for d in range(4):
        at = pl.multiple_of(lax.rem(y + 4 - d, 4) * 256, 256)
        if d == 2:
            full[pl.ds(c, 5), :, pl.ds(at, 256)] = p2a[...].reshape(5, COLS, 256)
            full[pl.ds(c + 5, 5), :, pl.ds(at, 256)] = p2b[...].reshape(5, COLS, 256)
        else:
            full[pl.ds(c, 10), :, pl.ds(at, 256)] = (p0, p1, p2a, p3)[d][...].reshape(10, COLS, 256)
        full[pl.ds(10 * (1 - c), 1), :, pl.ds(at, 256)] = swapped[d * 64 : d * 64 + 64].reshape(
            1, COLS, 256
        )

    def weight(a, b):
        tap = 3 * (2 - a) + 2 - b
        return jnp.concatenate([kern[tap], kother[tap]], 0)

    grad = conv_rows(acc, full[...], 9, weight, 1)
    turned = jnp.concatenate([grad[:, :, 128:], grad[:, :, :128]], 2)
    grad = jnp.where(c == 0, grad, turned)
    grad = jnp.where(inside_rows(16 * s - 1 + 9 * c, 9), grad, 0.0)
    gi_ref[0:576] = grad.astype(BF).reshape(576, 256)
    row = jnp.concatenate([part[0:1], part[0:1]], 1)
    gi_ref[576:592] = rows_block(split_rows(row), 16, 256)


def second_kernel(
    p0, p1, p2, p3, swapped, w_ref, hid_ref, stat_ref, e_ref, pre_ref, vec_ref, full, acc
):
    y, c, _, _, _, _ = place_of()
    score = jnp.zeros((1, 128), F32)
    for d, piece in enumerate((p0, p1, p2, p3)):
        score = score + sum_rows(piece[576:592])[:, :128] + sum_rows(swapped[d, 640:656])
        at = pl.multiple_of(lax.rem(y + 4 - d, 4) * 256, 256)
        near = pl.multiple_of(at + 128 * c, 128)
        away = pl.multiple_of(at + 128 * (1 - c), 128)
        full[pl.ds(c, 9), :, pl.ds(at, 256)] = piece[0:576].reshape(9, COLS, 256)
        full[pl.ds(9 * (1 - c), 1), :, pl.ds(near, 128)] = swapped[
            d, pl.ds(pl.multiple_of(8 * COLS * c, COLS), COLS)
        ].reshape(1, COLS, 128)
        full[pl.ds(9 * (1 - c), 1), :, pl.ds(away, 128)] = swapped[d, 576:640].reshape(1, COLS, 128)
    second = conv_rows(acc, full[...], 8, lambda a, b: w_ref[3 * a + b], 0)
    hidden = hid_ref[...]
    sig = jax.nn.sigmoid(hidden)
    slope = sig * (1.0 + hidden * (1.0 - sig))
    curve = sig * (1.0 - sig) * (2.0 + hidden * (1.0 - 2.0 * sig))
    e = e_ref[0:1, :].reshape(1, 1, 256)
    coeff = -jax.nn.sigmoid(-score[0:1, 0:1]) / IMAGES
    c3 = coeff.reshape(1, 1, 1)
    pre = c3 * e * slope * SCALE + GWEIGHT * second * e * curve * SCALE
    pre_ref[0:512] = pre.astype(BF).reshape(512, 256)
    part = jnp.sum(jnp.sum(second * slope, axis=0), axis=0, keepdims=True)
    vec = coeff * SCALE * stat_ref[0:1] + GWEIGHT * SCALE * part
    pre_ref[512:528] = rows_block(split_rows(vec), 16, 256)
    vec_ref[...] = jnp.broadcast_to(vec, (8, 256))


def power_of(top):
    power = 7.0 - jnp.ceil(jnp.log2(jnp.maximum(top, 1e-30)) + 0.01)
    return jnp.clip(power, -100.0, 100.0)


def encode(v, power):
    u = v * jnp.exp2(power)
    q = u * u
    q = q * q
    q = q * q
    q = q * q
    return jnp.where(u < 0, -q, q).astype(BF)


def decode(code, power):
    f = code.astype(F32)
    mag = jnp.exp2(jnp.log2(jnp.abs(f)) * (1.0 / 16.0) - power)
    return jnp.where(f < 0, -mag, mag)


def shifted(v, target):
    edge = jnp.zeros((16, 1, 128), F32)
    f = v.astype(F32)
    target[:, 0:128] = jnp.concatenate([f[:, 1:], edge], 1).astype(BF).reshape(1024, 128)
    target[:, 128:256] = v.reshape(1024, 128)
    target[:, 256:384] = jnp.concatenate([edge, f[:, : COLS - 1]], 1).astype(BF).reshape(1024, 128)


def lane_top(v):
    return power_of(jnp.max(jnp.abs(v), axis=0, keepdims=True))


def corr_kernel(
    h, x_ref, p0, p1, p2, p3, take, gh, gho, pre, preo, vec,
    own, m1, m2, m3, evec_ref, xh, gih, both, g_gh, g_pre, wsum,
):
    y, c, _, x, _, lo = place_of()
    lanes = slice(128 * h, 128 * h + 128)
    for k in range(4):
        at = pl.multiple_of((2 * k + c) * 128, 128)
        xh[:, k * 128 : (k + 1) * 128] = x_ref[:, pl.ds(at, 128)]
    half = pl.multiple_of(c * 128, 128)
    for d, piece in enumerate((p0, p1, p2, p3)):
        at = pl.multiple_of(lax.rem(y + 4 - d, 4) * 128, 128)
        here = pl.ds(pl.multiple_of(576 * c, 64), 576)
        there = pl.ds(pl.multiple_of(576 * (1 - c), 64), 576)
        gih[here, pl.ds(at, 128)] = piece[0:576, pl.ds(half, 128)]
        gih[there, pl.ds(at, 128)] = take[d, 0:576]
    own_rows = pl.ds(pl.multiple_of(128 - 128 * c, 128), 512)
    both[pl.ds(8 * c, 8)] = gh[own_rows, lanes].reshape(8, COLS, 128)
    both[pl.ds(8 * (1 - c), 8)] = gho[256:768, lanes].reshape(8, COLS, 128)
    shifted(both[...], g_gh)
    both[pl.ds(8 * c, 8)] = pre[0:512, lanes].reshape(8, COLS, 128)
    both[pl.ds(8 * (1 - c), 8)] = preo[0:512, lanes].reshape(8, COLS, 128)
    shifted(both[...], g_pre)
    for a in range(3):
        adv = lax.dot_general(
            xh[a * COLS : a * COLS + 1024], g_pre[...], (((0,), (0,)), ((), ())),
            preferred_element_type=F32,
        )
        direct = lax.dot_general(
            gih[a * COLS : a * COLS + 1024], g_gh[...], (((0,), (0,)), ((), ())),
            preferred_element_type=F32,
        )
        total = adv + GWEIGHT * direct
        for b in range(3):
            wsum[3 * a + b] = total[:, b * 128 : b * 128 + 128].reshape(4, 4, 32, 128)
    evec = vec[0:1, pl.ds(half, 128)] + sum_rows(preo[512:528, pl.ds(half, 128)])
    evec_ref[...] = jnp.broadcast_to(evec, (8, 128))
    extra = split_rows(evec)
    at = (x, lo)[h]
    own[...] = wsum[:, :, pl.ds(at, 1)].reshape(1152, 128)
    for d, m in enumerate((m1, m2, m3), 1):
        part = wsum[:, :, pl.ds(lax.rem(at + d, 4), 1)].reshape(1152, 128)
        power = lane_top(part)
        m[0:1152] = encode(part, power)
        m[1152:1168] = rows_block([power] + extra, 16, 128)


def added(own, messages, size):
    t = own[...]
    for m in messages:
        t = t + decode(m[0:size], m[size : size + 16][0:1].astype(F32))
    return t


def label_rows(label):
    tag = jnp.broadcast_to(label[...], (1, 128)).astype(F32)
    high = jnp.floor(tag * (1.0 / 32.0))
    return [high, tag - 32.0 * high]


def first_sum_kernel(h, own, evec_in, label, m1, m2, m3, mine, c1, c2, c3, evec_ref, total):
    _, _, _, x, _, lo = place_of()
    evec = evec_in[0:1]
    for m in (m1, m2, m3):
        evec = evec + sum_rows(m[1152:1168][1:4])
    evec_ref[...] = jnp.broadcast_to(evec, (8, 128))
    extra = split_rows(evec) + label_rows(label)
    at = (lo, x)[h]
    total[...] = added(own, (m1, m2, m3), 1152).reshape(36, 4, 8, 128)
    mine[...] = total[:, pl.ds(at, 1)].reshape(288, 128)
    for d, m in enumerate((c1, c2, c3), 1):
        part = total[:, pl.ds(lax.rem(at + d, 4), 1)].reshape(288, 128)
        power = lane_top(part)
        m[0:288] = encode(part, power)
        m[288:304] = rows_block([power] + extra, 16, 128)


def second_sum_kernel(h, own, evec_in, label, m1, m2, m3, m_ref):
    _, _, _, _, _, lo = place_of()
    t = added(own, (m1, m2, m3), 288)
    power = lane_top(t)
    m_ref[0:288] = encode(t, power)
    rows = [power]
    if h == 0:
        lane = lax.broadcasted_iota(jnp.int32, (1, 128), 1)
        found = [(lo, split_rows(evec_in[0:1]) + label_rows(label))]
        for d, m in enumerate((m1, m2, m3), 1):
            t = m[288:304].astype(F32)
            found.append((lax.rem(lo + 4 - d, 4), [t[k : k + 1] for k in range(1, 6)]))
        zero = jnp.zeros((1, 128), F32)
        for slot in range(4):
            for k in range(3):
                row = zero
                for at, parts in found:
                    row = jnp.where(at == slot, parts[k], row)
                rows.append(row)
        for k in (3, 4):
            row = zero
            for at, parts in found:
                row = jnp.where(lane == at, parts[k], row)
            rows.append(row)
    m_ref[288:304] = rows_block(rows, 16, 128)


def pair_kernel(h, mine, theirs, y0, y1, y2, y3, *rest):
    y, _, _, _, _, _ = place_of()
    total = rest[-1]
    t1 = mine[288:304].astype(F32)
    t2 = theirs[288:304].astype(F32)
    value = decode(mine[0:288], t1[0:1]) + decode(theirs[0:288], t2[0:1])
    total[...] = value.reshape(9, 4, 8, 128)
    for d, target in enumerate((y0, y1, y2, y3)):
        target[...] = total[:, pl.ds(lax.rem(y + d, 4), 1)].reshape(72, 128)
    if h == 0:
        row = lax.broadcasted_iota(jnp.int32, (1000, 128), 0)
        egrad = jnp.zeros((1000, 128), F32)
        for slot in range(4):
            at = 1 + 3 * slot
            vec = sum_rows(t1[at : at + 3]) + sum_rows(t2[at : at + 3])
            tag = 32.0 * t1[13:14, slot : slot + 1] + t1[14:15, slot : slot + 1]
            egrad = egrad + jnp.where(row == tag.astype(jnp.int32), vec, 0.0)
        rest[0][...] = egrad


def code_kernel(y0, y1, y2, y3, m_ref):
    y, _, _, _, _, _ = place_of()
    row = lax.broadcasted_iota(jnp.int32, (8, 128), 0)
    tail = jnp.zeros((8, 128), F32)
    for d, piece in enumerate((y0, y1, y2, y3)):
        at = lax.rem(y + 4 - d, 4)
        v = piece[...]
        power = lane_top(v)
        m_ref[pl.ds(9 * at, 9)] = encode(v, power).reshape(9, 8, 128)
        tail = jnp.where(row == at, power, tail)
    m_ref[36] = tail.astype(BF)


def final_kernel(a0, a1, a2, a3, b0, b1, b2, b3, out_ref):
    _, _, _, x, _, lo = place_of()
    for h, blocks in enumerate(((a0, a1, a2, a3), (b0, b1, b2, b3))):
        for d, block in enumerate(blocks):
            for k in range(4):
                if h == 0:
                    u = 32 * lax.rem(x + 4 - d, 4) + 8 * lax.rem(lo + 4 - k, 4)
                else:
                    u = 32 * lax.rem(lo + 4 - d, 4) + 8 * lax.rem(x + 4 - k, 4)
                rows = pl.ds(pl.multiple_of(u, 8), 8)
                powers = block[k, 36].astype(F32)
                for yy in range(4):
                    lanes = slice(yy * 256 + h * 128, yy * 256 + h * 128 + 128)
                    values = decode(
                        block[k, 9 * yy : 9 * yy + 9], powers[yy : yy + 1].reshape(1, 1, 128)
                    )
                    out_ref[:, rows, lanes] = values


def body(features, kernel, embedding, labels):
    t = lax.axis_index("tensor")
    y, c = t // 2, lax.rem(t, 2)
    first = c == 0

    def by_core(zero, one):
        return jnp.where(first, zero, one)

    def y_all(v):
        got = {d: y_send(v, d) for d in ORDER}
        return [v, got[1], got[2], got[3]]

    def x_all(values):
        got = {d: x_send(values[d - 1], d) for d in ORDER}
        return [got[d] for d in (1, 2, 3)]

    def z_all(values):
        got = {d: z_send(values[d - 1], Z_STEP[d]) for d in ORDER}
        return [got[d] for d in (1, 2, 3)]

    own = features.reshape(2 * COLS, CHANS)
    kern = kernel.reshape(9, 128, CHANS)
    halo_pairs = []
    for q in range(7):
        for k in range(2):
            halo_pairs.append((q * 8 + 6 + k, (q + 1) * 8 + 6 + k))
            halo_pairs.append(((q + 1) * 8 + k, q * 8 + k))

    def halo_pairs_y(d):
        return [(6 + k, 2 * ((3 + d) % 4) + k) for k in range(2)] + [
            (k, 2 * d + k) for k in range(2)
        ]

    halo = lax.ppermute(own, ("space", "tensor"), halo_pairs)
    m1, m2, m3 = call(
        pack_kernel,
        [out((13, 128, 256), BF), out((800, 256), BF), out((13, 128, 256), BF)],
        [pltpu.SemaphoreType.DMA((23,))],
        kern, own,
        far=range(2),
        far_out=range(3),
    )
    far = y_send(m2, 2)
    near = [y_send(m1, 1), y_send(m3, 3)]
    e_own = jnp.broadcast_to(lax.dynamic_slice_in_dim(embedding, labels[0], 1, 0), (8, 128))
    e_other = core_swap(e_own)
    e = by_core(
        jnp.concatenate([e_own, e_other], 1), jnp.concatenate([e_other, e_own], 1)
    )
    own_other, kother = core_swap(own), core_swap(kern)
    far, halo, e, own_other, kother = lax.optimization_barrier((far, halo, e, own_other, kother))
    quarter = far[0:288].reshape(9, 32, 256)
    quarters = [quarter] + x_all([quarter] * 3)
    *quarters, halo = lax.optimization_barrier((*quarters, halo))
    r1, r2, r3 = (lax.ppermute(halo, "tensor", halo_pairs_y(d)) for d in (1, 2, 3))
    r1, r2, r3, *near = lax.optimization_barrier((r1, r2, r3, *near))
    top = jnp.where(y == 0, r1, jnp.where(y == 1, r2, jnp.where(y == 2, r3, halo)))
    bottom = jnp.where(y == 0, halo, jnp.where(y == 1, r1, jnp.where(y == 2, r2, r3)))
    crossed = core_swap(by_core(bottom, top))
    near_other = [core_swap(v) for v in near]
    far_other = core_swap(
        jnp.concatenate([*quarters, far[288:800].reshape(16, 32, 256)], 0)
    )

    gh, hidden, stat, part, x_rows, w = call(
        hidden_kernel,
        [
            out((640, 256), BF),
            out((8, COLS, 256), F32),
            out((8, 256), F32),
            out((8, 128), F32),
            out((18 * COLS, CHANS), BF),
            out((9, CHANS, 256), BF),
        ],
        [
            pltpu.VMEM((22 * COLS, CHANS), BF),
            pltpu.VMEM((9, CHANS, 256), BF),
            pltpu.VMEM((3, 10, COLS, 256), F32),
            pltpu.SemaphoreType.DMA((60,)),
        ],
        own, own_other, kern, kother, *near, *near_other, far, far_other, *quarters,
        halo, r1, r2, r3, crossed, e,
        flops=2 * 640 * 9 * 1024 * 256,
        far=range(14),
        far_out=(4, 5),
    )

    p1, p3 = y_send(gh, 1), y_send(gh, 3)
    part = part + x_send(part, 1) + x_send(part, 2) + x_send(part, 3)
    part, late = lax.optimization_barrier((part, gh[0:320]))
    p2a = y_send(late, 2)
    part = part + lax.ppermute(part, "space", HI_SWAP)
    part, late = lax.optimization_barrier((part, gh[320:640]))
    p2b = y_send(late, 2)
    rows = [
        by_core(gh[576:640], gh[0:64]),
        by_core(p1[576:640], p1[0:64]),
        by_core(p2b[256:320], p2a[0:64]),
        by_core(p3[576:640], p3[0:64]),
        by_core(gh[128:640], gh[0:512]),
    ]
    gh_other = core_swap(jnp.concatenate(rows, 0))
    (gi,) = call(
        input_kernel,
        [out((592, 256), BF)],
        [pltpu.VMEM((11, COLS, CHANS), BF), pltpu.VMEM((3, 9, COLS, 256), F32)],
        gh, p1, p2a, p2b, p3, gh_other, kern, kother, part,
        flops=2 * 576 * 9 * 1024 * 256,
    )

    gi_pieces = y_all(gi)
    rows = []
    for p in gi_pieces:
        low, high = p[0:576, :128], p[0:576, 128:]
        edge = by_core(low[512:576], high[0:64])
        rows.append(jnp.concatenate([by_core(high, low), edge, p[576:592, :128]], 0))
    take = core_swap(jnp.stack(rows))
    pre, vec = call(
        second_kernel,
        [out((528, 256), BF), out((8, 256), F32)],
        [pltpu.VMEM((10, COLS, CHANS), BF), pltpu.VMEM((3, 8, COLS, 256), F32)],
        *gi_pieces, take, w, hidden, stat, e,
        flops=2 * 512 * 9 * 1024 * 256,
    )
    pre_other = core_swap(pre)

    def correlate(h):
        own_h, m1, m2, m3, evec = call(
            functools.partial(corr_kernel, h),
            [out((1152, 128), F32)] + [out((1168, 128), BF)] * 3 + [out((8, 128), F32)],
            [
                pltpu.VMEM((18 * COLS, 512), BF),
                pltpu.VMEM((18 * COLS, 512), BF),
                pltpu.VMEM((16, COLS, 128), BF),
                pltpu.VMEM((1024, 384), BF),
                pltpu.VMEM((1024, 384), BF),
                pltpu.VMEM((9, 4, 4, 32, 128), F32),
            ],
            x_rows, *gi_pieces, take, gh, gh_other, pre, pre_other, vec,
            flops=2 * 1024 * 9 * 512 * 256,
        )
        return own_h, evec, (m1, m2, m3)

    label = labels.reshape(1, 1)

    def reduced(h, own_h, evec, sent):
        send_first, send_then = ((x_all, z_all), (z_all, x_all))[h]
        got = send_first(sent)
        mine_h, c1, c2, c3, evec = call(
            functools.partial(first_sum_kernel, h),
            [out((288, 128), F32)] + [out((304, 128), BF)] * 3 + [out((8, 128), F32)],
            [pltpu.VMEM((36, 4, 8, 128), F32)],
            own_h, evec, label, *got,
        )
        got = send_then((c1, c2, c3))
        (message,) = call(
            functools.partial(second_sum_kernel, h),
            [out((304, 128), BF)],
            [],
            mine_h, evec, label, *got,
        )
        theirs = z_send(message, 4)
        y0, y1, y2, y3, *egrad = call(
            functools.partial(pair_kernel, h),
            [out((72, 128), F32)] * 4 + [out((1000, 128), F32)] * (1 - h),
            [pltpu.VMEM((9, 4, 8, 128), F32)],
            message, theirs,
        )
        sent = {1: y1, 2: y2, 3: y3}
        got = {d: y_send(sent[d], d) for d in ORDER}
        (code,) = call(code_kernel, [out((37, 8, 128), BF)], [], y0, got[1], got[2], got[3])
        code = jnp.stack([code] + send_then([code] * 3))
        return [code] + send_first([code] * 3), egrad

    first_half = correlate(0)
    second_half = correlate(1)
    codes_a, egrad = reduced(0, *first_half)
    codes_b, _ = reduced(1, *second_half)
    (wtotal,) = call(
        final_kernel,
        [out((9, 128, CHANS), F32)],
        [],
        *codes_a, *codes_b,
    )
    return (wtotal.reshape(3, 3, 128, CHANS), egrad[0])


def solution(mesh):
    placed = (
        P("dp", ("space", "tensor"), None, None),
        P(None, None, "tensor", None),
        P(None, "tensor"),
        P("dp"),
    )
    return jax.shard_map(
        body,
        mesh=mesh,
        in_specs=placed,
        out_specs=(P(None, None, "tensor", None), P(None, "tensor")),
        check_vma=False,
    )
```

```python
import functools
import math

import jax
import jax.numpy as jnp
from jax import lax
from jax.experimental import pallas as pl
from jax.experimental.pallas import tpu as pltpu
from jax.sharding import PartitionSpec as P

r1_factor = 1000.0
BF = jnp.bfloat16
F32 = jnp.float32

IMAGES, HEIGHT, COLS, CHANS = 4, 128, 64, 1024
SCALE = 1.0 / math.sqrt(HEIGHT * COLS * CHANS)
GWEIGHT = r1_factor / IMAGES

CORE_SWAP = [(t, t ^ 1) for t in range(8)]
HI_SWAP = [(s, s ^ 1) for s in range(8)]
X_PAIRS = [(s, s ^ 2) for s in range(8)]
X_FAR = [(s, s ^ 4) for s in range(8)]
ORDER = (2, 1, 3)
Z_STEP = {1: 1, 2: 2, 3: 7}


def y_perm(d):
    return [(2 * y + c, 2 * ((y + d) % 4) + c) for y in range(4) for c in range(2)]


def x_perm(d):
    return [(2 * x + h, 2 * ((x + d) % 4) + h) for x in range(4) for h in range(2)]


def z_perm(d):
    pairs = []
    for z in range(8):
        w = (z + d) % 8
        for x in range(4):
            pairs.append(((z % 4) * 8 + 2 * x + z // 4, (w % 4) * 8 + 2 * x + w // 4))
    return pairs


def core_swap(v):
    return lax.ppermute(v, "tensor", CORE_SWAP)


def y_send(v, d):
    return lax.ppermute(v, "tensor", y_perm(d))


def x_send(v, d):
    return lax.ppermute(v, "space", x_perm(d))


def z_send(v, d):
    return lax.ppermute(v, ("dp", "space"), z_perm(d))


def place_of():
    t = lax.axis_index("tensor")
    s = lax.axis_index("space")
    lo = lax.axis_index("dp")
    return t // 2, lax.rem(t, 2), s, s // 2, 4 * lax.rem(s, 2) + lo, lo


def call(kernel, outs, scratch, *args, flops=0, far=(), far_out=()):
    vm = pl.BlockSpec(memory_space=pltpu.VMEM)
    anywhere = pl.BlockSpec(memory_space=pl.ANY)
    total = sum(math.prod(a.shape) * a.dtype.itemsize for a in args)
    total += sum(math.prod(o.shape) * o.dtype.itemsize for o in outs)
    return pl.pallas_call(
        kernel,
        out_shape=tuple(outs),
        in_specs=[anywhere if k in far else vm for k in range(len(args))],
        out_specs=tuple(anywhere if k in far_out else vm for k in range(len(outs))),
        scratch_shapes=scratch,
        compiler_params=pltpu.CompilerParams(vmem_limit_bytes=48 << 20),
        cost_estimate=pl.CostEstimate(flops=flops, bytes_accessed=total, transcendentals=0),
    )(*args)


def out(shape, dtype):
    return jax.ShapeDtypeStruct(shape, dtype)


def conv_rows(acc, source, rows, weight, contract):
    flat = source.reshape(-1, CHANS)
    for b in range(3):
        total = None
        for a in range(3):
            part = lax.dot_general(
                flat[a * COLS : (a + rows) * COLS],
                weight(a, b),
                (((1,), (contract,)), ((), ())),
                preferred_element_type=F32,
            )
            total = part if total is None else total + part
        acc[b] = total.reshape(rows, COLS, 256)
    edge = jnp.zeros((rows, 1, 256), F32)
    left, right = acc[0], acc[2]
    return (
        acc[1]
        + jnp.concatenate([edge, left[:, : COLS - 1]], 1)
        + jnp.concatenate([right[:, 1:], edge], 1)
    )


def inside_rows(start, rows):
    row = start + lax.broadcasted_iota(jnp.int32, (rows, COLS, 256), 0)
    return (row >= 0) & (row < HEIGHT)


def split_rows(row):
    hi = row.astype(BF).astype(F32)
    mid = (row - hi).astype(BF).astype(F32)
    return [hi, mid, row - hi - mid]


def rows_block(rows, height, width):
    at = lax.broadcasted_iota(jnp.int32, (height, width), 0)
    block = jnp.zeros((height, width), F32)
    for k, row in enumerate(rows):
        block = jnp.where(at == k, row, block)
    return block.astype(BF)


def pack_kernel(kern, m1, m2, m3, sems):
    y, _, _, _, _, _ = place_of()
    jobs = []
    for d, m in enumerate((m1, m2, m3), 1):
        columns = pl.ds(pl.multiple_of(lax.rem(y + d, 4) * 256, 256), 256)
        job = pltpu.make_async_copy(kern.at[:, :, columns], m, sems.at[d - 1])
        job.start()
        jobs.append(job)
    for job in jobs:
        job.wait()


def hidden_kernel(*refs):
    mine, other, (halo, kern, kother) = refs[0:4], refs[4:8], refs[8:11]
    cols, cols_other, e_ref = refs[11:14], refs[14:17], refs[17]
    gh_ref, hid_ref, stat_ref, part_ref, x_out, w_out = refs[18:24]
    x_ref, w_ref, acc, sems = refs[24:28]
    y, c, s, _, _, _ = place_of()
    columns = pl.ds(pl.multiple_of(y * 256, 256), 256)
    copies = []

    def copy(source, target):
        job = pltpu.make_async_copy(source, target, sems.at[len(copies)])
        job.start()
        copies.append(job)

    for d in range(4):
        at = lax.rem(y + 4 - d, 4)
        rows = pl.ds(pl.multiple_of((3 + 4 * at + 2 * c) * COLS, COLS), 2 * COLS)
        copy(mine[d], x_ref.at[rows, :])
        rows = pl.ds(pl.multiple_of((5 + 4 * at - 2 * c) * COLS, COLS), 2 * COLS)
        copy(other[d], x_ref.at[rows, :])
        for core, whole, pieces in ((c, kern, cols), (1 - c, kother, cols_other)):
            block = pl.ds(pl.multiple_of((2 * at + core) * 128, 128), 128)
            source = pieces[d - 1] if d else whole.at[:, :, columns]
            copy(source, w_ref.at[:, block, :])
    copy(halo, x_ref.at[pl.ds(pl.multiple_of(19 * COLS * c, COLS), 3 * COLS), :])
    for job in copies:
        job.wait()
    jobs = [
        pltpu.make_async_copy(x_ref.at[2 * COLS : 20 * COLS], x_out, sems.at[17]),
        pltpu.make_async_copy(w_ref, w_out, sems.at[18]),
    ]
    for job in jobs:
        job.start()
    hidden = conv_rows(acc, x_ref[pl.ds(pl.multiple_of(640 * c, 128), 768)], 10, lambda a, b: w_ref[3 * a + b], 0)
    acc[0] = hidden
    sig = jax.nn.sigmoid(hidden)
    slope = sig * (1.0 + hidden * (1.0 - sig))
    e = e_ref[0:1, :].reshape(1, 1, 256)
    gh = jnp.where(inside_rows(16 * s - 2 + 10 * c, 10), e * slope * SCALE, 0.0)
    gh_ref[...] = gh.astype(BF).reshape(640, 256)
    own = acc[0, pl.ds(2 - 2 * c, 8)]
    hid_ref[...] = own
    act = own * jax.nn.sigmoid(own)
    act_sum = jnp.sum(jnp.sum(act, axis=0), axis=0, keepdims=True)
    part = SCALE * jnp.sum(act_sum * e_ref[0:1, :])
    stat_ref[...] = jnp.broadcast_to(act_sum, (8, 256))
    part_ref[...] = jnp.full((8, 128), part, F32)
    for job in jobs:
        job.wait()


def sum_rows(tail):
    t = tail.astype(F32)
    return t[0:1] + t[1:2] + t[2:3]


def input_kernel(p0, p1, p2a, p2b, p3, swapped, kern, kother, part, gi_ref, full, acc):
    y, c, s, _, _, _ = place_of()
    for d in range(4):
        at = pl.multiple_of(lax.rem(y + 4 - d, 4) * 256, 256)
        if d == 2:
            full[pl.ds(c, 5), :, pl.ds(at, 256)] = p2a[...].reshape(5, COLS, 256)
            full[pl.ds(c + 5, 5), :, pl.ds(at, 256)] = p2b[...].reshape(5, COLS, 256)
        else:
            full[pl.ds(c, 10), :, pl.ds(at, 256)] = (p0, p1, p2a, p3)[d][...].reshape(10, COLS, 256)
        full[pl.ds(10 * (1 - c), 1), :, pl.ds(at, 256)] = swapped[d * 64 : d * 64 + 64].reshape(
            1, COLS, 256
        )

    def weight(a, b):
        tap = 3 * (2 - a) + 2 - b
        return jnp.concatenate([kern[tap], kother[tap]], 0)

    grad = conv_rows(acc, full[...], 9, weight, 1)
    turned = jnp.concatenate([grad[:, :, 128:], grad[:, :, :128]], 2)
    grad = jnp.where(c == 0, grad, turned)
    grad = jnp.where(inside_rows(16 * s - 1 + 9 * c, 9), grad, 0.0)
    gi_ref[0:576] = grad.astype(BF).reshape(576, 256)
    row = jnp.concatenate([part[0:1], part[0:1]], 1)
    gi_ref[576:592] = rows_block(split_rows(row), 16, 256)


def second_kernel(
    p0, p1, p2, p3, swapped, w_ref, hid_ref, stat_ref, e_ref, pre_ref, vec_ref, full, acc
):
    y, c, _, _, _, _ = place_of()
    score = jnp.zeros((1, 128), F32)
    for d, piece in enumerate((p0, p1, p2, p3)):
        score = score + sum_rows(piece[576:592])[:, :128] + sum_rows(swapped[d, 640:656])
        at = pl.multiple_of(lax.rem(y + 4 - d, 4) * 256, 256)
        near = pl.multiple_of(at + 128 * c, 128)
        away = pl.multiple_of(at + 128 * (1 - c), 128)
        full[pl.ds(c, 9), :, pl.ds(at, 256)] = piece[0:576].reshape(9, COLS, 256)
        full[pl.ds(9 * (1 - c), 1), :, pl.ds(near, 128)] = swapped[
            d, pl.ds(pl.multiple_of(8 * COLS * c, COLS), COLS)
        ].reshape(1, COLS, 128)
        full[pl.ds(9 * (1 - c), 1), :, pl.ds(away, 128)] = swapped[d, 576:640].reshape(1, COLS, 128)
    second = conv_rows(acc, full[...], 8, lambda a, b: w_ref[3 * a + b], 0)
    hidden = hid_ref[...]
    sig = jax.nn.sigmoid(hidden)
    slope = sig * (1.0 + hidden * (1.0 - sig))
    curve = sig * (1.0 - sig) * (2.0 + hidden * (1.0 - 2.0 * sig))
    e = e_ref[0:1, :].reshape(1, 1, 256)
    coeff = -jax.nn.sigmoid(-score[0:1, 0:1]) / IMAGES
    c3 = coeff.reshape(1, 1, 1)
    pre = c3 * e * slope * SCALE + GWEIGHT * second * e * curve * SCALE
    pre_ref[0:512] = pre.astype(BF).reshape(512, 256)
    part = jnp.sum(jnp.sum(second * slope, axis=0), axis=0, keepdims=True)
    vec = coeff * SCALE * stat_ref[0:1] + GWEIGHT * SCALE * part
    pre_ref[512:528] = rows_block(split_rows(vec), 16, 256)
    vec_ref[...] = jnp.broadcast_to(vec, (8, 256))


def power_of(top):
    power = 7.0 - jnp.ceil(jnp.log2(jnp.maximum(top, 1e-30)) + 0.01)
    return jnp.clip(power, -100.0, 100.0)


def encode(v, power):
    u = v * jnp.exp2(power)
    q = u * u
    q = q * q
    q = q * q
    q = q * q
    return jnp.where(u < 0, -q, q).astype(BF)


def decode(code, power):
    f = code.astype(F32)
    mag = jnp.exp2(jnp.log2(jnp.abs(f)) * (1.0 / 16.0) - power)
    return jnp.where(f < 0, -mag, mag)


def shifted(v, target):
    edge = jnp.zeros((16, 1, 128), F32)
    f = v.astype(F32)
    target[:, 0:128] = jnp.concatenate([f[:, 1:], edge], 1).astype(BF).reshape(1024, 128)
    target[:, 128:256] = v.reshape(1024, 128)
    target[:, 256:384] = jnp.concatenate([edge, f[:, : COLS - 1]], 1).astype(BF).reshape(1024, 128)


def lane_top(v):
    return power_of(jnp.max(jnp.abs(v), axis=0, keepdims=True))


def corr_kernel(
    h, x_ref, x_edge, p0, p1, p2, p3, take, gh, gho, pre, preo, vec,
    own, m1, m2, m3, evec_ref, xh, gih, both, g_gh, g_pre, wsum,
):
    y, c, _, x, _, lo = place_of()
    lanes = slice(128 * h, 128 * h + 128)
    for k in range(4):
        at = pl.multiple_of((2 * k + c) * 128, 128)
        xh[:, k * 128 : (k + 1) * 128] = x_ref[:, pl.ds(at, 128)]
        edge = pl.ds(pl.multiple_of(17 * COLS * (1 - c), COLS), COLS)
        xh[edge, k * 128 : (k + 1) * 128] = x_edge[:, k * 128 : (k + 1) * 128]
    half = pl.multiple_of(c * 128, 128)
    for d, piece in enumerate((p0, p1, p2, p3)):
        at = pl.multiple_of(lax.rem(y + 4 - d, 4) * 128, 128)
        here = pl.ds(pl.multiple_of(576 * c, 64), 576)
        there = pl.ds(pl.multiple_of(576 * (1 - c), 64), 576)
        gih[here, pl.ds(at, 128)] = piece[0:576, pl.ds(half, 128)]
        gih[there, pl.ds(at, 128)] = take[d, 0:576]
    own_rows = pl.ds(pl.multiple_of(128 - 128 * c, 128), 512)
    both[pl.ds(8 * c, 8)] = gh[own_rows, lanes].reshape(8, COLS, 128)
    both[pl.ds(8 * (1 - c), 8)] = gho[256:768, lanes].reshape(8, COLS, 128)
    shifted(both[...], g_gh)
    both[pl.ds(8 * c, 8)] = pre[0:512, lanes].reshape(8, COLS, 128)
    both[pl.ds(8 * (1 - c), 8)] = preo[0:512, lanes].reshape(8, COLS, 128)
    shifted(both[...], g_pre)
    t_gh, t_pre = g_gh[...].T, g_pre[...].T
    for a in range(3):
        rows = slice(a * COLS, a * COLS + 1024)
        adv = jnp.dot(t_pre, xh[rows], preferred_element_type=F32)
        direct = jnp.dot(t_gh, gih[rows], preferred_element_type=F32)
        total = (adv + GWEIGHT * direct).T
        for b in range(3):
            wsum[3 * a + b] = total[:, b * 128 : b * 128 + 128].reshape(4, 4, 32, 128)
    evec = vec[0:1, pl.ds(half, 128)] + sum_rows(preo[512:528, pl.ds(half, 128)])
    evec_ref[...] = jnp.broadcast_to(evec, (8, 128))
    extra = split_rows(evec)
    at = (x, lo)[h]
    own[...] = wsum[:, :, pl.ds(at, 1)].reshape(1152, 128)
    for d, m in enumerate((m1, m2, m3), 1):
        part = wsum[:, :, pl.ds(lax.rem(at + d, 4), 1)].reshape(1152, 128)
        power = lane_top(part)
        m[0:1152] = encode(part, power)
        m[1152:1168] = rows_block([power] + extra, 16, 128)


def added(own, messages, size):
    t = own[...]
    for m in messages:
        t = t + decode(m[0:size], m[size : size + 16][0:1].astype(F32))
    return t


def label_rows(label):
    tag = jnp.broadcast_to(label[...], (1, 128)).astype(F32)
    high = jnp.floor(tag * (1.0 / 32.0))
    return [high, tag - 32.0 * high]


def first_sum_kernel(h, own, evec_in, label, m1, m2, m3, mine, c1, c2, c3, evec_ref, total):
    _, _, _, x, _, lo = place_of()
    evec = evec_in[0:1]
    for m in (m1, m2, m3):
        evec = evec + sum_rows(m[1152:1168][1:4])
    evec_ref[...] = jnp.broadcast_to(evec, (8, 128))
    extra = split_rows(evec) + label_rows(label)
    at = (lo, x)[h]
    total[...] = added(own, (m1, m2, m3), 1152).reshape(36, 4, 8, 128)
    mine[...] = total[:, pl.ds(at, 1)].reshape(288, 128)
    for d, m in enumerate((c1, c2, c3), 1):
        part = total[:, pl.ds(lax.rem(at + d, 4), 1)].reshape(288, 128)
        power = lane_top(part)
        m[0:288] = encode(part, power)
        m[288:304] = rows_block([power] + extra, 16, 128)


def second_sum_kernel(h, own, evec_in, label, m1, m2, m3, m_ref):
    _, _, _, _, _, lo = place_of()
    t = added(own, (m1, m2, m3), 288)
    power = lane_top(t)
    m_ref[0:288] = encode(t, power)
    rows = [power]
    if h == 0:
        lane = lax.broadcasted_iota(jnp.int32, (1, 128), 1)
        found = [(lo, split_rows(evec_in[0:1]) + label_rows(label))]
        for d, m in enumerate((m1, m2, m3), 1):
            t = m[288:304].astype(F32)
            found.append((lax.rem(lo + 4 - d, 4), [t[k : k + 1] for k in range(1, 6)]))
        zero = jnp.zeros((1, 128), F32)
        for slot in range(4):
            for k in range(3):
                row = zero
                for at, parts in found:
                    row = jnp.where(at == slot, parts[k], row)
                rows.append(row)
        for k in (3, 4):
            row = zero
            for at, parts in found:
                row = jnp.where(lane == at, parts[k], row)
            rows.append(row)
    m_ref[288:304] = rows_block(rows, 16, 128)


def pair_kernel(h, mine, theirs, y0, y1, y2, y3, *rest):
    y, _, _, _, _, _ = place_of()
    total = rest[-1]
    t1 = mine[288:304].astype(F32)
    t2 = theirs[288:304].astype(F32)
    value = decode(mine[0:288], t1[0:1]) + decode(theirs[0:288], t2[0:1])
    total[...] = value.reshape(9, 4, 8, 128)
    for d, target in enumerate((y0, y1, y2, y3)):
        target[...] = total[:, pl.ds(lax.rem(y + d, 4), 1)].reshape(72, 128)
    if h == 0:
        row = lax.broadcasted_iota(jnp.int32, (1000, 128), 0)
        egrad = jnp.zeros((1000, 128), F32)
        for slot in range(4):
            at = 1 + 3 * slot
            vec = sum_rows(t1[at : at + 3]) + sum_rows(t2[at : at + 3])
            tag = 32.0 * t1[13:14, slot : slot + 1] + t1[14:15, slot : slot + 1]
            egrad = egrad + jnp.where(row == tag.astype(jnp.int32), vec, 0.0)
        rest[0][...] = egrad


def code_kernel(y0, y1, y2, y3, m_ref):
    y, _, _, _, _, _ = place_of()
    row = lax.broadcasted_iota(jnp.int32, (8, 128), 0)
    tail = jnp.zeros((8, 128), F32)
    for d, piece in enumerate((y0, y1, y2, y3)):
        at = lax.rem(y + 4 - d, 4)
        v = piece[...]
        power = lane_top(v)
        m_ref[pl.ds(9 * at, 9)] = encode(v, power).reshape(9, 8, 128)
        tail = jnp.where(row == at, power, tail)
    m_ref[36] = tail.astype(BF)


def final_kernel(a0, a1, a2, a3, b0, b1, b2, b3, out_ref):
    _, _, _, x, _, lo = place_of()
    for h, blocks in enumerate(((a0, a1, a2, a3), (b0, b1, b2, b3))):
        for d, block in enumerate(blocks):
            for k in range(4):
                if h == 0:
                    u = 32 * lax.rem(x + 4 - d, 4) + 8 * lax.rem(lo + 4 - k, 4)
                else:
                    u = 32 * lax.rem(lo + 4 - d, 4) + 8 * lax.rem(x + 4 - k, 4)
                rows = pl.ds(pl.multiple_of(u, 8), 8)
                powers = block[k, 36].astype(F32)
                for yy in range(4):
                    lanes = slice(yy * 256 + h * 128, yy * 256 + h * 128 + 128)
                    values = decode(
                        block[k, 9 * yy : 9 * yy + 9], powers[yy : yy + 1].reshape(1, 1, 128)
                    )
                    out_ref[:, rows, lanes] = values


def body(features, kernel, embedding, labels):
    t = lax.axis_index("tensor")
    y, c = t // 2, lax.rem(t, 2)
    first = c == 0

    def by_core(zero, one):
        return jnp.where(first, zero, one)

    def y_all(v):
        got = {d: y_send(v, d) for d in ORDER}
        return [v, got[1], got[2], got[3]]

    def x_all(values):
        got = {d: x_send(values[d - 1], d) for d in ORDER}
        return [got[d] for d in (1, 2, 3)]

    def y_all_of(values):
        got = {d: y_send(values[d - 1], d) for d in ORDER}
        return [got[d] for d in (1, 2, 3)]

    def mine_at(pieces, at, y):
        where = lax.rem(y + 4 - at, 4)
        return jnp.where(
            where == 0,
            pieces[0],
            jnp.where(where == 1, pieces[1], jnp.where(where == 2, pieces[2], pieces[3])),
        )

    def other_at(pieces, at, y):
        return mine_at([pieces[d] for d in range(4)], at, y)

    def z_all(values):
        got = {d: z_send(values[d - 1], Z_STEP[d]) for d in ORDER}
        return [got[d] for d in (1, 2, 3)]

    own = features.reshape(2 * COLS, CHANS)
    kern = kernel.reshape(9, 128, CHANS)
    slices = call(
        pack_kernel,
        [out((9, 128, 256), BF)] * 3,
        [pltpu.SemaphoreType.DMA((3,))],
        kern,
        far=range(1),
        far_out=range(3),
    )
    e_own = jnp.broadcast_to(lax.dynamic_slice_in_dim(embedding, labels[0], 1, 0), (8, 128))
    e_other = core_swap(e_own)
    e = by_core(
        jnp.concatenate([e_own, e_other], 1), jnp.concatenate([e_other, e_own], 1)
    )
    mine = y_all(own)
    kother, own_other = core_swap(kern), core_swap(own)
    *mine, e, kother, own_other, s1, s2, s3 = lax.optimization_barrier(
        (*mine, e, kother, own_other, *slices)
    )
    other = [own_other] + [core_swap(v) for v in mine[1:]]
    *other, s1, s2, s3 = lax.optimization_barrier((*other, s1, s2, s3))
    cols = y_all_of((s1, s2, s3))
    first_rows = jnp.concatenate([mine_at(mine, 0, y), other_at(other, 0, y)[:COLS]], 0)
    last_rows = jnp.concatenate([other_at(other, 3, y)[COLS:], mine_at(mine, 3, y)], 0)
    halo_pairs = []
    for q in range(7):
        for k in range(4):
            halo_pairs.append((q * 8 + 2 * k + 1, (q + 1) * 8 + 2 * k))
            halo_pairs.append(((q + 1) * 8 + 2 * k, q * 8 + 2 * k + 1))
    halo = lax.ppermute(by_core(first_rows, last_rows), ("space", "tensor"), halo_pairs)
    *cols, halo = lax.optimization_barrier((*cols, halo))
    cols_other = [core_swap(v) for v in cols]

    gh, hidden, stat, part, x_rows, w = call(
        hidden_kernel,
        [
            out((640, 256), BF),
            out((8, COLS, 256), F32),
            out((8, 256), F32),
            out((8, 128), F32),
            out((18 * COLS, CHANS), BF),
            out((9, CHANS, 256), BF),
        ],
        [
            pltpu.VMEM((22 * COLS, CHANS), BF),
            pltpu.VMEM((9, CHANS, 256), BF),
            pltpu.VMEM((3, 10, COLS, 256), F32),
            pltpu.SemaphoreType.DMA((19,)),
        ],
        *mine, *other, halo, kern, kother, *cols, *cols_other, e,
        flops=2 * 640 * 9 * 1024 * 256,
        far=range(17),
        far_out=(4, 5),
    )

    p1, p3 = y_send(gh, 1), y_send(gh, 3)
    part = part + lax.ppermute(part, "space", HI_SWAP)
    part, late = lax.optimization_barrier((part, gh[0:320]))
    p2a = y_send(late, 2)
    part = part + x_send(part, 1) + x_send(part, 2) + x_send(part, 3)
    part, late = lax.optimization_barrier((part, gh[320:640]))
    p2b = y_send(late, 2)
    rows = [
        by_core(gh[576:640], gh[0:64]),
        by_core(p1[576:640], p1[0:64]),
        by_core(p2b[256:320], p2a[0:64]),
        by_core(p3[576:640], p3[0:64]),
        by_core(gh[128:640], gh[0:512]),
    ]
    gh_other = core_swap(jnp.concatenate(rows, 0))
    (gi,) = call(
        input_kernel,
        [out((592, 256), BF)],
        [pltpu.VMEM((11, COLS, CHANS), BF), pltpu.VMEM((3, 9, COLS, 256), F32)],
        gh, p1, p2a, p2b, p3, gh_other, kern, kother, part,
        flops=2 * 576 * 9 * 1024 * 256,
    )

    gi_pieces = y_all(gi)
    edge = by_core(x_rows[0:COLS], x_rows[17 * COLS :]).reshape(COLS, 4, 2, 128)
    give_edge = by_core(edge[:, :, 1], edge[:, :, 0]).reshape(COLS, 512)
    rows = []
    for p in gi_pieces:
        low, high = p[0:576, :128], p[0:576, 128:]
        edge = by_core(low[512:576], high[0:64])
        rows.append(jnp.concatenate([by_core(high, low), edge, p[576:592, :128]], 0))
    take = core_swap(jnp.stack(rows))
    x_edge = core_swap(give_edge)
    pre, vec = call(
        second_kernel,
        [out((528, 256), BF), out((8, 256), F32)],
        [pltpu.VMEM((10, COLS, CHANS), BF), pltpu.VMEM((3, 8, COLS, 256), F32)],
        *gi_pieces, take, w, hidden, stat, e,
        flops=2 * 512 * 9 * 1024 * 256,
    )
    pre_other = core_swap(pre)

    def correlate(h):
        own_h, m1, m2, m3, evec = call(
            functools.partial(corr_kernel, h),
            [out((1152, 128), F32)] + [out((1168, 128), BF)] * 3 + [out((8, 128), F32)],
            [
                pltpu.VMEM((18 * COLS, 512), BF),
                pltpu.VMEM((18 * COLS, 512), BF),
                pltpu.VMEM((16, COLS, 128), BF),
                pltpu.VMEM((1024, 384), BF),
                pltpu.VMEM((1024, 384), BF),
                pltpu.VMEM((9, 4, 4, 32, 128), F32),
            ],
            x_rows, x_edge, *gi_pieces, take, gh, gh_other, pre, pre_other, vec,
            flops=2 * 1024 * 9 * 512 * 256,
        )
        return own_h, evec, (m1, m2, m3)

    label = labels.reshape(1, 1)

    def reduced(h, own_h, evec, sent):
        send_first, send_then = ((x_all, z_all), (z_all, x_all))[h]
        got = send_first(sent)
        mine_h, c1, c2, c3, evec = call(
            functools.partial(first_sum_kernel, h),
            [out((288, 128), F32)] + [out((304, 128), BF)] * 3 + [out((8, 128), F32)],
            [pltpu.VMEM((36, 4, 8, 128), F32)],
            own_h, evec, label, *got,
        )
        got = send_then((c1, c2, c3))
        (message,) = call(
            functools.partial(second_sum_kernel, h),
            [out((304, 128), BF)],
            [],
            mine_h, evec, label, *got,
        )
        theirs = z_send(message, 4)
        y0, y1, y2, y3, *egrad = call(
            functools.partial(pair_kernel, h),
            [out((72, 128), F32)] * 4 + [out((1000, 128), F32)] * (1 - h),
            [pltpu.VMEM((9, 4, 8, 128), F32)],
            message, theirs,
        )
        sent = {1: y1, 2: y2, 3: y3}
        got = {d: y_send(sent[d], d) for d in ORDER}
        (code,) = call(code_kernel, [out((37, 8, 128), BF)], [], y0, got[1], got[2], got[3])
        code = jnp.stack([code] + send_then([code] * 3))
        return [code] + send_first([code] * 3), egrad

    first_half = correlate(0)
    second_half = correlate(1)
    codes_a, egrad = reduced(0, *first_half)
    codes_b, _ = reduced(1, *second_half)
    (wtotal,) = call(
        final_kernel,
        [out((9, 128, CHANS), F32)],
        [],
        *codes_a, *codes_b,
    )
    return (wtotal.reshape(3, 3, 128, CHANS), egrad[0])


def solution(mesh):
    placed = (
        P("dp", ("space", "tensor"), None, None),
        P(None, None, "tensor", None),
        P(None, "tensor"),
        P("dp"),
    )
    return jax.shard_map(
        body,
        mesh=mesh,
        in_specs=placed,
        out_specs=(P(None, None, "tensor", None), P(None, "tensor")),
        check_vma=False,
    )
```

```python
import functools
import math

import jax
import jax.numpy as jnp
from jax import lax
from jax.experimental import pallas as pl
from jax.experimental.pallas import tpu as pltpu
from jax.sharding import PartitionSpec as P

r1_factor = 1000.0
BF = jnp.bfloat16
F32 = jnp.float32

IMAGES, HEIGHT, COLS, CHANS = 4, 128, 64, 1024
SCALE = 1.0 / math.sqrt(HEIGHT * COLS * CHANS)
GWEIGHT = r1_factor / IMAGES

CORE_SWAP = [(t, t ^ 1) for t in range(8)]
HI_SWAP = [(s, s ^ 1) for s in range(8)]
X_PAIRS = [(s, s ^ 2) for s in range(8)]
X_FAR = [(s, s ^ 4) for s in range(8)]
ORDER = (2, 1, 3)
Z_STEP = {1: 1, 2: 2, 3: 7}


def y_perm(d):
    return [(2 * y + c, 2 * ((y + d) % 4) + c) for y in range(4) for c in range(2)]


def x_perm(d):
    return [(2 * x + h, 2 * ((x + d) % 4) + h) for x in range(4) for h in range(2)]


def z_perm(d):
    pairs = []
    for z in range(8):
        w = (z + d) % 8
        for x in range(4):
            pairs.append(((z % 4) * 8 + 2 * x + z // 4, (w % 4) * 8 + 2 * x + w // 4))
    return pairs


def core_swap(v):
    return lax.ppermute(v, "tensor", CORE_SWAP)


def y_send(v, d):
    return lax.ppermute(v, "tensor", y_perm(d))


def x_send(v, d):
    return lax.ppermute(v, "space", x_perm(d))


def z_send(v, d):
    return lax.ppermute(v, ("dp", "space"), z_perm(d))


def place_of():
    t = lax.axis_index("tensor")
    s = lax.axis_index("space")
    lo = lax.axis_index("dp")
    return t // 2, lax.rem(t, 2), s, s // 2, 4 * lax.rem(s, 2) + lo, lo


def call(kernel, outs, scratch, *args, flops=0, far=(), far_out=()):
    vm = pl.BlockSpec(memory_space=pltpu.VMEM)
    anywhere = pl.BlockSpec(memory_space=pl.ANY)
    total = sum(math.prod(a.shape) * a.dtype.itemsize for a in args)
    total += sum(math.prod(o.shape) * o.dtype.itemsize for o in outs)
    return pl.pallas_call(
        kernel,
        out_shape=tuple(outs),
        in_specs=[anywhere if k in far else vm for k in range(len(args))],
        out_specs=tuple(anywhere if k in far_out else vm for k in range(len(outs))),
        scratch_shapes=scratch,
        compiler_params=pltpu.CompilerParams(vmem_limit_bytes=48 << 20),
        cost_estimate=pl.CostEstimate(flops=flops, bytes_accessed=total, transcendentals=0),
    )(*args)


def out(shape, dtype):
    return jax.ShapeDtypeStruct(shape, dtype)


def conv_rows(acc, source, rows, weight, contract):
    flat = source.reshape(-1, CHANS)
    for b in range(3):
        total = None
        for a in range(3):
            part = lax.dot_general(
                flat[a * COLS : (a + rows) * COLS],
                weight(a, b),
                (((1,), (contract,)), ((), ())),
                preferred_element_type=F32,
            )
            total = part if total is None else total + part
        acc[b] = total.reshape(rows, COLS, 256)
    edge = jnp.zeros((rows, 1, 256), F32)
    left, right = acc[0], acc[2]
    return (
        acc[1]
        + jnp.concatenate([edge, left[:, : COLS - 1]], 1)
        + jnp.concatenate([right[:, 1:], edge], 1)
    )


def inside_rows(start, rows):
    row = start + lax.broadcasted_iota(jnp.int32, (rows, COLS, 256), 0)
    return (row >= 0) & (row < HEIGHT)


def split_rows(row):
    hi = row.astype(BF).astype(F32)
    mid = (row - hi).astype(BF).astype(F32)
    return [hi, mid, row - hi - mid]


def rows_block(rows, height, width):
    at = lax.broadcasted_iota(jnp.int32, (height, width), 0)
    block = jnp.zeros((height, width), F32)
    for k, row in enumerate(rows):
        block = jnp.where(at == k, row, block)
    return block.astype(BF)


def pack_kernel(kern, m1, m2, m3, sems):
    y, _, _, _, _, _ = place_of()
    jobs = []
    for d, m in enumerate((m1, m2, m3), 1):
        columns = pl.ds(pl.multiple_of(lax.rem(y + d, 4) * 256, 256), 256)
        job = pltpu.make_async_copy(kern.at[:, :, columns], m, sems.at[d - 1])
        job.start()
        jobs.append(job)
    for job in jobs:
        job.wait()


def hidden_kernel(*refs):
    mine, other, (halo, kern, kother) = refs[0:4], refs[4:8], refs[8:11]
    cols, cols_other, e_ref = refs[11:14], refs[14:17], refs[17]
    gh_ref, hid_ref, stat_ref, part_ref, x_out, w_out = refs[18:24]
    x_ref, w_ref, acc, sems = refs[24:28]
    y, c, s, _, _, _ = place_of()
    columns = pl.ds(pl.multiple_of(y * 256, 256), 256)
    copies = []

    def copy(source, target):
        job = pltpu.make_async_copy(source, target, sems.at[len(copies)])
        job.start()
        copies.append(job)

    for d in range(4):
        at = lax.rem(y + 4 - d, 4)
        rows = pl.ds(pl.multiple_of((3 + 4 * at + 2 * c) * COLS, COLS), 2 * COLS)
        copy(mine[d], x_ref.at[rows, :])
        rows = pl.ds(pl.multiple_of((5 + 4 * at - 2 * c) * COLS, COLS), 2 * COLS)
        copy(other[d], x_ref.at[rows, :])
        for core, whole, pieces in ((c, kern, cols), (1 - c, kother, cols_other)):
            block = pl.ds(pl.multiple_of((2 * at + core) * 128, 128), 128)
            source = pieces[d - 1] if d else whole.at[:, :, columns]
            copy(source, w_ref.at[:, block, :])
    copy(halo, x_ref.at[pl.ds(pl.multiple_of(19 * COLS * c, COLS), 3 * COLS), :])
    for job in copies:
        job.wait()
    jobs = [
        pltpu.make_async_copy(x_ref.at[2 * COLS : 20 * COLS], x_out, sems.at[17]),
        pltpu.make_async_copy(w_ref, w_out, sems.at[18]),
    ]
    for job in jobs:
        job.start()
    hidden = conv_rows(acc, x_ref[pl.ds(pl.multiple_of(640 * c, 128), 768)], 10, lambda a, b: w_ref[3 * a + b], 0)
    acc[0] = hidden
    sig = jax.nn.sigmoid(hidden)
    slope = sig * (1.0 + hidden * (1.0 - sig))
    e = e_ref[0:1, :].reshape(1, 1, 256)
    gh = jnp.where(inside_rows(16 * s - 2 + 10 * c, 10), e * slope * SCALE, 0.0)
    gh_ref[...] = gh.astype(BF).reshape(640, 256)
    own = acc[0, pl.ds(2 - 2 * c, 8)]
    hid_ref[...] = own
    act = own * jax.nn.sigmoid(own)
    act_sum = jnp.sum(jnp.sum(act, axis=0), axis=0, keepdims=True)
    part = SCALE * jnp.sum(act_sum * e_ref[0:1, :])
    stat_ref[...] = jnp.broadcast_to(act_sum, (8, 256))
    part_ref[...] = jnp.full((8, 128), part, F32)
    for job in jobs:
        job.wait()


def sum_rows(tail):
    t = tail.astype(F32)
    return t[0:1] + t[1:2] + t[2:3]


def input_kernel(p0, p1, p2a, p2b, p3, swapped, kern, kother, part, gi_ref, full, acc):
    y, c, s, _, _, _ = place_of()
    for d in range(4):
        at = pl.multiple_of(lax.rem(y + 4 - d, 4) * 256, 256)
        if d == 2:
            full[pl.ds(c, 5), :, pl.ds(at, 256)] = p2a[...].reshape(5, COLS, 256)
            full[pl.ds(c + 5, 5), :, pl.ds(at, 256)] = p2b[...].reshape(5, COLS, 256)
        else:
            full[pl.ds(c, 10), :, pl.ds(at, 256)] = (p0, p1, p2a, p3)[d][...].reshape(10, COLS, 256)
        full[pl.ds(10 * (1 - c), 1), :, pl.ds(at, 256)] = swapped[d * 64 : d * 64 + 64].reshape(
            1, COLS, 256
        )

    def weight(a, b):
        tap = 3 * (2 - a) + 2 - b
        return jnp.concatenate([kern[tap], kother[tap]], 0)

    grad = conv_rows(acc, full[...], 9, weight, 1)
    turned = jnp.concatenate([grad[:, :, 128:], grad[:, :, :128]], 2)
    grad = jnp.where(c == 0, grad, turned)
    grad = jnp.where(inside_rows(16 * s - 1 + 9 * c, 9), grad, 0.0)
    gi_ref[0:576] = grad.astype(BF).reshape(576, 256)
    row = jnp.concatenate([part[0:1], part[0:1]], 1)
    gi_ref[576:592] = rows_block(split_rows(row), 16, 256)


def second_kernel(
    p0, p1, p2, p3, swapped, w_ref, hid_ref, stat_ref, e_ref, pre_ref, vec_ref, full, acc
):
    y, c, _, _, _, _ = place_of()
    score = jnp.zeros((1, 128), F32)
    for d, piece in enumerate((p0, p1, p2, p3)):
        score = score + sum_rows(piece[576:592])[:, :128] + sum_rows(swapped[d, 640:656])
        at = pl.multiple_of(lax.rem(y + 4 - d, 4) * 256, 256)
        near = pl.multiple_of(at + 128 * c, 128)
        away = pl.multiple_of(at + 128 * (1 - c), 128)
        full[pl.ds(c, 9), :, pl.ds(at, 256)] = piece[0:576].reshape(9, COLS, 256)
        full[pl.ds(9 * (1 - c), 1), :, pl.ds(near, 128)] = swapped[
            d, pl.ds(pl.multiple_of(8 * COLS * c, COLS), COLS)
        ].reshape(1, COLS, 128)
        full[pl.ds(9 * (1 - c), 1), :, pl.ds(away, 128)] = swapped[d, 576:640].reshape(1, COLS, 128)
    second = conv_rows(acc, full[...], 8, lambda a, b: w_ref[3 * a + b], 0)
    hidden = hid_ref[...]
    sig = jax.nn.sigmoid(hidden)
    slope = sig * (1.0 + hidden * (1.0 - sig))
    curve = sig * (1.0 - sig) * (2.0 + hidden * (1.0 - 2.0 * sig))
    e = e_ref[0:1, :].reshape(1, 1, 256)
    coeff = -jax.nn.sigmoid(-score[0:1, 0:1]) / IMAGES
    c3 = coeff.reshape(1, 1, 1)
    pre = c3 * e * slope * SCALE + GWEIGHT * second * e * curve * SCALE
    pre_ref[0:512] = pre.astype(BF).reshape(512, 256)
    part = jnp.sum(jnp.sum(second * slope, axis=0), axis=0, keepdims=True)
    vec = coeff * SCALE * stat_ref[0:1] + GWEIGHT * SCALE * part
    pre_ref[512:528] = rows_block(split_rows(vec), 16, 256)
    vec_ref[...] = jnp.broadcast_to(vec, (8, 256))


def power_of(top):
    power = 7.0 - jnp.ceil(jnp.log2(jnp.maximum(top, 1e-30)) + 0.01)
    return jnp.clip(power, -100.0, 100.0)


def encode(v, power):
    u = v * jnp.exp2(power)
    q = u * u
    q = q * q
    q = q * q
    q = q * q
    return jnp.where(u < 0, -q, q).astype(BF)


def decode(code, power):
    f = code.astype(F32)
    mag = jnp.exp2(jnp.log2(jnp.abs(f)) * (1.0 / 16.0) - power)
    return jnp.where(f < 0, -mag, mag)


def shifted(v, target):
    edge = jnp.zeros((16, 1, 128), F32)
    f = v.astype(F32)
    target[:, 0:128] = jnp.concatenate([f[:, 1:], edge], 1).astype(BF).reshape(1024, 128)
    target[:, 128:256] = v.reshape(1024, 128)
    target[:, 256:384] = jnp.concatenate([edge, f[:, : COLS - 1]], 1).astype(BF).reshape(1024, 128)


def lane_top(v):
    return power_of(jnp.max(jnp.abs(v), axis=0, keepdims=True))


def corr_kernel(
    h, x_ref, x_edge, p0, p1, p2, p3, take, gh, gho, pre, preo, vec,
    own, m1, m2, m3, evec_ref, xh, gih, both, g_gh, g_pre, wsum,
):
    y, c, _, x, _, lo = place_of()
    lanes = slice(128 * h, 128 * h + 128)
    for k in range(4):
        at = pl.multiple_of((2 * k + c) * 128, 128)
        xh[:, k * 128 : (k + 1) * 128] = x_ref[:, pl.ds(at, 128)]
        edge = pl.ds(pl.multiple_of(17 * COLS * (1 - c), COLS), COLS)
        xh[edge, k * 128 : (k + 1) * 128] = x_edge[:, k * 128 : (k + 1) * 128]
    half = pl.multiple_of(c * 128, 128)
    for d, piece in enumerate((p0, p1, p2, p3)):
        at = pl.multiple_of(lax.rem(y + 4 - d, 4) * 128, 128)
        here = pl.ds(pl.multiple_of(576 * c, 64), 576)
        there = pl.ds(pl.multiple_of(576 * (1 - c), 64), 576)
        gih[here, pl.ds(at, 128)] = piece[0:576, pl.ds(half, 128)]
        gih[there, pl.ds(at, 128)] = take[d, 0:576]
    own_rows = pl.ds(pl.multiple_of(128 - 128 * c, 128), 512)
    both[pl.ds(8 * c, 8)] = gh[own_rows, lanes].reshape(8, COLS, 128)
    both[pl.ds(8 * (1 - c), 8)] = gho[256:768, lanes].reshape(8, COLS, 128)
    shifted(both[...], g_gh)
    both[pl.ds(8 * c, 8)] = pre[0:512, lanes].reshape(8, COLS, 128)
    both[pl.ds(8 * (1 - c), 8)] = preo[0:512, lanes].reshape(8, COLS, 128)
    shifted(both[...], g_pre)
    t_gh, t_pre = g_gh[...].T, g_pre[...].T
    for a in range(3):
        rows = slice(a * COLS, a * COLS + 1024)
        adv = jnp.dot(t_pre, xh[rows], preferred_element_type=F32)
        direct = jnp.dot(t_gh, gih[rows], preferred_element_type=F32)
        total = (adv + GWEIGHT * direct).T
        for b in range(3):
            wsum[3 * a + b] = total[:, b * 128 : b * 128 + 128].reshape(4, 4, 32, 128)
    evec = vec[0:1, pl.ds(half, 128)] + sum_rows(preo[512:528, pl.ds(half, 128)])
    evec_ref[...] = jnp.broadcast_to(evec, (8, 128))
    extra = split_rows(evec)
    at = (x, lo)[h]
    own[...] = wsum[:, :, pl.ds(at, 1)].reshape(1152, 128)
    for d, m in enumerate((m1, m2, m3), 1):
        part = wsum[:, :, pl.ds(lax.rem(at + d, 4), 1)].reshape(1152, 128)
        power = lane_top(part)
        m[0:1152] = encode(part, power)
        m[1152:1168] = rows_block([power] + extra, 16, 128)


def added(own, messages, size):
    t = own[...]
    for m in messages:
        t = t + decode(m[0:size], m[size : size + 16][0:1].astype(F32))
    return t


def label_rows(label):
    tag = jnp.broadcast_to(label[...], (1, 128)).astype(F32)
    high = jnp.floor(tag * (1.0 / 32.0))
    return [high, tag - 32.0 * high]


def first_sum_kernel(h, own, evec_in, label, m1, m2, m3, mine, c1, c2, c3, evec_ref, total):
    _, _, _, x, _, lo = place_of()
    evec = evec_in[0:1]
    for m in (m1, m2, m3):
        evec = evec + sum_rows(m[1152:1168][1:4])
    evec_ref[...] = jnp.broadcast_to(evec, (8, 128))
    extra = split_rows(evec) + label_rows(label)
    at = (lo, x)[h]
    total[...] = added(own, (m1, m2, m3), 1152).reshape(36, 4, 8, 128)
    mine[...] = total[:, pl.ds(at, 1)].reshape(288, 128)
    for d, m in enumerate((c1, c2, c3), 1):
        part = total[:, pl.ds(lax.rem(at + d, 4), 1)].reshape(288, 128)
        power = lane_top(part)
        m[0:288] = encode(part, power)
        m[288:304] = rows_block([power] + extra, 16, 128)


def second_sum_kernel(h, own, evec_in, label, m1, m2, m3, m_ref):
    _, _, _, _, _, lo = place_of()
    t = added(own, (m1, m2, m3), 288)
    power = lane_top(t)
    m_ref[0:288] = encode(t, power)
    rows = [power]
    if h == 0:
        lane = lax.broadcasted_iota(jnp.int32, (1, 128), 1)
        found = [(lo, split_rows(evec_in[0:1]) + label_rows(label))]
        for d, m in enumerate((m1, m2, m3), 1):
            t = m[288:304].astype(F32)
            found.append((lax.rem(lo + 4 - d, 4), [t[k : k + 1] for k in range(1, 6)]))
        zero = jnp.zeros((1, 128), F32)
        for slot in range(4):
            for k in range(3):
                row = zero
                for at, parts in found:
                    row = jnp.where(at == slot, parts[k], row)
                rows.append(row)
        for k in (3, 4):
            row = zero
            for at, parts in found:
                row = jnp.where(lane == at, parts[k], row)
            rows.append(row)
    m_ref[288:304] = rows_block(rows, 16, 128)


def pair_kernel(h, mine, theirs, y0, y1, y2, y3, *rest):
    y, _, _, _, _, _ = place_of()
    total = rest[-1]
    t1 = mine[288:304].astype(F32)
    t2 = theirs[288:304].astype(F32)
    value = decode(mine[0:288], t1[0:1]) + decode(theirs[0:288], t2[0:1])
    total[...] = value.reshape(9, 4, 8, 128)
    for d, target in enumerate((y0, y1, y2, y3)):
        target[...] = total[:, pl.ds(lax.rem(y + d, 4), 1)].reshape(72, 128)
    if h == 0:
        row = lax.broadcasted_iota(jnp.int32, (1000, 128), 0)
        egrad = jnp.zeros((1000, 128), F32)
        for slot in range(4):
            at = 1 + 3 * slot
            vec = sum_rows(t1[at : at + 3]) + sum_rows(t2[at : at + 3])
            tag = 32.0 * t1[13:14, slot : slot + 1] + t1[14:15, slot : slot + 1]
            egrad = egrad + jnp.where(row == tag.astype(jnp.int32), vec, 0.0)
        rest[0][...] = egrad


def code_kernel(y0, y1, y2, y3, m_ref):
    y, _, _, _, _, _ = place_of()
    row = lax.broadcasted_iota(jnp.int32, (8, 128), 0)
    tail = jnp.zeros((8, 128), F32)
    for d, piece in enumerate((y0, y1, y2, y3)):
        at = lax.rem(y + 4 - d, 4)
        v = piece[...]
        power = lane_top(v)
        m_ref[pl.ds(9 * at, 9)] = encode(v, power).reshape(9, 8, 128)
        tail = jnp.where(row == at, power, tail)
    m_ref[36] = tail.astype(BF)


def final_kernel(a0, a1, a2, a3, b0, b1, b2, b3, out_ref):
    _, _, _, x, _, lo = place_of()
    for h, blocks in enumerate(((a0, a1, a2, a3), (b0, b1, b2, b3))):
        for d, block in enumerate(blocks):
            for k in range(4):
                if h == 0:
                    u = 32 * lax.rem(x + 4 - d, 4) + 8 * lax.rem(lo + 4 - k, 4)
                else:
                    u = 32 * lax.rem(lo + 4 - d, 4) + 8 * lax.rem(x + 4 - k, 4)
                rows = pl.ds(pl.multiple_of(u, 8), 8)
                powers = block[k, 36].astype(F32)
                for yy in range(4):
                    lanes = slice(yy * 256 + h * 128, yy * 256 + h * 128 + 128)
                    values = decode(
                        block[k, 9 * yy : 9 * yy + 9], powers[yy : yy + 1].reshape(1, 1, 128)
                    )
                    out_ref[:, rows, lanes] = values


def body(features, kernel, embedding, labels):
    t = lax.axis_index("tensor")
    y, c = t // 2, lax.rem(t, 2)
    first = c == 0

    def by_core(zero, one):
        return jnp.where(first, zero, one)

    def y_all(v):
        got = {d: y_send(v, d) for d in ORDER}
        return [v, got[1], got[2], got[3]]

    def x_all(values):
        got = {d: x_send(values[d - 1], d) for d in ORDER}
        return [got[d] for d in (1, 2, 3)]

    def y_all_of(values):
        got = {d: y_send(values[d - 1], d) for d in ORDER}
        return [got[d] for d in (1, 2, 3)]

    def mine_at(pieces, at, y):
        where = lax.rem(y + 4 - at, 4)
        return jnp.where(
            where == 0,
            pieces[0],
            jnp.where(where == 1, pieces[1], jnp.where(where == 2, pieces[2], pieces[3])),
        )

    def other_at(pieces, at, y):
        return mine_at([pieces[d] for d in range(4)], at, y)

    def z_all(values):
        got = {d: z_send(values[d - 1], Z_STEP[d]) for d in ORDER}
        return [got[d] for d in (1, 2, 3)]

    own = features.reshape(2 * COLS, CHANS)
    kern = kernel.reshape(9, 128, CHANS)
    slices = call(
        pack_kernel,
        [out((9, 128, 256), BF)] * 3,
        [pltpu.SemaphoreType.DMA((3,))],
        kern,
        far=range(1),
        far_out=range(3),
    )
    e_own = jnp.broadcast_to(lax.dynamic_slice_in_dim(embedding, labels[0], 1, 0), (8, 128))
    e_other = core_swap(e_own)
    e = by_core(
        jnp.concatenate([e_own, e_other], 1), jnp.concatenate([e_other, e_own], 1)
    )
    mine = y_all(own)
    kother, own_other = core_swap(kern), core_swap(own)
    *mine, e, kother, own_other, s1, s2, s3 = lax.optimization_barrier(
        (*mine, e, kother, own_other, *slices)
    )
    other = [own_other] + [core_swap(v) for v in mine[1:]]
    *other, s1, s2, s3 = lax.optimization_barrier((*other, s1, s2, s3))
    cols = y_all_of((s1, s2, s3))
    first_rows = jnp.concatenate([mine_at(mine, 0, y), other_at(other, 0, y)[:COLS]], 0)
    last_rows = jnp.concatenate([other_at(other, 3, y)[COLS:], mine_at(mine, 3, y)], 0)
    halo_pairs = []
    for q in range(7):
        for k in range(4):
            halo_pairs.append((q * 8 + 2 * k + 1, (q + 1) * 8 + 2 * k))
            halo_pairs.append(((q + 1) * 8 + 2 * k, q * 8 + 2 * k + 1))
    halo = lax.ppermute(by_core(first_rows, last_rows), ("space", "tensor"), halo_pairs)
    *cols, halo = lax.optimization_barrier((*cols, halo))
    cols_other = [core_swap(v) for v in cols]

    gh, hidden, stat, part, x_rows, w = call(
        hidden_kernel,
        [
            out((640, 256), BF),
            out((8, COLS, 256), F32),
            out((8, 256), F32),
            out((8, 128), F32),
            out((18 * COLS, CHANS), BF),
            out((9, CHANS, 256), BF),
        ],
        [
            pltpu.VMEM((22 * COLS, CHANS), BF),
            pltpu.VMEM((9, CHANS, 256), BF),
            pltpu.VMEM((3, 10, COLS, 256), F32),
            pltpu.SemaphoreType.DMA((19,)),
        ],
        *mine, *other, halo, kern, kother, *cols, *cols_other, e,
        flops=2 * 640 * 9 * 1024 * 256,
        far=range(17),
        far_out=(4, 5),
    )

    p1, p3 = y_send(gh, 1), y_send(gh, 3)
    part = part + lax.ppermute(part, "space", HI_SWAP)
    part, late = lax.optimization_barrier((part, gh[0:320]))
    p2a = y_send(late, 2)
    part = part + x_send(part, 1) + x_send(part, 2) + x_send(part, 3)
    part, late = lax.optimization_barrier((part, gh[320:640]))
    p2b = y_send(late, 2)
    rows = [
        by_core(gh[576:640], gh[0:64]),
        by_core(p1[576:640], p1[0:64]),
        by_core(p2b[256:320], p2a[0:64]),
        by_core(p3[576:640], p3[0:64]),
        by_core(gh[128:640], gh[0:512]),
    ]
    gh_other = core_swap(jnp.concatenate(rows, 0))
    (gi,) = call(
        input_kernel,
        [out((592, 256), BF)],
        [pltpu.VMEM((11, COLS, CHANS), BF), pltpu.VMEM((3, 9, COLS, 256), F32)],
        gh, p1, p2a, p2b, p3, gh_other, kern, kother, part,
        flops=2 * 576 * 9 * 1024 * 256,
    )

    gi_pieces = y_all(gi)
    edge = by_core(x_rows[0:COLS], x_rows[17 * COLS :]).reshape(COLS, 4, 2, 128)
    give_edge = by_core(edge[:, :, 1], edge[:, :, 0]).reshape(COLS, 512)
    rows = []
    for p in gi_pieces:
        low, high = p[0:576, :128], p[0:576, 128:]
        edge = by_core(low[512:576], high[0:64])
        rows.append(jnp.concatenate([by_core(high, low), edge, p[576:592, :128]], 0))
    take = core_swap(jnp.stack(rows))
    x_edge = core_swap(give_edge)
    pre, vec = call(
        second_kernel,
        [out((528, 256), BF), out((8, 256), F32)],
        [pltpu.VMEM((10, COLS, CHANS), BF), pltpu.VMEM((3, 8, COLS, 256), F32)],
        *gi_pieces, take, w, hidden, stat, e,
        flops=2 * 512 * 9 * 1024 * 256,
    )
    pre_other = core_swap(pre)

    def correlate(h, pre):
        own_h, m1, m2, m3, evec = call(
            functools.partial(corr_kernel, h),
            [out((1152, 128), F32)] + [out((1168, 128), BF)] * 3 + [out((8, 128), F32)],
            [
                pltpu.VMEM((18 * COLS, 512), BF),
                pltpu.VMEM((18 * COLS, 512), BF),
                pltpu.VMEM((16, COLS, 128), BF),
                pltpu.VMEM((1024, 384), BF),
                pltpu.VMEM((1024, 384), BF),
                pltpu.VMEM((9, 4, 4, 32, 128), F32),
            ],
            x_rows, x_edge, *gi_pieces, take, gh, gh_other, pre, pre_other, vec,
            flops=2 * 1024 * 9 * 512 * 256,
        )
        return own_h, evec, [m1, m2, m3]

    label = labels.reshape(1, 1)
    send_first, send_then = (x_all, z_all), (z_all, x_all)

    def first_sum(h, own_h, evec, got):
        mine_h, c1, c2, c3, evec = call(
            functools.partial(first_sum_kernel, h),
            [out((288, 128), F32)] + [out((304, 128), BF)] * 3 + [out((8, 128), F32)],
            [pltpu.VMEM((36, 4, 8, 128), F32)],
            own_h, evec, label, *got,
        )
        return mine_h, evec, [c1, c2, c3]

    def second_sum(h, mine_h, evec, got):
        (message,) = call(
            functools.partial(second_sum_kernel, h),
            [out((304, 128), BF)],
            [],
            mine_h, evec, label, *got,
        )
        return message

    def pair_sum(h, message, theirs):
        y0, y1, y2, y3, *egrad = call(
            functools.partial(pair_kernel, h),
            [out((72, 128), F32)] * 4 + [out((1000, 128), F32)] * (1 - h),
            [pltpu.VMEM((9, 4, 8, 128), F32)],
            message, theirs,
        )
        return y0, [y1, y2, y3], egrad

    def code_of(y0, got):
        (code,) = call(code_kernel, [out((37, 8, 128), BF)], [], y0, *got)
        return code

    def y_all_of(values):
        got = {d: y_send(values[d - 1], d) for d in ORDER}
        return [got[d] for d in (1, 2, 3)]

    def after(values, *others):
        tied = lax.optimization_barrier((*values, *others))
        return list(tied[: len(values)])

    f, g = 1, 0
    own_f, evec_f, sent_f = correlate(f, pre)
    got_f = send_first[f](sent_f)
    own_g, evec_g, sent_g = correlate(g, pre)
    got_g = send_first[g](sent_g)
    own_f, evec_f, sent_f = first_sum(f, own_f, evec_f, got_f)
    got_f = send_then[f](sent_f)
    own_g, evec_g, sent_g = first_sum(g, own_g, evec_g, got_g)
    got_g = send_then[g](sent_g)
    message_f = second_sum(f, own_f, evec_f, after(got_f, evec_g))
    theirs_f = z_send(message_f, 4)
    message_g = second_sum(g, own_g, evec_g, got_g)
    theirs_g = z_send(message_g, 4)
    y_f, sent_f, _ = pair_sum(f, message_f, *after([theirs_f], message_g))
    got_f = y_all_of(sent_f)
    y_g, sent_g, egrad = pair_sum(g, message_g, theirs_g)
    got_g = y_all_of(sent_g)
    code_f = code_of(y_f, after(got_f, y_g))
    got_f = send_then[f]([code_f] * 3)
    code_g = code_of(y_g, got_g)
    got_g = send_then[g]([code_g] * 3)
    code_f = jnp.stack([code_f] + after(got_f, code_g))
    codes_f = [code_f] + send_first[f]([code_f] * 3)
    code_g = jnp.stack([code_g] + got_g)
    codes_g = [code_g] + send_first[g]([code_g] * 3)
    codes_a, codes_b = codes_g, codes_f
    (wtotal,) = call(
        final_kernel,
        [out((9, 128, CHANS), F32)],
        [],
        *codes_a, *codes_b,
    )
    return (wtotal.reshape(3, 3, 128, CHANS), egrad[0])


def solution(mesh):
    placed = (
        P("dp", ("space", "tensor"), None, None),
        P(None, None, "tensor", None),
        P(None, "tensor"),
        P("dp"),
    )
    return jax.shard_map(
        body,
        mesh=mesh,
        in_specs=placed,
        out_specs=(P(None, None, "tensor", None), P(None, "tensor")),
        check_vma=False,
    )
```

```python
import functools
import math

import jax
import jax.numpy as jnp
from jax import lax
from jax.experimental import pallas as pl
from jax.experimental.pallas import tpu as pltpu
from jax.sharding import PartitionSpec as P

r1_factor = 1000.0
BF = jnp.bfloat16
F32 = jnp.float32

IMAGES, HEIGHT, COLS, CHANS = 4, 128, 64, 1024
SCALE = 1.0 / math.sqrt(HEIGHT * COLS * CHANS)
GWEIGHT = r1_factor / IMAGES

CORE_SWAP = [(t, t ^ 1) for t in range(8)]
HI_SWAP = [(s, s ^ 1) for s in range(8)]
X_PAIRS = [(s, s ^ 2) for s in range(8)]
X_FAR = [(s, s ^ 4) for s in range(8)]
ORDER = (2, 1, 3)
Z_STEP = {1: 1, 2: 2, 3: 7}


def y_perm(d):
    return [(2 * y + c, 2 * ((y + d) % 4) + c) for y in range(4) for c in range(2)]


def x_perm(d):
    return [(2 * x + h, 2 * ((x + d) % 4) + h) for x in range(4) for h in range(2)]


def z_perm(d):
    pairs = []
    for z in range(8):
        w = (z + d) % 8
        for x in range(4):
            pairs.append(((z % 4) * 8 + 2 * x + z // 4, (w % 4) * 8 + 2 * x + w // 4))
    return pairs


def core_swap(v):
    return lax.ppermute(v, "tensor", CORE_SWAP)


def y_send(v, d):
    return lax.ppermute(v, "tensor", y_perm(d))


def x_send(v, d):
    return lax.ppermute(v, "space", x_perm(d))


def z_send(v, d):
    return lax.ppermute(v, ("dp", "space"), z_perm(d))


def place_of():
    t = lax.axis_index("tensor")
    s = lax.axis_index("space")
    lo = lax.axis_index("dp")
    return t // 2, lax.rem(t, 2), s, s // 2, 4 * lax.rem(s, 2) + lo, lo


def call(kernel, outs, scratch, *args, flops=0, far=(), far_out=(), alias=None):
    vm = pl.BlockSpec(memory_space=pltpu.VMEM)
    anywhere = pl.BlockSpec(memory_space=pl.ANY)
    total = sum(math.prod(a.shape) * a.dtype.itemsize for a in args)
    total += sum(math.prod(o.shape) * o.dtype.itemsize for o in outs)
    return pl.pallas_call(
        kernel,
        out_shape=tuple(outs),
        in_specs=[anywhere if k in far else vm for k in range(len(args))],
        out_specs=tuple(anywhere if k in far_out else vm for k in range(len(outs))),
        scratch_shapes=scratch,
        input_output_aliases=alias or {},
        compiler_params=pltpu.CompilerParams(vmem_limit_bytes=48 << 20),
        cost_estimate=pl.CostEstimate(flops=flops, bytes_accessed=total, transcendentals=0),
    )(*args)


def out(shape, dtype):
    return jax.ShapeDtypeStruct(shape, dtype)


def conv_rows(acc, source, rows, weight, contract):
    flat = source.reshape(-1, CHANS)
    for b in range(3):
        total = None
        for a in range(3):
            part = lax.dot_general(
                flat[a * COLS : (a + rows) * COLS],
                weight(a, b),
                (((1,), (contract,)), ((), ())),
                preferred_element_type=F32,
            )
            total = part if total is None else total + part
        acc[b] = total.reshape(rows, COLS, 256)
    edge = jnp.zeros((rows, 1, 256), F32)
    left, right = acc[0], acc[2]
    return (
        acc[1]
        + jnp.concatenate([edge, left[:, : COLS - 1]], 1)
        + jnp.concatenate([right[:, 1:], edge], 1)
    )


def inside_rows(start, rows):
    row = start + lax.broadcasted_iota(jnp.int32, (rows, COLS, 256), 0)
    return (row >= 0) & (row < HEIGHT)


def split_rows(row):
    hi = row.astype(BF).astype(F32)
    mid = (row - hi).astype(BF).astype(F32)
    return [hi, mid, row - hi - mid]


def rows_block(rows, height, width):
    at = lax.broadcasted_iota(jnp.int32, (height, width), 0)
    block = jnp.zeros((height, width), F32)
    for k, row in enumerate(rows):
        block = jnp.where(at == k, row, block)
    return block.astype(BF)


def pack_kernel(kern, m1, m2, m3, sems):
    y, _, _, _, _, _ = place_of()
    jobs = []
    for d, m in enumerate((m1, m2, m3), 1):
        columns = pl.ds(pl.multiple_of(lax.rem(y + d, 4) * 256, 256), 256)
        job = pltpu.make_async_copy(kern.at[:, :, columns], m, sems.at[d - 1])
        job.start()
        jobs.append(job)
    for job in jobs:
        job.wait()


def hidden_kernel(*refs):
    mine, other, (halo, kern, kother) = refs[0:4], refs[4:8], refs[8:11]
    cols, cols_other, e_ref = refs[11:14], refs[14:17], refs[17]
    gh_ref, hid_ref, stat_ref, part_ref, x_out, w_out = refs[18:24]
    x_ref, w_ref, acc, sems = refs[24:28]
    y, c, s, _, _, _ = place_of()
    columns = pl.ds(pl.multiple_of(y * 256, 256), 256)
    copies = []

    def copy(source, target):
        job = pltpu.make_async_copy(source, target, sems.at[len(copies)])
        job.start()
        copies.append(job)

    for d in range(4):
        at = lax.rem(y + 4 - d, 4)
        rows = pl.ds(pl.multiple_of((3 + 4 * at + 2 * c) * COLS, COLS), 2 * COLS)
        copy(mine[d], x_ref.at[rows, :])
        rows = pl.ds(pl.multiple_of((5 + 4 * at - 2 * c) * COLS, COLS), 2 * COLS)
        copy(other[d], x_ref.at[rows, :])
        for core, whole, pieces in ((c, kern, cols), (1 - c, kother, cols_other)):
            block = pl.ds(pl.multiple_of((2 * at + core) * 128, 128), 128)
            source = pieces[d - 1] if d else whole.at[:, :, columns]
            copy(source, w_ref.at[:, block, :])
    copy(halo, x_ref.at[pl.ds(pl.multiple_of(19 * COLS * c, COLS), 3 * COLS), :])
    for job in copies:
        job.wait()
    jobs = [
        pltpu.make_async_copy(x_ref.at[2 * COLS : 20 * COLS], x_out, sems.at[17]),
        pltpu.make_async_copy(w_ref, w_out, sems.at[18]),
    ]
    for job in jobs:
        job.start()
    hidden = conv_rows(acc, x_ref[pl.ds(pl.multiple_of(640 * c, 128), 768)], 10, lambda a, b: w_ref[3 * a + b], 0)
    acc[0] = hidden
    sig = jax.nn.sigmoid(hidden)
    slope = sig * (1.0 + hidden * (1.0 - sig))
    e = e_ref[0:1, :].reshape(1, 1, 256)
    gh = jnp.where(inside_rows(16 * s - 2 + 10 * c, 10), e * slope * SCALE, 0.0)
    gh_ref[...] = gh.astype(BF).reshape(640, 256)
    own = acc[0, pl.ds(2 - 2 * c, 8)]
    hid_ref[...] = own
    act = own * jax.nn.sigmoid(own)
    act_sum = jnp.sum(jnp.sum(act, axis=0), axis=0, keepdims=True)
    part = SCALE * jnp.sum(act_sum * e_ref[0:1, :])
    stat_ref[...] = jnp.broadcast_to(act_sum, (8, 256))
    part_ref[...] = jnp.full((8, 128), part, F32)
    for job in jobs:
        job.wait()


def sum_rows(tail):
    t = tail.astype(F32)
    return t[0:1] + t[1:2] + t[2:3]


def input_kernel(p0, p1, p2a, p2b, p3, swapped, kern, kother, part, gi_ref, full, acc):
    y, c, s, _, _, _ = place_of()
    for d in range(4):
        at = pl.multiple_of(lax.rem(y + 4 - d, 4) * 256, 256)
        if d == 2:
            full[pl.ds(c, 5), :, pl.ds(at, 256)] = p2a[...].reshape(5, COLS, 256)
            full[pl.ds(c + 5, 5), :, pl.ds(at, 256)] = p2b[...].reshape(5, COLS, 256)
        else:
            full[pl.ds(c, 10), :, pl.ds(at, 256)] = (p0, p1, p2a, p3)[d][...].reshape(10, COLS, 256)
        full[pl.ds(10 * (1 - c), 1), :, pl.ds(at, 256)] = swapped[d * 64 : d * 64 + 64].reshape(
            1, COLS, 256
        )

    def weight(a, b):
        tap = 3 * (2 - a) + 2 - b
        return jnp.concatenate([kern[tap], kother[tap]], 0)

    grad = conv_rows(acc, full[...], 9, weight, 1)
    turned = jnp.concatenate([grad[:, :, 128:], grad[:, :, :128]], 2)
    grad = jnp.where(c == 0, grad, turned)
    grad = jnp.where(inside_rows(16 * s - 1 + 9 * c, 9), grad, 0.0)
    gi_ref[0:576] = grad.astype(BF).reshape(576, 256)
    row = jnp.concatenate([part[0:1], part[0:1]], 1)
    gi_ref[576:592] = rows_block(split_rows(row), 16, 256)


def second_kernel(
    p0, p1, p2, p3, swapped, w_ref, hid_ref, stat_ref, e_ref, pre_ref, vec_ref, full, acc
):
    y, c, _, _, _, _ = place_of()
    score = jnp.zeros((1, 128), F32)
    for d, piece in enumerate((p0, p1, p2, p3)):
        score = score + sum_rows(piece[576:592])[:, :128] + sum_rows(swapped[d, 640:656])
        at = pl.multiple_of(lax.rem(y + 4 - d, 4) * 256, 256)
        near = pl.multiple_of(at + 128 * c, 128)
        away = pl.multiple_of(at + 128 * (1 - c), 128)
        full[pl.ds(c, 9), :, pl.ds(at, 256)] = piece[0:576].reshape(9, COLS, 256)
        full[pl.ds(9 * (1 - c), 1), :, pl.ds(near, 128)] = swapped[
            d, pl.ds(pl.multiple_of(8 * COLS * c, COLS), COLS)
        ].reshape(1, COLS, 128)
        full[pl.ds(9 * (1 - c), 1), :, pl.ds(away, 128)] = swapped[d, 576:640].reshape(1, COLS, 128)
    second = conv_rows(acc, full[...], 8, lambda a, b: w_ref[3 * a + b], 0)
    hidden = hid_ref[...]
    sig = jax.nn.sigmoid(hidden)
    slope = sig * (1.0 + hidden * (1.0 - sig))
    curve = sig * (1.0 - sig) * (2.0 + hidden * (1.0 - 2.0 * sig))
    e = e_ref[0:1, :].reshape(1, 1, 256)
    coeff = -jax.nn.sigmoid(-score[0:1, 0:1]) / IMAGES
    c3 = coeff.reshape(1, 1, 1)
    pre = c3 * e * slope * SCALE + GWEIGHT * second * e * curve * SCALE
    pre_ref[0:512] = pre.astype(BF).reshape(512, 256)
    part = jnp.sum(jnp.sum(second * slope, axis=0), axis=0, keepdims=True)
    vec = coeff * SCALE * stat_ref[0:1] + GWEIGHT * SCALE * part
    pre_ref[512:528] = rows_block(split_rows(vec), 16, 256)
    vec_ref[...] = jnp.broadcast_to(vec, (8, 256))


def power_of(top):
    power = 7.0 - jnp.ceil(jnp.log2(jnp.maximum(top, 1e-30)) + 0.01)
    return jnp.clip(power, -100.0, 100.0)


def encode(v, power):
    u = v * jnp.exp2(power)
    q = u * u
    q = q * q
    q = q * q
    q = q * q
    return jnp.where(u < 0, -q, q).astype(BF)


def decode(code, power):
    f = code.astype(F32)
    mag = jnp.exp2(jnp.log2(jnp.abs(f)) * (1.0 / 16.0) - power)
    return jnp.where(f < 0, -mag, mag)


def shifted(v, target):
    edge = jnp.zeros((16, 1, 128), F32)
    f = v.astype(F32)
    target[:, 0:128] = jnp.concatenate([f[:, 1:], edge], 1).astype(BF).reshape(1024, 128)
    target[:, 128:256] = v.reshape(1024, 128)
    target[:, 256:384] = jnp.concatenate([edge, f[:, : COLS - 1]], 1).astype(BF).reshape(1024, 128)


def lane_top(v):
    return power_of(jnp.max(jnp.abs(v), axis=0, keepdims=True))


def corr_kernel(
    h, x_ref, x_edge, p0, p1, p2, p3, take, gh, gho, pre, preo, vec,
    own, m1, m2, m3, evec_ref, xh, gih, both, g_gh, g_pre, wsum,
):
    y, c, _, x, _, lo = place_of()
    lanes = slice(128 * h, 128 * h + 128)
    for k in range(4):
        at = pl.multiple_of((2 * k + c) * 128, 128)
        xh[:, k * 128 : (k + 1) * 128] = x_ref[:, pl.ds(at, 128)]
        edge = pl.ds(pl.multiple_of(17 * COLS * (1 - c), COLS), COLS)
        xh[edge, k * 128 : (k + 1) * 128] = x_edge[:, k * 128 : (k + 1) * 128]
    half = pl.multiple_of(c * 128, 128)
    for d, piece in enumerate((p0, p1, p2, p3)):
        at = pl.multiple_of(lax.rem(y + 4 - d, 4) * 128, 128)
        here = pl.ds(pl.multiple_of(576 * c, 64), 576)
        there = pl.ds(pl.multiple_of(576 * (1 - c), 64), 576)
        gih[here, pl.ds(at, 128)] = piece[0:576, pl.ds(half, 128)]
        gih[there, pl.ds(at, 128)] = take[d, 0:576]
    own_rows = pl.ds(pl.multiple_of(128 - 128 * c, 128), 512)
    both[pl.ds(8 * c, 8)] = gh[own_rows, lanes].reshape(8, COLS, 128)
    both[pl.ds(8 * (1 - c), 8)] = gho[256:768, lanes].reshape(8, COLS, 128)
    shifted(both[...], g_gh)
    both[pl.ds(8 * c, 8)] = pre[0:512, lanes].reshape(8, COLS, 128)
    both[pl.ds(8 * (1 - c), 8)] = preo[0:512, lanes].reshape(8, COLS, 128)
    shifted(both[...], g_pre)
    t_gh, t_pre = g_gh[...].T, g_pre[...].T
    for a in range(3):
        rows = slice(a * COLS, a * COLS + 1024)
        adv = jnp.dot(t_pre, xh[rows], preferred_element_type=F32)
        direct = jnp.dot(t_gh, gih[rows], preferred_element_type=F32)
        total = (adv + GWEIGHT * direct).T
        for b in range(3):
            wsum[3 * a + b] = total[:, b * 128 : b * 128 + 128].reshape(4, 4, 32, 128)
    evec = vec[0:1, pl.ds(half, 128)] + sum_rows(preo[512:528, pl.ds(half, 128)])
    evec_ref[...] = jnp.broadcast_to(evec, (8, 128))
    extra = split_rows(evec)
    at = (x, lo)[h]
    own[...] = wsum[:, :, pl.ds(at, 1)].reshape(1152, 128)
    for d, m in enumerate((m1, m2, m3), 1):
        part = wsum[:, :, pl.ds(lax.rem(at + d, 4), 1)].reshape(1152, 128)
        power = lane_top(part)
        m[0:1152] = encode(part, power)
        m[1152:1168] = rows_block([power] + extra, 16, 128)


def added(own, messages, size):
    t = own[...]
    for m in messages:
        t = t + decode(m[0:size], m[size : size + 16][0:1].astype(F32))
    return t


def label_rows(label):
    tag = jnp.broadcast_to(label[...], (1, 128)).astype(F32)
    high = jnp.floor(tag * (1.0 / 32.0))
    return [high, tag - 32.0 * high]


def first_sum_kernel(h, own, evec_in, label, m1, m2, m3, mine, c1, c2, c3, evec_ref, total):
    _, _, _, x, _, lo = place_of()
    evec = evec_in[0:1]
    for m in (m1, m2, m3):
        evec = evec + sum_rows(m[1152:1168][1:4])
    evec_ref[...] = jnp.broadcast_to(evec, (8, 128))
    extra = split_rows(evec) + label_rows(label)
    at = (lo, x)[h]
    total[...] = added(own, (m1, m2, m3), 1152).reshape(36, 4, 8, 128)
    mine[...] = total[:, pl.ds(at, 1)].reshape(288, 128)
    for d, m in enumerate((c1, c2, c3), 1):
        part = total[:, pl.ds(lax.rem(at + d, 4), 1)].reshape(288, 128)
        power = lane_top(part)
        m[0:288] = encode(part, power)
        m[288:304] = rows_block([power] + extra, 16, 128)


def second_sum_kernel(h, own, evec_in, label, m1, m2, m3, m_ref):
    _, _, _, _, _, lo = place_of()
    t = added(own, (m1, m2, m3), 288)
    power = lane_top(t)
    m_ref[0:288] = encode(t, power)
    rows = [power]
    if h == 0:
        lane = lax.broadcasted_iota(jnp.int32, (1, 128), 1)
        found = [(lo, split_rows(evec_in[0:1]) + label_rows(label))]
        for d, m in enumerate((m1, m2, m3), 1):
            t = m[288:304].astype(F32)
            found.append((lax.rem(lo + 4 - d, 4), [t[k : k + 1] for k in range(1, 6)]))
        zero = jnp.zeros((1, 128), F32)
        for slot in range(4):
            for k in range(3):
                row = zero
                for at, parts in found:
                    row = jnp.where(at == slot, parts[k], row)
                rows.append(row)
        for k in (3, 4):
            row = zero
            for at, parts in found:
                row = jnp.where(lane == at, parts[k], row)
            rows.append(row)
    m_ref[288:304] = rows_block(rows, 16, 128)


def pair_kernel(mine, theirs, y0, y1, y2, y3, total):
    y, _, _, _, _, _ = place_of()
    t1 = mine[288:304].astype(F32)
    t2 = theirs[288:304].astype(F32)
    value = decode(mine[0:288], t1[0:1]) + decode(theirs[0:288], t2[0:1])
    total[...] = value.reshape(9, 4, 8, 128)
    for d, target in enumerate((y0, y1, y2, y3)):
        target[...] = total[:, pl.ds(lax.rem(y + d, 4), 1)].reshape(72, 128)


def egrad_kernel(mine, theirs, egrad_ref):
    t1 = mine[288:304].astype(F32)
    t2 = theirs[288:304].astype(F32)
    row = lax.broadcasted_iota(jnp.int32, (1000, 128), 0)
    egrad = jnp.zeros((1000, 128), F32)
    for slot in range(4):
        at = 1 + 3 * slot
        vec = sum_rows(t1[at : at + 3]) + sum_rows(t2[at : at + 3])
        tag = 32.0 * t1[13:14, slot : slot + 1] + t1[14:15, slot : slot + 1]
        egrad = egrad + jnp.where(row == tag.astype(jnp.int32), vec, 0.0)
    egrad_ref[...] = egrad


def code_kernel(y0, y1, y2, y3, m_ref):
    y, _, _, _, _, _ = place_of()
    row = lax.broadcasted_iota(jnp.int32, (8, 128), 0)
    tail = jnp.zeros((8, 128), F32)
    for d, piece in enumerate((y0, y1, y2, y3)):
        at = lax.rem(y + 4 - d, 4)
        v = piece[...]
        power = lane_top(v)
        m_ref[pl.ds(9 * at, 9)] = encode(v, power).reshape(9, 8, 128)
        tail = jnp.where(row == at, power, tail)
    m_ref[36] = tail.astype(BF)


def final_kernel(h, *refs):
    blocks, out_ref, values, sems = refs[:4], refs[-3], refs[-2], refs[-1]
    _, _, _, x, _, lo = place_of()
    for d, block in enumerate(blocks):
        for k in range(4):
            if h == 0:
                u = 32 * lax.rem(x + 4 - d, 4) + 8 * lax.rem(lo + 4 - k, 4)
            else:
                u = 32 * lax.rem(lo + 4 - d, 4) + 8 * lax.rem(x + 4 - k, 4)
            rows = pl.ds(pl.multiple_of(u, 8), 8)
            powers = block[k, 36].astype(F32)
            for yy in range(4):
                values[yy, :, rows, :] = decode(
                    block[k, 9 * yy : 9 * yy + 9], powers[yy : yy + 1].reshape(1, 1, 128)
                )
    jobs = []
    for yy in range(4):
        lanes = slice(yy * 256 + h * 128, yy * 256 + h * 128 + 128)
        job = pltpu.make_async_copy(values.at[yy], out_ref.at[:, :, lanes], sems.at[yy])
        job.start()
        jobs.append(job)
    for job in jobs:
        job.wait()


def body(features, kernel, embedding, labels):
    t = lax.axis_index("tensor")
    y, c = t // 2, lax.rem(t, 2)
    first = c == 0

    def by_core(zero, one):
        return jnp.where(first, zero, one)

    def y_all(v):
        got = {d: y_send(v, d) for d in ORDER}
        return [v, got[1], got[2], got[3]]

    def x_all(values):
        got = {d: x_send(values[d - 1], d) for d in ORDER}
        return [got[d] for d in (1, 2, 3)]

    def y_all_of(values):
        got = {d: y_send(values[d - 1], d) for d in ORDER}
        return [got[d] for d in (1, 2, 3)]

    def mine_at(pieces, at, y):
        where = lax.rem(y + 4 - at, 4)
        return jnp.where(
            where == 0,
            pieces[0],
            jnp.where(where == 1, pieces[1], jnp.where(where == 2, pieces[2], pieces[3])),
        )

    def other_at(pieces, at, y):
        return mine_at([pieces[d] for d in range(4)], at, y)

    def z_all(values):
        got = {d: z_send(values[d - 1], Z_STEP[d]) for d in ORDER}
        return [got[d] for d in (1, 2, 3)]

    own = features.reshape(2 * COLS, CHANS)
    kern = kernel.reshape(9, 128, CHANS)
    slices = call(
        pack_kernel,
        [out((9, 128, 256), BF)] * 3,
        [pltpu.SemaphoreType.DMA((3,))],
        kern,
        far=range(1),
        far_out=range(3),
    )
    e_own = jnp.broadcast_to(lax.dynamic_slice_in_dim(embedding, labels[0], 1, 0), (8, 128))
    e_other = core_swap(e_own)
    e = by_core(
        jnp.concatenate([e_own, e_other], 1), jnp.concatenate([e_other, e_own], 1)
    )
    mine = y_all(own)
    kother, own_other = core_swap(kern), core_swap(own)
    *mine, e, kother, own_other, s1, s2, s3 = lax.optimization_barrier(
        (*mine, e, kother, own_other, *slices)
    )
    other = [own_other] + [core_swap(v) for v in mine[1:]]
    *other, s1, s2, s3 = lax.optimization_barrier((*other, s1, s2, s3))
    cols = y_all_of((s1, s2, s3))
    first_rows = jnp.concatenate([mine_at(mine, 0, y), other_at(other, 0, y)[:COLS]], 0)
    last_rows = jnp.concatenate([other_at(other, 3, y)[COLS:], mine_at(mine, 3, y)], 0)
    halo_pairs = []
    for q in range(7):
        for k in range(4):
            halo_pairs.append((q * 8 + 2 * k + 1, (q + 1) * 8 + 2 * k))
            halo_pairs.append(((q + 1) * 8 + 2 * k, q * 8 + 2 * k + 1))
    halo = lax.ppermute(by_core(first_rows, last_rows), ("space", "tensor"), halo_pairs)
    *cols, halo = lax.optimization_barrier((*cols, halo))
    cols_other = [core_swap(v) for v in cols]

    gh, hidden, stat, part, x_rows, w = call(
        hidden_kernel,
        [
            out((640, 256), BF),
            out((8, COLS, 256), F32),
            out((8, 256), F32),
            out((8, 128), F32),
            out((18 * COLS, CHANS), BF),
            out((9, CHANS, 256), BF),
        ],
        [
            pltpu.VMEM((22 * COLS, CHANS), BF),
            pltpu.VMEM((9, CHANS, 256), BF),
            pltpu.VMEM((3, 10, COLS, 256), F32),
            pltpu.SemaphoreType.DMA((19,)),
        ],
        *mine, *other, halo, kern, kother, *cols, *cols_other, e,
        flops=2 * 640 * 9 * 1024 * 256,
        far=range(17),
        far_out=(4, 5),
    )

    p1, p3 = y_send(gh, 1), y_send(gh, 3)
    part = part + lax.ppermute(part, "space", HI_SWAP)
    part, late = lax.optimization_barrier((part, gh[0:320]))
    p2a = y_send(late, 2)
    part = part + x_send(part, 1) + x_send(part, 2) + x_send(part, 3)
    part, late = lax.optimization_barrier((part, gh[320:640]))
    p2b = y_send(late, 2)
    rows = [
        by_core(gh[576:640], gh[0:64]),
        by_core(p1[576:640], p1[0:64]),
        by_core(p2b[256:320], p2a[0:64]),
        by_core(p3[576:640], p3[0:64]),
        by_core(gh[128:640], gh[0:512]),
    ]
    edge = by_core(x_rows[0:COLS], x_rows[17 * COLS :]).reshape(COLS, 4, 2, 128)
    x_edge = core_swap(by_core(edge[:, :, 1], edge[:, :, 0]).reshape(COLS, 512))
    *rows, x_edge = lax.optimization_barrier((*rows, x_edge))
    gh_other = core_swap(jnp.concatenate(rows, 0))
    (gi,) = call(
        input_kernel,
        [out((592, 256), BF)],
        [pltpu.VMEM((11, COLS, CHANS), BF), pltpu.VMEM((3, 9, COLS, 256), F32)],
        gh, p1, p2a, p2b, p3, gh_other, kern, kother, part,
        flops=2 * 576 * 9 * 1024 * 256,
    )

    gi_pieces = y_all(gi)
    rows = []
    for p in gi_pieces:
        low, high = p[0:576, :128], p[0:576, 128:]
        edge = by_core(low[512:576], high[0:64])
        rows.append(jnp.concatenate([by_core(high, low), edge, p[576:592, :128]], 0))
    take = core_swap(jnp.stack(rows))
    pre, vec = call(
        second_kernel,
        [out((528, 256), BF), out((8, 256), F32)],
        [pltpu.VMEM((10, COLS, CHANS), BF), pltpu.VMEM((3, 8, COLS, 256), F32)],
        *gi_pieces, take, w, hidden, stat, e,
        flops=2 * 512 * 9 * 1024 * 256,
    )
    pre_other = core_swap(pre)

    def correlate(h, pre):
        own_h, m1, m2, m3, evec = call(
            functools.partial(corr_kernel, h),
            [out((1152, 128), F32)] + [out((1168, 128), BF)] * 3 + [out((8, 128), F32)],
            [
                pltpu.VMEM((18 * COLS, 512), BF),
                pltpu.VMEM((18 * COLS, 512), BF),
                pltpu.VMEM((16, COLS, 128), BF),
                pltpu.VMEM((1024, 384), BF),
                pltpu.VMEM((1024, 384), BF),
                pltpu.VMEM((9, 4, 4, 32, 128), F32),
            ],
            x_rows, x_edge, *gi_pieces, take, gh, gh_other, pre, pre_other, vec,
            flops=2 * 1024 * 9 * 512 * 256,
        )
        return own_h, evec, [m1, m2, m3]

    label = labels.reshape(1, 1)
    send_first, send_then = (x_all, z_all), (z_all, x_all)

    def first_sum(h, own_h, evec, got):
        mine_h, c1, c2, c3, evec = call(
            functools.partial(first_sum_kernel, h),
            [out((288, 128), F32)] + [out((304, 128), BF)] * 3 + [out((8, 128), F32)],
            [pltpu.VMEM((36, 4, 8, 128), F32)],
            own_h, evec, label, *got,
        )
        return mine_h, evec, [c1, c2, c3]

    def second_sum(h, mine_h, evec, got):
        (message,) = call(
            functools.partial(second_sum_kernel, h),
            [out((304, 128), BF)],
            [],
            mine_h, evec, label, *got,
        )
        return message

    def pair_sum(message, theirs):
        y0, *rest = call(
            pair_kernel,
            [out((72, 128), F32)] * 4,
            [pltpu.VMEM((9, 4, 8, 128), F32)],
            message, theirs,
        )
        return y0, rest

    def code_of(y0, got):
        (code,) = call(code_kernel, [out((37, 8, 128), BF)], [], y0, *got)
        return code

    def y_all_of(values):
        got = {d: y_send(values[d - 1], d) for d in ORDER}
        return [got[d] for d in (1, 2, 3)]

    def after(values, *others):
        tied = lax.optimization_barrier((*values, *others))
        return list(tied[: len(values)])

    f, g = 1, 0
    own_f, evec_f, sent_f = correlate(f, pre)
    got_f = send_first[f](sent_f)
    own_g, evec_g, sent_g = correlate(g, pre)
    got_g = send_first[g](sent_g)
    own_f, evec_f, sent_f = first_sum(f, own_f, evec_f, got_f)
    got_f = send_then[f](sent_f)
    own_g, evec_g, sent_g = first_sum(g, own_g, evec_g, got_g)
    got_g = send_then[g](sent_g)
    message_f = second_sum(f, own_f, evec_f, after(got_f, evec_g))
    theirs_f = z_send(message_f, 4)
    message_g = second_sum(g, own_g, evec_g, got_g)
    theirs_g = z_send(message_g, 4)
    y_f, sent_f = pair_sum(message_f, *after([theirs_f], message_g))
    got_f = y_all_of(sent_f)
    y_g, sent_g = pair_sum(message_g, theirs_g)
    (egrad,) = call(egrad_kernel, [out((1000, 128), F32)], [], message_g, theirs_g)
    got_g = y_all_of(sent_g)
    code_f = code_of(y_f, after(got_f, y_g))
    got_f = send_then[f]([code_f] * 3)
    code_g = code_of(y_g, got_g)
    got_g = send_then[g]([code_g] * 3)
    code_f = jnp.stack([code_f] + after(got_f, code_g))
    codes_f = [code_f] + send_first[f]([code_f] * 3)
    code_g = jnp.stack([code_g] + got_g)
    codes_g = [code_g] + send_first[g]([code_g] * 3)
    wtotal = ()
    for h, codes in ((f, codes_f), (g, codes_g)):
        wtotal = call(
            functools.partial(final_kernel, h),
            [out((9, 128, CHANS), F32)],
            [pltpu.VMEM((4, 9, 128, 128), F32), pltpu.SemaphoreType.DMA((4,))],
            *codes, *wtotal,
            far=range(4, 5),
            far_out=range(1),
            alias={4: 0} if wtotal else None,
        )
    return (wtotal[0].reshape(3, 3, 128, CHANS), egrad)


def solution(mesh):
    placed = (
        P("dp", ("space", "tensor"), None, None),
        P(None, None, "tensor", None),
        P(None, "tensor"),
        P("dp"),
    )
    return jax.shard_map(
        body,
        mesh=mesh,
        in_specs=placed,
        out_specs=(P(None, None, "tensor", None), P(None, "tensor")),
        check_vma=False,
    )
```

```python
import functools
import math

import jax
import jax.numpy as jnp
from jax import lax
from jax.experimental import pallas as pl
from jax.experimental.pallas import tpu as pltpu
from jax.sharding import PartitionSpec as P

r1_factor = 1000.0
BF = jnp.bfloat16
F32 = jnp.float32

IMAGES, HEIGHT, COLS, CHANS = 4, 128, 64, 1024
SCALE = 1.0 / math.sqrt(HEIGHT * COLS * CHANS)
GWEIGHT = r1_factor / IMAGES

CORE_SWAP = [(t, t ^ 1) for t in range(8)]
HI_SWAP = [(s, s ^ 1) for s in range(8)]
X_PAIRS = [(s, s ^ 2) for s in range(8)]
X_FAR = [(s, s ^ 4) for s in range(8)]
ORDER = (2, 1, 3)
Z_STEP = {1: 1, 2: 2, 3: 7}


def y_perm(d):
    return [(2 * y + c, 2 * ((y + d) % 4) + c) for y in range(4) for c in range(2)]


def x_perm(d):
    return [(2 * x + h, 2 * ((x + d) % 4) + h) for x in range(4) for h in range(2)]


def z_perm(d):
    pairs = []
    for z in range(8):
        w = (z + d) % 8
        for x in range(4):
            pairs.append(((z % 4) * 8 + 2 * x + z // 4, (w % 4) * 8 + 2 * x + w // 4))
    return pairs


def core_swap(v):
    return lax.ppermute(v, "tensor", CORE_SWAP)


def y_send(v, d):
    return lax.ppermute(v, "tensor", y_perm(d))


def x_send(v, d):
    return lax.ppermute(v, "space", x_perm(d))


def z_send(v, d):
    return lax.ppermute(v, ("dp", "space"), z_perm(d))


def place_of():
    t = lax.axis_index("tensor")
    s = lax.axis_index("space")
    lo = lax.axis_index("dp")
    return t // 2, lax.rem(t, 2), s, s // 2, 4 * lax.rem(s, 2) + lo, lo


def call(kernel, outs, scratch, *args, flops=0, far=(), far_out=(), alias=None):
    vm = pl.BlockSpec(memory_space=pltpu.VMEM)
    anywhere = pl.BlockSpec(memory_space=pl.ANY)
    total = sum(math.prod(a.shape) * a.dtype.itemsize for a in args)
    total += sum(math.prod(o.shape) * o.dtype.itemsize for o in outs)
    return pl.pallas_call(
        kernel,
        out_shape=tuple(outs),
        in_specs=[anywhere if k in far else vm for k in range(len(args))],
        out_specs=tuple(anywhere if k in far_out else vm for k in range(len(outs))),
        scratch_shapes=scratch,
        input_output_aliases=alias or {},
        compiler_params=pltpu.CompilerParams(vmem_limit_bytes=48 << 20),
        cost_estimate=pl.CostEstimate(flops=flops, bytes_accessed=total, transcendentals=0),
    )(*args)


def out(shape, dtype):
    return jax.ShapeDtypeStruct(shape, dtype)


def conv_rows(acc, source, rows, weight, contract):
    flat = source.reshape(-1, CHANS)
    for b in range(3):
        total = None
        for a in range(3):
            part = lax.dot_general(
                flat[a * COLS : (a + rows) * COLS],
                weight(a, b),
                (((1,), (contract,)), ((), ())),
                preferred_element_type=F32,
            )
            total = part if total is None else total + part
        acc[b] = total.reshape(rows, COLS, 256)
    edge = jnp.zeros((rows, 1, 256), F32)
    left, right = acc[0], acc[2]
    return (
        acc[1]
        + jnp.concatenate([edge, left[:, : COLS - 1]], 1)
        + jnp.concatenate([right[:, 1:], edge], 1)
    )


def inside_rows(start, rows):
    row = start + lax.broadcasted_iota(jnp.int32, (rows, COLS, 256), 0)
    return (row >= 0) & (row < HEIGHT)


def split_rows(row):
    hi = row.astype(BF).astype(F32)
    mid = (row - hi).astype(BF).astype(F32)
    return [hi, mid, row - hi - mid]


def rows_block(rows, height, width):
    at = lax.broadcasted_iota(jnp.int32, (height, width), 0)
    block = jnp.zeros((height, width), F32)
    for k, row in enumerate(rows):
        block = jnp.where(at == k, row, block)
    return block.astype(BF)


def pack_kernel(kern, m1, m2, m3, sems):
    y, _, _, _, _, _ = place_of()
    jobs = []
    for d, m in enumerate((m1, m2, m3), 1):
        columns = pl.ds(pl.multiple_of(lax.rem(y + d, 4) * 256, 256), 256)
        job = pltpu.make_async_copy(kern.at[:, :, columns], m, sems.at[d - 1])
        job.start()
        jobs.append(job)
    for job in jobs:
        job.wait()


def hidden_kernel(*refs):
    mine, other, (halo, kern, kother) = refs[0:4], refs[4:8], refs[8:11]
    cols, cols_other, e_ref = refs[11:14], refs[14:17], refs[17]
    gh_ref, hid_ref, stat_ref, part_ref, edge_ref, x_out, w_out = refs[18:25]
    x_ref, w_ref, acc, sems = refs[25:29]
    y, c, s, _, _, _ = place_of()
    columns = pl.ds(pl.multiple_of(y * 256, 256), 256)
    copies = []

    def copy(source, target):
        job = pltpu.make_async_copy(source, target, sems.at[len(copies)])
        job.start()
        copies.append(job)

    for d in range(4):
        at = lax.rem(y + 4 - d, 4)
        rows = pl.ds(pl.multiple_of((3 + 4 * at + 2 * c) * COLS, COLS), 2 * COLS)
        copy(mine[d], x_ref.at[rows, :])
        rows = pl.ds(pl.multiple_of((5 + 4 * at - 2 * c) * COLS, COLS), 2 * COLS)
        copy(other[d], x_ref.at[rows, :])
        for core, whole, pieces in ((c, kern, cols), (1 - c, kother, cols_other)):
            block = pl.ds(pl.multiple_of((2 * at + core) * 128, 128), 128)
            source = pieces[d - 1] if d else whole.at[:, :, columns]
            copy(source, w_ref.at[:, block, :])
    copy(halo, x_ref.at[pl.ds(pl.multiple_of(19 * COLS * c, COLS), 3 * COLS), :])
    for job in copies:
        job.wait()
    jobs = [
        pltpu.make_async_copy(x_ref.at[2 * COLS : 20 * COLS], x_out, sems.at[17]),
        pltpu.make_async_copy(w_ref, w_out, sems.at[18]),
    ]
    for job in jobs:
        job.start()
    hidden = conv_rows(acc, x_ref[pl.ds(pl.multiple_of(640 * c, 128), 768)], 10, lambda a, b: w_ref[3 * a + b], 0)
    acc[0] = hidden
    sig = jax.nn.sigmoid(hidden)
    slope = sig * (1.0 + hidden * (1.0 - sig))
    e = e_ref[0:1, :].reshape(1, 1, 256)
    gh = jnp.where(inside_rows(16 * s - 2 + 10 * c, 10), e * slope * SCALE, 0.0)
    gh_ref[...] = gh.astype(BF).reshape(640, 256)
    own = acc[0, pl.ds(2 - 2 * c, 8)]
    hid_ref[...] = own
    act = own * jax.nn.sigmoid(own)
    act_sum = jnp.sum(jnp.sum(act, axis=0), axis=0, keepdims=True)
    part = SCALE * jnp.sum(act_sum * e_ref[0:1, :])
    stat_ref[...] = jnp.broadcast_to(act_sum, (8, 256))
    part_ref[...] = jnp.full((8, 128), part, F32)
    edge = pl.ds(pl.multiple_of((2 + 17 * c) * COLS, COLS), COLS)
    for k in range(4):
        at = pl.multiple_of((2 * k + 1 - c) * 128, 128)
        edge_ref[:, k * 128 : (k + 1) * 128] = x_ref[edge, pl.ds(at, 128)]
    for job in jobs:
        job.wait()


def sum_rows(tail):
    t = tail.astype(F32)
    return t[0:1] + t[1:2] + t[2:3]


def input_kernel(p0, p1, p2a, p2b, p3, swapped, kern, kother, part, gi_ref, full, acc):
    y, c, s, _, _, _ = place_of()
    for d in range(4):
        at = pl.multiple_of(lax.rem(y + 4 - d, 4) * 256, 256)
        if d == 2:
            full[pl.ds(c, 5), :, pl.ds(at, 256)] = p2a[...].reshape(5, COLS, 256)
            full[pl.ds(c + 5, 5), :, pl.ds(at, 256)] = p2b[...].reshape(5, COLS, 256)
        else:
            full[pl.ds(c, 10), :, pl.ds(at, 256)] = (p0, p1, p2a, p3)[d][...].reshape(10, COLS, 256)
        full[pl.ds(10 * (1 - c), 1), :, pl.ds(at, 256)] = swapped[d * 64 : d * 64 + 64].reshape(
            1, COLS, 256
        )

    def weight(a, b):
        tap = 3 * (2 - a) + 2 - b
        return jnp.concatenate([kern[tap], kother[tap]], 0)

    grad = conv_rows(acc, full[...], 9, weight, 1)
    turned = jnp.concatenate([grad[:, :, 128:], grad[:, :, :128]], 2)
    grad = jnp.where(c == 0, grad, turned)
    grad = jnp.where(inside_rows(16 * s - 1 + 9 * c, 9), grad, 0.0)
    gi_ref[0:576] = grad.astype(BF).reshape(576, 256)
    row = jnp.concatenate([part[0:1], part[0:1]], 1)
    gi_ref[576:592] = rows_block(split_rows(row), 16, 256)


def second_kernel(
    p0, p1, p2, p3, swapped, w_ref, hid_ref, stat_ref, e_ref, pre_ref, vec_ref, full, acc
):
    y, c, _, _, _, _ = place_of()
    score = jnp.zeros((1, 128), F32)
    for d, piece in enumerate((p0, p1, p2, p3)):
        score = score + sum_rows(piece[576:592])[:, :128] + sum_rows(swapped[d, 640:656])
        at = pl.multiple_of(lax.rem(y + 4 - d, 4) * 256, 256)
        near = pl.multiple_of(at + 128 * c, 128)
        away = pl.multiple_of(at + 128 * (1 - c), 128)
        full[pl.ds(c, 9), :, pl.ds(at, 256)] = piece[0:576].reshape(9, COLS, 256)
        full[pl.ds(9 * (1 - c), 1), :, pl.ds(near, 128)] = swapped[
            d, pl.ds(pl.multiple_of(8 * COLS * c, COLS), COLS)
        ].reshape(1, COLS, 128)
        full[pl.ds(9 * (1 - c), 1), :, pl.ds(away, 128)] = swapped[d, 576:640].reshape(1, COLS, 128)
    second = conv_rows(acc, full[...], 8, lambda a, b: w_ref[3 * a + b], 0)
    hidden = hid_ref[...]
    sig = jax.nn.sigmoid(hidden)
    slope = sig * (1.0 + hidden * (1.0 - sig))
    curve = sig * (1.0 - sig) * (2.0 + hidden * (1.0 - 2.0 * sig))
    e = e_ref[0:1, :].reshape(1, 1, 256)
    coeff = -jax.nn.sigmoid(-score[0:1, 0:1]) / IMAGES
    c3 = coeff.reshape(1, 1, 1)
    pre = c3 * e * slope * SCALE + GWEIGHT * second * e * curve * SCALE
    pre_ref[0:512] = pre.astype(BF).reshape(512, 256)
    part = jnp.sum(jnp.sum(second * slope, axis=0), axis=0, keepdims=True)
    vec = coeff * SCALE * stat_ref[0:1] + GWEIGHT * SCALE * part
    pre_ref[512:528] = rows_block(split_rows(vec), 16, 256)
    vec_ref[...] = jnp.broadcast_to(vec, (8, 256))


def power_of(top):
    power = 7.0 - jnp.ceil(jnp.log2(jnp.maximum(top, 1e-30)) + 0.01)
    return jnp.clip(power, -100.0, 100.0)


def encode(v, power):
    u = v * jnp.exp2(power)
    q = u * u
    q = q * q
    q = q * q
    q = q * q
    return jnp.where(u < 0, -q, q).astype(BF)


def decode(code, power):
    f = code.astype(F32)
    mag = jnp.exp2(jnp.log2(jnp.abs(f)) * (1.0 / 16.0) - power)
    return jnp.where(f < 0, -mag, mag)


def shifted(v, target):
    edge = jnp.zeros((16, 1, 128), F32)
    f = v.astype(F32)
    target[:, 0:128] = jnp.concatenate([f[:, 1:], edge], 1).astype(BF).reshape(1024, 128)
    target[:, 128:256] = v.reshape(1024, 128)
    target[:, 256:384] = jnp.concatenate([edge, f[:, : COLS - 1]], 1).astype(BF).reshape(1024, 128)


def lane_top(v):
    return power_of(jnp.max(jnp.abs(v), axis=0, keepdims=True))


def corr_kernel(
    h, x_ref, x_edge, p0, p1, p2, p3, take, gh, gho, pre, preo, vec,
    own, m1, m2, m3, evec_ref, xh, gih, both, g_gh, g_pre, wsum,
):
    y, c, _, x, _, lo = place_of()
    lanes = slice(128 * h, 128 * h + 128)
    for k in range(4):
        at = pl.multiple_of((2 * k + c) * 128, 128)
        xh[:, k * 128 : (k + 1) * 128] = x_ref[:, pl.ds(at, 128)]
        edge = pl.ds(pl.multiple_of(17 * COLS * (1 - c), COLS), COLS)
        xh[edge, k * 128 : (k + 1) * 128] = x_edge[:, k * 128 : (k + 1) * 128]
    half = pl.multiple_of(c * 128, 128)
    for d, piece in enumerate((p0, p1, p2, p3)):
        at = pl.multiple_of(lax.rem(y + 4 - d, 4) * 128, 128)
        here = pl.ds(pl.multiple_of(576 * c, 64), 576)
        there = pl.ds(pl.multiple_of(576 * (1 - c), 64), 576)
        gih[here, pl.ds(at, 128)] = piece[0:576, pl.ds(half, 128)]
        gih[there, pl.ds(at, 128)] = take[d, 0:576]
    own_rows = pl.ds(pl.multiple_of(128 - 128 * c, 128), 512)
    both[pl.ds(8 * c, 8)] = gh[own_rows, lanes].reshape(8, COLS, 128)
    both[pl.ds(8 * (1 - c), 8)] = gho[256:768, lanes].reshape(8, COLS, 128)
    shifted(both[...], g_gh)
    both[pl.ds(8 * c, 8)] = pre[0:512, lanes].reshape(8, COLS, 128)
    both[pl.ds(8 * (1 - c), 8)] = preo[0:512, lanes].reshape(8, COLS, 128)
    shifted(both[...], g_pre)
    t_gh, t_pre = g_gh[...].T, g_pre[...].T
    for a in range(3):
        rows = slice(a * COLS, a * COLS + 1024)
        adv = jnp.dot(t_pre, xh[rows], preferred_element_type=F32)
        direct = jnp.dot(t_gh, gih[rows], preferred_element_type=F32)
        total = (adv + GWEIGHT * direct).T
        for b in range(3):
            wsum[3 * a + b] = total[:, b * 128 : b * 128 + 128].reshape(4, 4, 32, 128)
    evec = vec[0:1, pl.ds(half, 128)] + sum_rows(preo[512:528, pl.ds(half, 128)])
    evec_ref[...] = jnp.broadcast_to(evec, (8, 128))
    extra = split_rows(evec)
    at = (x, lo)[h]
    own[...] = wsum[:, :, pl.ds(at, 1)].reshape(1152, 128)
    for d, m in enumerate((m1, m2, m3), 1):
        part = wsum[:, :, pl.ds(lax.rem(at + d, 4), 1)].reshape(1152, 128)
        power = lane_top(part)
        m[0:1152] = encode(part, power)
        m[1152:1168] = rows_block([power] + extra, 16, 128)


def added(own, messages, size):
    t = own[...]
    for m in messages:
        t = t + decode(m[0:size], m[size : size + 16][0:1].astype(F32))
    return t


def label_rows(label):
    tag = jnp.broadcast_to(label[...], (1, 128)).astype(F32)
    high = jnp.floor(tag * (1.0 / 32.0))
    return [high, tag - 32.0 * high]


def first_sum_kernel(h, own, evec_in, label, m1, m2, m3, mine, c1, c2, c3, evec_ref, total):
    _, _, _, x, _, lo = place_of()
    evec = evec_in[0:1]
    for m in (m1, m2, m3):
        evec = evec + sum_rows(m[1152:1168][1:4])
    evec_ref[...] = jnp.broadcast_to(evec, (8, 128))
    extra = split_rows(evec) + label_rows(label)
    at = (lo, x)[h]
    total[...] = added(own, (m1, m2, m3), 1152).reshape(36, 4, 8, 128)
    mine[...] = total[:, pl.ds(at, 1)].reshape(288, 128)
    for d, m in enumerate((c1, c2, c3), 1):
        part = total[:, pl.ds(lax.rem(at + d, 4), 1)].reshape(288, 128)
        power = lane_top(part)
        m[0:288] = encode(part, power)
        m[288:304] = rows_block([power] + extra, 16, 128)


def second_sum_kernel(h, own, evec_in, label, m1, m2, m3, m_ref):
    _, _, _, _, _, lo = place_of()
    t = added(own, (m1, m2, m3), 288)
    power = lane_top(t)
    m_ref[0:288] = encode(t, power)
    rows = [power]
    if h == 0:
        lane = lax.broadcasted_iota(jnp.int32, (1, 128), 1)
        found = [(lo, split_rows(evec_in[0:1]) + label_rows(label))]
        for d, m in enumerate((m1, m2, m3), 1):
            t = m[288:304].astype(F32)
            found.append((lax.rem(lo + 4 - d, 4), [t[k : k + 1] for k in range(1, 6)]))
        zero = jnp.zeros((1, 128), F32)
        for slot in range(4):
            for k in range(3):
                row = zero
                for at, parts in found:
                    row = jnp.where(at == slot, parts[k], row)
                rows.append(row)
        for k in (3, 4):
            row = zero
            for at, parts in found:
                row = jnp.where(lane == at, parts[k], row)
            rows.append(row)
    m_ref[288:304] = rows_block(rows, 16, 128)


def pair_kernel(mine, theirs, y0, y1, y2, y3, total):
    y, _, _, _, _, _ = place_of()
    t1 = mine[288:304].astype(F32)
    t2 = theirs[288:304].astype(F32)
    value = decode(mine[0:288], t1[0:1]) + decode(theirs[0:288], t2[0:1])
    total[...] = value.reshape(9, 4, 8, 128)
    for d, target in enumerate((y0, y1, y2, y3)):
        target[...] = total[:, pl.ds(lax.rem(y + d, 4), 1)].reshape(72, 128)


def egrad_kernel(mine, theirs, egrad_ref):
    t1 = mine[288:304].astype(F32)
    t2 = theirs[288:304].astype(F32)
    row = lax.broadcasted_iota(jnp.int32, (1000, 128), 0)
    egrad = jnp.zeros((1000, 128), F32)
    for slot in range(4):
        at = 1 + 3 * slot
        vec = sum_rows(t1[at : at + 3]) + sum_rows(t2[at : at + 3])
        tag = 32.0 * t1[13:14, slot : slot + 1] + t1[14:15, slot : slot + 1]
        egrad = egrad + jnp.where(row == tag.astype(jnp.int32), vec, 0.0)
    egrad_ref[...] = egrad


def code_kernel(y0, y1, y2, y3, m_ref):
    y, _, _, _, _, _ = place_of()
    row = lax.broadcasted_iota(jnp.int32, (8, 128), 0)
    tail = jnp.zeros((8, 128), F32)
    for d, piece in enumerate((y0, y1, y2, y3)):
        at = lax.rem(y + 4 - d, 4)
        v = piece[...]
        power = lane_top(v)
        m_ref[pl.ds(9 * at, 9)] = encode(v, power).reshape(9, 8, 128)
        tail = jnp.where(row == at, power, tail)
    m_ref[36] = tail.astype(BF)


def final_kernel(h, *refs):
    blocks, out_ref, values, sems = refs[:4], refs[-3], refs[-2], refs[-1]
    _, _, _, x, _, lo = place_of()
    for d, block in enumerate(blocks):
        for k in range(4):
            if h == 0:
                u = 32 * lax.rem(x + 4 - d, 4) + 8 * lax.rem(lo + 4 - k, 4)
            else:
                u = 32 * lax.rem(lo + 4 - d, 4) + 8 * lax.rem(x + 4 - k, 4)
            rows = pl.ds(pl.multiple_of(u, 8), 8)
            powers = block[k, 36].astype(F32)
            for yy in range(4):
                values[yy, :, rows, :] = decode(
                    block[k, 9 * yy : 9 * yy + 9], powers[yy : yy + 1].reshape(1, 1, 128)
                )
    jobs = []
    for yy in range(4):
        lanes = slice(yy * 256 + h * 128, yy * 256 + h * 128 + 128)
        job = pltpu.make_async_copy(values.at[yy], out_ref.at[:, :, lanes], sems.at[yy])
        job.start()
        jobs.append(job)
    for job in jobs:
        job.wait()


def body(features, kernel, embedding, labels):
    t = lax.axis_index("tensor")
    y, c = t // 2, lax.rem(t, 2)
    first = c == 0

    def by_core(zero, one):
        return jnp.where(first, zero, one)

    def y_all(v):
        got = {d: y_send(v, d) for d in ORDER}
        return [v, got[1], got[2], got[3]]

    def x_all(values):
        got = {d: x_send(values[d - 1], d) for d in ORDER}
        return [got[d] for d in (1, 2, 3)]

    def y_all_of(values):
        got = {d: y_send(values[d - 1], d) for d in ORDER}
        return [got[d] for d in (1, 2, 3)]

    def mine_at(pieces, at, y):
        where = lax.rem(y + 4 - at, 4)
        return jnp.where(
            where == 0,
            pieces[0],
            jnp.where(where == 1, pieces[1], jnp.where(where == 2, pieces[2], pieces[3])),
        )

    def other_at(pieces, at, y):
        return mine_at([pieces[d] for d in range(4)], at, y)

    def z_all(values):
        got = {d: z_send(values[d - 1], Z_STEP[d]) for d in ORDER}
        return [got[d] for d in (1, 2, 3)]

    own = features.reshape(2 * COLS, CHANS)
    kern = kernel.reshape(9, 128, CHANS)
    slices = call(
        pack_kernel,
        [out((9, 128, 256), BF)] * 3,
        [pltpu.SemaphoreType.DMA((3,))],
        kern,
        far=range(1),
        far_out=range(3),
    )
    e_own = jnp.broadcast_to(lax.dynamic_slice_in_dim(embedding, labels[0], 1, 0), (8, 128))
    e_other = core_swap(e_own)
    e = by_core(
        jnp.concatenate([e_own, e_other], 1), jnp.concatenate([e_other, e_own], 1)
    )
    mine = y_all(own)
    kother, own_other = core_swap(kern), core_swap(own)
    *mine, e, kother, own_other, s1, s2, s3 = lax.optimization_barrier(
        (*mine, e, kother, own_other, *slices)
    )
    other = [own_other] + [core_swap(v) for v in mine[1:]]
    *other, s1, s2, s3 = lax.optimization_barrier((*other, s1, s2, s3))
    cols = y_all_of((s1, s2, s3))
    first_rows = jnp.concatenate([mine_at(mine, 0, y), other_at(other, 0, y)[:COLS]], 0)
    last_rows = jnp.concatenate([other_at(other, 3, y)[COLS:], mine_at(mine, 3, y)], 0)
    halo_pairs = []
    for q in range(7):
        for k in range(4):
            halo_pairs.append((q * 8 + 2 * k + 1, (q + 1) * 8 + 2 * k))
            halo_pairs.append(((q + 1) * 8 + 2 * k, q * 8 + 2 * k + 1))
    halo = lax.ppermute(by_core(first_rows, last_rows), ("space", "tensor"), halo_pairs)
    *cols, halo = lax.optimization_barrier((*cols, halo))
    cols_other = [core_swap(v) for v in cols]

    gh, hidden, stat, part, give_edge, x_rows, w = call(
        hidden_kernel,
        [
            out((640, 256), BF),
            out((8, COLS, 256), F32),
            out((8, 256), F32),
            out((8, 128), F32),
            out((COLS, 512), BF),
            out((18 * COLS, CHANS), BF),
            out((9, CHANS, 256), BF),
        ],
        [
            pltpu.VMEM((22 * COLS, CHANS), BF),
            pltpu.VMEM((9, CHANS, 256), BF),
            pltpu.VMEM((3, 10, COLS, 256), F32),
            pltpu.SemaphoreType.DMA((19,)),
        ],
        *mine, *other, halo, kern, kother, *cols, *cols_other, e,
        flops=2 * 640 * 9 * 1024 * 256,
        far=range(17),
        far_out=(5, 6),
    )

    p1, p3 = y_send(gh, 1), y_send(gh, 3)
    part = part + lax.ppermute(part, "space", HI_SWAP)
    part, late = lax.optimization_barrier((part, gh[0:320]))
    p2a = y_send(late, 2)
    part = part + x_send(part, 1) + x_send(part, 2) + x_send(part, 3)
    part, late = lax.optimization_barrier((part, gh[320:640]))
    p2b = y_send(late, 2)
    rows = [
        by_core(gh[576:640], gh[0:64]),
        by_core(p1[576:640], p1[0:64]),
        by_core(p2b[256:320], p2a[0:64]),
        by_core(p3[576:640], p3[0:64]),
        by_core(gh[128:640], gh[0:512]),
    ]
    gh_other = core_swap(jnp.concatenate(rows, 0))
    (gi,) = call(
        input_kernel,
        [out((592, 256), BF)],
        [pltpu.VMEM((11, COLS, CHANS), BF), pltpu.VMEM((3, 9, COLS, 256), F32)],
        gh, p1, p2a, p2b, p3, gh_other, kern, kother, part,
        flops=2 * 576 * 9 * 1024 * 256,
    )

    gi_pieces = y_all(gi)
    rows = []
    for p in gi_pieces:
        low, high = p[0:576, :128], p[0:576, 128:]
        edge = by_core(low[512:576], high[0:64])
        rows.append(jnp.concatenate([by_core(high, low), edge, p[576:592, :128]], 0))
    take, x_edge = lax.optimization_barrier((core_swap(jnp.stack(rows)), core_swap(give_edge)))
    pre, vec = call(
        second_kernel,
        [out((528, 256), BF), out((8, 256), F32)],
        [pltpu.VMEM((10, COLS, CHANS), BF), pltpu.VMEM((3, 8, COLS, 256), F32)],
        *gi_pieces, take, w, hidden, stat, e,
        flops=2 * 512 * 9 * 1024 * 256,
    )
    pre_other = core_swap(pre)

    def correlate(h, pre):
        own_h, m1, m2, m3, evec = call(
            functools.partial(corr_kernel, h),
            [out((1152, 128), F32)] + [out((1168, 128), BF)] * 3 + [out((8, 128), F32)],
            [
                pltpu.VMEM((18 * COLS, 512), BF),
                pltpu.VMEM((18 * COLS, 512), BF),
                pltpu.VMEM((16, COLS, 128), BF),
                pltpu.VMEM((1024, 384), BF),
                pltpu.VMEM((1024, 384), BF),
                pltpu.VMEM((9, 4, 4, 32, 128), F32),
            ],
            x_rows, x_edge, *gi_pieces, take, gh, gh_other, pre, pre_other, vec,
            flops=2 * 1024 * 9 * 512 * 256,
        )
        return own_h, evec, [m1, m2, m3]

    label = labels.reshape(1, 1)
    send_first, send_then = (x_all, z_all), (z_all, x_all)

    def first_sum(h, own_h, evec, got):
        mine_h, c1, c2, c3, evec = call(
            functools.partial(first_sum_kernel, h),
            [out((288, 128), F32)] + [out((304, 128), BF)] * 3 + [out((8, 128), F32)],
            [pltpu.VMEM((36, 4, 8, 128), F32)],
            own_h, evec, label, *got,
        )
        return mine_h, evec, [c1, c2, c3]

    def second_sum(h, mine_h, evec, got):
        (message,) = call(
            functools.partial(second_sum_kernel, h),
            [out((304, 128), BF)],
            [],
            mine_h, evec, label, *got,
        )
        return message

    def pair_sum(message, theirs):
        y0, *rest = call(
            pair_kernel,
            [out((72, 128), F32)] * 4,
            [pltpu.VMEM((9, 4, 8, 128), F32)],
            message, theirs,
        )
        return y0, rest

    def code_of(y0, got):
        (code,) = call(code_kernel, [out((37, 8, 128), BF)], [], y0, *got)
        return code

    def y_all_of(values):
        got = {d: y_send(values[d - 1], d) for d in ORDER}
        return [got[d] for d in (1, 2, 3)]

    def after(values, *others):
        tied = lax.optimization_barrier((*values, *others))
        return list(tied[: len(values)])

    f, g = 1, 0
    own_f, evec_f, sent_f = correlate(f, pre)
    got_f = send_first[f](sent_f)
    own_g, evec_g, sent_g = correlate(g, pre)
    got_g = send_first[g](sent_g)
    own_f, evec_f, sent_f = first_sum(f, own_f, evec_f, got_f)
    got_f = send_then[f](sent_f)
    own_g, evec_g, sent_g = first_sum(g, own_g, evec_g, got_g)
    got_g = send_then[g](sent_g)
    message_f = second_sum(f, own_f, evec_f, after(got_f, evec_g))
    theirs_f = z_send(message_f, 4)
    message_g = second_sum(g, own_g, evec_g, got_g)
    theirs_g = z_send(message_g, 4)
    y_f, sent_f = pair_sum(message_f, *after([theirs_f], message_g))
    got_f = y_all_of(sent_f)
    y_g, sent_g = pair_sum(message_g, theirs_g)
    (egrad,) = call(egrad_kernel, [out((1000, 128), F32)], [], message_g, theirs_g)
    got_g = y_all_of(sent_g)
    code_f = code_of(y_f, after(got_f, y_g))
    got_f = send_then[f]([code_f] * 3)
    code_g = code_of(y_g, got_g)
    got_g = send_then[g]([code_g] * 3)
    code_f = jnp.stack([code_f] + after(got_f, code_g))
    codes_f = [code_f] + send_first[f]([code_f] * 3)
    code_g = jnp.stack([code_g] + got_g)
    codes_g = [code_g] + send_first[g]([code_g] * 3)
    wtotal = ()
    for h, codes in ((f, codes_f), (g, codes_g)):
        wtotal = call(
            functools.partial(final_kernel, h),
            [out((9, 128, CHANS), F32)],
            [pltpu.VMEM((4, 9, 128, 128), F32), pltpu.SemaphoreType.DMA((4,))],
            *codes, *wtotal,
            far=range(4, 5),
            far_out=range(1),
            alias={4: 0} if wtotal else None,
        )
    return (wtotal[0].reshape(3, 3, 128, CHANS), egrad)


def solution(mesh):
    placed = (
        P("dp", ("space", "tensor"), None, None),
        P(None, None, "tensor", None),
        P(None, "tensor"),
        P("dp"),
    )
    return jax.shard_map(
        body,
        mesh=mesh,
        in_specs=placed,
        out_specs=(P(None, None, "tensor", None), P(None, "tensor")),
        check_vma=False,
    )
```

```python
import functools
import math

import jax
import jax.numpy as jnp
from jax import lax
from jax.experimental import pallas as pl
from jax.experimental.pallas import tpu as pltpu
from jax.sharding import PartitionSpec as P

r1_factor = 1000.0
BF = jnp.bfloat16
F32 = jnp.float32

IMAGES, HEIGHT, COLS, CHANS = 4, 128, 64, 1024
SCALE = 1.0 / math.sqrt(HEIGHT * COLS * CHANS)
GWEIGHT = r1_factor / IMAGES

CORE_SWAP = [(t, t ^ 1) for t in range(8)]
HI_SWAP = [(s, s ^ 1) for s in range(8)]
X_PAIRS = [(s, s ^ 2) for s in range(8)]
X_FAR = [(s, s ^ 4) for s in range(8)]
ORDER = (2, 1, 3)
Z_STEP = {1: 1, 2: 2, 3: 7}


def y_perm(d):
    return [(2 * y + c, 2 * ((y + d) % 4) + c) for y in range(4) for c in range(2)]


def x_perm(d):
    return [(2 * x + h, 2 * ((x + d) % 4) + h) for x in range(4) for h in range(2)]


def z_perm(d):
    pairs = []
    for z in range(8):
        w = (z + d) % 8
        for x in range(4):
            pairs.append(((z % 4) * 8 + 2 * x + z // 4, (w % 4) * 8 + 2 * x + w // 4))
    return pairs


def core_swap(v):
    return lax.ppermute(v, "tensor", CORE_SWAP)


def y_send(v, d):
    return lax.ppermute(v, "tensor", y_perm(d))


def x_send(v, d):
    return lax.ppermute(v, "space", x_perm(d))


def z_send(v, d):
    return lax.ppermute(v, ("dp", "space"), z_perm(d))


def place_of():
    t = lax.axis_index("tensor")
    s = lax.axis_index("space")
    lo = lax.axis_index("dp")
    return t // 2, lax.rem(t, 2), s, s // 2, 4 * lax.rem(s, 2) + lo, lo


def call(kernel, outs, scratch, *args, flops=0, far=(), far_out=(), alias=None):
    vm = pl.BlockSpec(memory_space=pltpu.VMEM)
    anywhere = pl.BlockSpec(memory_space=pl.ANY)
    total = sum(math.prod(a.shape) * a.dtype.itemsize for a in args)
    total += sum(math.prod(o.shape) * o.dtype.itemsize for o in outs)
    return pl.pallas_call(
        kernel,
        out_shape=tuple(outs),
        in_specs=[anywhere if k in far else vm for k in range(len(args))],
        out_specs=tuple(anywhere if k in far_out else vm for k in range(len(outs))),
        scratch_shapes=scratch,
        input_output_aliases=alias or {},
        compiler_params=pltpu.CompilerParams(vmem_limit_bytes=48 << 20),
        cost_estimate=pl.CostEstimate(flops=flops, bytes_accessed=total, transcendentals=0),
    )(*args)


def out(shape, dtype):
    return jax.ShapeDtypeStruct(shape, dtype)


def conv_rows(acc, source, rows, weight, contract):
    flat = source.reshape(-1, CHANS)
    for b in range(3):
        total = None
        for a in range(3):
            part = lax.dot_general(
                flat[a * COLS : (a + rows) * COLS],
                weight(a, b),
                (((1,), (contract,)), ((), ())),
                preferred_element_type=F32,
            )
            total = part if total is None else total + part
        acc[b] = total.reshape(rows, COLS, 256)
    edge = jnp.zeros((rows, 1, 256), F32)
    left, right = acc[0], acc[2]
    return (
        acc[1]
        + jnp.concatenate([edge, left[:, : COLS - 1]], 1)
        + jnp.concatenate([right[:, 1:], edge], 1)
    )


def inside_rows(start, rows):
    row = start + lax.broadcasted_iota(jnp.int32, (rows, COLS, 256), 0)
    return (row >= 0) & (row < HEIGHT)


def split_rows(row):
    hi = row.astype(BF).astype(F32)
    mid = (row - hi).astype(BF).astype(F32)
    return [hi, mid, row - hi - mid]


def rows_block(rows, height, width):
    at = lax.broadcasted_iota(jnp.int32, (height, width), 0)
    block = jnp.zeros((height, width), F32)
    for k, row in enumerate(rows):
        block = jnp.where(at == k, row, block)
    return block.astype(BF)


def pack_kernel(kern, m1, m2, m3, sems):
    y, _, _, _, _, _ = place_of()
    jobs = []
    for d, m in enumerate((m1, m2, m3), 1):
        columns = pl.ds(pl.multiple_of(lax.rem(y + d, 4) * 256, 256), 256)
        job = pltpu.make_async_copy(kern.at[:, :, columns], m, sems.at[d - 1])
        job.start()
        jobs.append(job)
    for job in jobs:
        job.wait()


def hidden_kernel(*refs):
    mine, other, (halo, kern, kother) = refs[0:4], refs[4:8], refs[8:11]
    cols, cols_other, e_ref = refs[11:14], refs[14:17], refs[17]
    gh_ref, hid_ref, stat_ref, part_ref, edge_ref, x_out, w_out = refs[18:25]
    x_ref, w_ref, acc, sems = refs[25:29]
    y, c, s, _, _, _ = place_of()
    columns = pl.ds(pl.multiple_of(y * 256, 256), 256)
    copies = []

    def copy(source, target):
        job = pltpu.make_async_copy(source, target, sems.at[len(copies)])
        job.start()
        copies.append(job)

    for d in range(4):
        at = lax.rem(y + 4 - d, 4)
        rows = pl.ds(pl.multiple_of((3 + 4 * at + 2 * c) * COLS, COLS), 2 * COLS)
        copy(mine[d], x_ref.at[rows, :])
        rows = pl.ds(pl.multiple_of((5 + 4 * at - 2 * c) * COLS, COLS), 2 * COLS)
        copy(other[d], x_ref.at[rows, :])
        for core, whole, pieces in ((c, kern, cols), (1 - c, kother, cols_other)):
            block = pl.ds(pl.multiple_of((2 * at + core) * 128, 128), 128)
            source = pieces[d - 1] if d else whole.at[:, :, columns]
            copy(source, w_ref.at[:, block, :])
    copy(halo, x_ref.at[pl.ds(pl.multiple_of(19 * COLS * c, COLS), 3 * COLS), :])
    for job in copies:
        job.wait()
    jobs = [
        pltpu.make_async_copy(x_ref.at[2 * COLS : 20 * COLS], x_out, sems.at[17]),
        pltpu.make_async_copy(w_ref, w_out, sems.at[18]),
    ]
    for job in jobs:
        job.start()
    hidden = conv_rows(acc, x_ref[pl.ds(pl.multiple_of(640 * c, 128), 768)], 10, lambda a, b: w_ref[3 * a + b], 0)
    acc[0] = hidden
    sig = jax.nn.sigmoid(hidden)
    slope = sig * (1.0 + hidden * (1.0 - sig))
    e = e_ref[0:1, :].reshape(1, 1, 256)
    gh = jnp.where(inside_rows(16 * s - 2 + 10 * c, 10), e * slope * SCALE, 0.0)
    gh_ref[...] = gh.astype(BF).reshape(640, 256)
    own = acc[0, pl.ds(2 - 2 * c, 8)]
    hid_ref[...] = own
    act = own * jax.nn.sigmoid(own)
    act_sum = jnp.sum(jnp.sum(act, axis=0), axis=0, keepdims=True)
    part = SCALE * jnp.sum(act_sum * e_ref[0:1, :])
    stat_ref[...] = jnp.broadcast_to(act_sum, (8, 256))
    part_ref[...] = jnp.full((8, 128), part, F32)
    edge = pl.ds(pl.multiple_of((2 + 17 * c) * COLS, COLS), COLS)
    for k in range(4):
        at = pl.multiple_of((2 * k + 1 - c) * 128, 128)
        edge_ref[:, k * 128 : (k + 1) * 128] = x_ref[edge, pl.ds(at, 128)]
    for job in jobs:
        job.wait()


def sum_rows(tail):
    t = tail.astype(F32)
    return t[0:1] + t[1:2] + t[2:3]


def input_kernel(p0, p1, p2a, p2b, p3, swapped, kern, kother, part, gi_ref, full, acc):
    y, c, s, _, _, _ = place_of()
    for d in range(4):
        at = pl.multiple_of(lax.rem(y + 4 - d, 4) * 256, 256)
        if d == 2:
            full[pl.ds(c, 5), :, pl.ds(at, 256)] = p2a[...].reshape(5, COLS, 256)
            full[pl.ds(c + 5, 5), :, pl.ds(at, 256)] = p2b[...].reshape(5, COLS, 256)
        else:
            full[pl.ds(c, 10), :, pl.ds(at, 256)] = (p0, p1, p2a, p3)[d][...].reshape(10, COLS, 256)
        full[pl.ds(10 * (1 - c), 1), :, pl.ds(at, 256)] = swapped[d * 64 : d * 64 + 64].reshape(
            1, COLS, 256
        )

    def weight(a, b):
        tap = 3 * (2 - a) + 2 - b
        return jnp.concatenate([kern[tap], kother[tap]], 0)

    grad = conv_rows(acc, full[...], 9, weight, 1)
    turned = jnp.concatenate([grad[:, :, 128:], grad[:, :, :128]], 2)
    grad = jnp.where(c == 0, grad, turned)
    grad = jnp.where(inside_rows(16 * s - 1 + 9 * c, 9), grad, 0.0)
    gi_ref[0:576] = grad.astype(BF).reshape(576, 256)
    row = jnp.concatenate([part[0:1], part[0:1]], 1)
    gi_ref[576:592] = rows_block(split_rows(row), 16, 256)


def second_kernel(
    p0, p1, p2, p3, swapped, w_ref, hid_ref, stat_ref, e_ref, pre_ref, vec_ref, full, acc
):
    y, c, _, _, _, _ = place_of()
    score = jnp.zeros((1, 128), F32)
    for d, piece in enumerate((p0, p1, p2, p3)):
        score = score + sum_rows(piece[576:592])[:, :128] + sum_rows(swapped[d, 640:656])
        at = pl.multiple_of(lax.rem(y + 4 - d, 4) * 256, 256)
        near = pl.multiple_of(at + 128 * c, 128)
        away = pl.multiple_of(at + 128 * (1 - c), 128)
        full[pl.ds(c, 9), :, pl.ds(at, 256)] = piece[0:576].reshape(9, COLS, 256)
        full[pl.ds(9 * (1 - c), 1), :, pl.ds(near, 128)] = swapped[
            d, pl.ds(pl.multiple_of(8 * COLS * c, COLS), COLS)
        ].reshape(1, COLS, 128)
        full[pl.ds(9 * (1 - c), 1), :, pl.ds(away, 128)] = swapped[d, 576:640].reshape(1, COLS, 128)
    second = conv_rows(acc, full[...], 8, lambda a, b: w_ref[3 * a + b], 0)
    hidden = hid_ref[...]
    sig = jax.nn.sigmoid(hidden)
    slope = sig * (1.0 + hidden * (1.0 - sig))
    curve = sig * (1.0 - sig) * (2.0 + hidden * (1.0 - 2.0 * sig))
    e = e_ref[0:1, :].reshape(1, 1, 256)
    coeff = -jax.nn.sigmoid(-score[0:1, 0:1]) / IMAGES
    c3 = coeff.reshape(1, 1, 1)
    pre = c3 * e * slope * SCALE + GWEIGHT * second * e * curve * SCALE
    pre_ref[0:512] = pre.astype(BF).reshape(512, 256)
    part = jnp.sum(jnp.sum(second * slope, axis=0), axis=0, keepdims=True)
    vec = coeff * SCALE * stat_ref[0:1] + GWEIGHT * SCALE * part
    pre_ref[512:528] = rows_block(split_rows(vec), 16, 256)
    vec_ref[...] = jnp.broadcast_to(vec, (8, 256))


def power_of(top):
    power = 7.0 - jnp.ceil(jnp.log2(jnp.maximum(top, 1e-30)) + 0.01)
    return jnp.clip(power, -100.0, 100.0)


def encode(v, power):
    u = v * jnp.exp2(power)
    q = u * u
    q = q * q
    q = q * q
    q = q * q
    return jnp.where(u < 0, -q, q).astype(BF)


def decode(code, power):
    f = code.astype(F32)
    mag = jnp.exp2(jnp.log2(jnp.abs(f)) * (1.0 / 16.0) - power)
    return jnp.where(f < 0, -mag, mag)


def shifted(v, target):
    edge = jnp.zeros((16, 1, 128), F32)
    f = v.astype(F32)
    target[:, 0:128] = jnp.concatenate([f[:, 1:], edge], 1).astype(BF).reshape(1024, 128)
    target[:, 128:256] = v.reshape(1024, 128)
    target[:, 256:384] = jnp.concatenate([edge, f[:, : COLS - 1]], 1).astype(BF).reshape(1024, 128)


def lane_top(v):
    return power_of(jnp.max(jnp.abs(v), axis=0, keepdims=True))


def corr_kernel(
    h, x_ref, x_edge, p0, p1, p2, p3, take, gh, gho, pre, preo, vec,
    own, m1, m2, m3, evec_ref, xh, gih, both, g_gh, g_pre, wsum,
):
    y, c, _, x, _, lo = place_of()
    lanes = slice(128 * h, 128 * h + 128)
    for k in range(4):
        at = pl.multiple_of((2 * k + c) * 128, 128)
        xh[:, k * 128 : (k + 1) * 128] = x_ref[:, pl.ds(at, 128)]
        edge = pl.ds(pl.multiple_of(17 * COLS * (1 - c), COLS), COLS)
        xh[edge, k * 128 : (k + 1) * 128] = x_edge[:, k * 128 : (k + 1) * 128]
    half = pl.multiple_of(c * 128, 128)
    for d, piece in enumerate((p0, p1, p2, p3)):
        at = pl.multiple_of(lax.rem(y + 4 - d, 4) * 128, 128)
        here = pl.ds(pl.multiple_of(576 * c, 64), 576)
        there = pl.ds(pl.multiple_of(576 * (1 - c), 64), 576)
        gih[here, pl.ds(at, 128)] = piece[0:576, pl.ds(half, 128)]
        gih[there, pl.ds(at, 128)] = take[d, 0:576]
    own_rows = pl.ds(pl.multiple_of(128 - 128 * c, 128), 512)
    both[pl.ds(8 * c, 8)] = gh[own_rows, lanes].reshape(8, COLS, 128)
    both[pl.ds(8 * (1 - c), 8)] = gho[256:768, lanes].reshape(8, COLS, 128)
    shifted(both[...], g_gh)
    both[pl.ds(8 * c, 8)] = pre[0:512, lanes].reshape(8, COLS, 128)
    both[pl.ds(8 * (1 - c), 8)] = preo[0:512, lanes].reshape(8, COLS, 128)
    shifted(both[...], g_pre)
    t_gh, t_pre = g_gh[...].T, g_pre[...].T
    for a in range(3):
        rows = slice(a * COLS, a * COLS + 1024)
        adv = jnp.dot(t_pre, xh[rows], preferred_element_type=F32)
        direct = jnp.dot(t_gh, gih[rows], preferred_element_type=F32)
        total = (adv + GWEIGHT * direct).T
        for b in range(3):
            wsum[3 * a + b] = total[:, b * 128 : b * 128 + 128].reshape(4, 4, 32, 128)
    evec = vec[0:1, pl.ds(half, 128)] + sum_rows(preo[512:528, pl.ds(half, 128)])
    evec_ref[...] = jnp.broadcast_to(evec, (8, 128))
    extra = split_rows(evec)
    at = (x, lo)[h]
    own[...] = wsum[:, :, pl.ds(at, 1)].reshape(1152, 128)
    for d, m in enumerate((m1, m2, m3), 1):
        part = wsum[:, :, pl.ds(lax.rem(at + d, 4), 1)].reshape(1152, 128)
        power = lane_top(part)
        m[0:1152] = encode(part, power)
        m[1152:1168] = rows_block([power] + extra, 16, 128)


def added(own, messages, size):
    t = own[...]
    for m in messages:
        t = t + decode(m[0:size], m[size : size + 16][0:1].astype(F32))
    return t


def label_rows(label):
    tag = jnp.broadcast_to(label[...], (1, 128)).astype(F32)
    high = jnp.floor(tag * (1.0 / 32.0))
    return [high, tag - 32.0 * high]


def first_sum_kernel(h, own, evec_in, label, m1, m2, m3, mine, c1, c2, c3, evec_ref, total):
    _, _, _, x, _, lo = place_of()
    evec = evec_in[0:1]
    for m in (m1, m2, m3):
        evec = evec + sum_rows(m[1152:1168][1:4])
    evec_ref[...] = jnp.broadcast_to(evec, (8, 128))
    extra = split_rows(evec) + label_rows(label)
    at = (lo, x)[h]
    total[...] = added(own, (m1, m2, m3), 1152).reshape(36, 4, 8, 128)
    mine[...] = total[:, pl.ds(at, 1)].reshape(288, 128)
    for d, m in enumerate((c1, c2, c3), 1):
        part = total[:, pl.ds(lax.rem(at + d, 4), 1)].reshape(288, 128)
        power = lane_top(part)
        m[0:288] = encode(part, power)
        m[288:304] = rows_block([power] + extra, 16, 128)


def second_sum_kernel(h, own, evec_in, label, m1, m2, m3, m_ref):
    _, _, _, _, _, lo = place_of()
    t = added(own, (m1, m2, m3), 288)
    power = lane_top(t)
    m_ref[0:288] = encode(t, power)
    rows = [power]
    if h == 0:
        lane = lax.broadcasted_iota(jnp.int32, (1, 128), 1)
        found = [(lo, split_rows(evec_in[0:1]) + label_rows(label))]
        for d, m in enumerate((m1, m2, m3), 1):
            t = m[288:304].astype(F32)
            found.append((lax.rem(lo + 4 - d, 4), [t[k : k + 1] for k in range(1, 6)]))
        zero = jnp.zeros((1, 128), F32)
        for slot in range(4):
            for k in range(3):
                row = zero
                for at, parts in found:
                    row = jnp.where(at == slot, parts[k], row)
                rows.append(row)
        for k in (3, 4):
            row = zero
            for at, parts in found:
                row = jnp.where(lane == at, parts[k], row)
            rows.append(row)
    m_ref[288:304] = rows_block(rows, 16, 128)


def pair_kernel(mine, theirs, y0, y1, y2, y3, total):
    y, _, _, _, _, _ = place_of()
    t1 = mine[288:304].astype(F32)
    t2 = theirs[288:304].astype(F32)
    value = decode(mine[0:288], t1[0:1]) + decode(theirs[0:288], t2[0:1])
    total[...] = value.reshape(9, 4, 8, 128)
    for d, target in enumerate((y0, y1, y2, y3)):
        target[...] = total[:, pl.ds(lax.rem(y + d, 4), 1)].reshape(72, 128)


def egrad_kernel(mine, theirs, egrad_ref):
    t1 = mine[288:304].astype(F32)
    t2 = theirs[288:304].astype(F32)
    row = lax.broadcasted_iota(jnp.int32, (1000, 128), 0)
    egrad = jnp.zeros((1000, 128), F32)
    for slot in range(4):
        at = 1 + 3 * slot
        vec = sum_rows(t1[at : at + 3]) + sum_rows(t2[at : at + 3])
        tag = 32.0 * t1[13:14, slot : slot + 1] + t1[14:15, slot : slot + 1]
        egrad = egrad + jnp.where(row == tag.astype(jnp.int32), vec, 0.0)
    egrad_ref[...] = egrad


def code_kernel(y0, y1, y2, y3, m_ref):
    y, _, _, _, _, _ = place_of()
    row = lax.broadcasted_iota(jnp.int32, (8, 128), 0)
    tail = jnp.zeros((8, 128), F32)
    for d, piece in enumerate((y0, y1, y2, y3)):
        at = lax.rem(y + 4 - d, 4)
        v = piece[...]
        power = lane_top(v)
        m_ref[pl.ds(9 * at, 9)] = encode(v, power).reshape(9, 8, 128)
        tail = jnp.where(row == at, power, tail)
    m_ref[36] = tail.astype(BF)


def final_kernel(h, *refs):
    blocks, out_ref, values, sems = refs[:4], refs[-3], refs[-2], refs[-1]
    _, _, _, x, _, lo = place_of()
    for d, block in enumerate(blocks):
        for k in range(4):
            if h == 0:
                u = 32 * lax.rem(x + 4 - d, 4) + 8 * lax.rem(lo + 4 - k, 4)
            else:
                u = 32 * lax.rem(lo + 4 - d, 4) + 8 * lax.rem(x + 4 - k, 4)
            rows = pl.ds(pl.multiple_of(u, 8), 8)
            powers = block[k, 36].astype(F32)
            for yy in range(4):
                values[yy, :, rows, :] = decode(
                    block[k, 9 * yy : 9 * yy + 9], powers[yy : yy + 1].reshape(1, 1, 128)
                )
    jobs = []
    for yy in range(4):
        lanes = slice(yy * 256 + h * 128, yy * 256 + h * 128 + 128)
        job = pltpu.make_async_copy(values.at[yy], out_ref.at[:, :, lanes], sems.at[yy])
        job.start()
        jobs.append(job)
    for job in jobs:
        job.wait()


def body(features, kernel, embedding, labels):
    t = lax.axis_index("tensor")
    y, c = t // 2, lax.rem(t, 2)
    first = c == 0

    def by_core(zero, one):
        return jnp.where(first, zero, one)

    def y_all(v):
        got = {d: y_send(v, d) for d in ORDER}
        return [v, got[1], got[2], got[3]]

    def x_all(values):
        got = {d: x_send(values[d - 1], d) for d in ORDER}
        return [got[d] for d in (1, 2, 3)]

    def y_all_of(values):
        got = {d: y_send(values[d - 1], d) for d in ORDER}
        return [got[d] for d in (1, 2, 3)]

    def mine_at(pieces, at, y):
        where = lax.rem(y + 4 - at, 4)
        return jnp.where(
            where == 0,
            pieces[0],
            jnp.where(where == 1, pieces[1], jnp.where(where == 2, pieces[2], pieces[3])),
        )

    def other_at(pieces, at, y):
        return mine_at([pieces[d] for d in range(4)], at, y)

    def z_all(values):
        got = {d: z_send(values[d - 1], Z_STEP[d]) for d in ORDER}
        return [got[d] for d in (1, 2, 3)]

    own = features.reshape(2 * COLS, CHANS)
    kern = kernel.reshape(9, 128, CHANS)
    slices = call(
        pack_kernel,
        [out((9, 128, 256), BF)] * 3,
        [pltpu.SemaphoreType.DMA((3,))],
        kern,
        far=range(1),
        far_out=range(3),
    )
    e_own = jnp.broadcast_to(lax.dynamic_slice_in_dim(embedding, labels[0], 1, 0), (8, 128))
    e_other = core_swap(e_own)
    e = by_core(
        jnp.concatenate([e_own, e_other], 1), jnp.concatenate([e_other, e_own], 1)
    )
    mine = y_all(own)
    kother, own_other = core_swap(kern), core_swap(own)
    *mine, e, kother, own_other, s1, s2, s3 = lax.optimization_barrier(
        (*mine, e, kother, own_other, *slices)
    )
    other = [own_other] + [core_swap(v) for v in mine[1:]]
    *other, s1, s2, s3 = lax.optimization_barrier((*other, s1, s2, s3))
    cols = y_all_of((s1, s2, s3))
    first_rows = jnp.concatenate([mine_at(mine, 0, y), other_at(other, 0, y)[:COLS]], 0)
    last_rows = jnp.concatenate([other_at(other, 3, y)[COLS:], mine_at(mine, 3, y)], 0)
    halo_pairs = []
    for q in range(7):
        for k in range(4):
            halo_pairs.append((q * 8 + 2 * k + 1, (q + 1) * 8 + 2 * k))
            halo_pairs.append(((q + 1) * 8 + 2 * k, q * 8 + 2 * k + 1))
    halo = lax.ppermute(by_core(first_rows, last_rows), ("space", "tensor"), halo_pairs)
    *cols, halo = lax.optimization_barrier((*cols, halo))
    cols_other = [core_swap(v) for v in cols]

    gh, hidden, stat, part, give_edge, x_rows, w = call(
        hidden_kernel,
        [
            out((640, 256), BF),
            out((8, COLS, 256), F32),
            out((8, 256), F32),
            out((8, 128), F32),
            out((COLS, 512), BF),
            out((18 * COLS, CHANS), BF),
            out((9, CHANS, 256), BF),
        ],
        [
            pltpu.VMEM((22 * COLS, CHANS), BF),
            pltpu.VMEM((9, CHANS, 256), BF),
            pltpu.VMEM((3, 10, COLS, 256), F32),
            pltpu.SemaphoreType.DMA((19,)),
        ],
        *mine, *other, halo, kern, kother, *cols, *cols_other, e,
        flops=2 * 640 * 9 * 1024 * 256,
        far=range(17),
        far_out=(5, 6),
    )

    p1, p3 = y_send(gh, 1), y_send(gh, 3)
    part = part + x_send(part, 1) + x_send(part, 2) + x_send(part, 3)
    part, late = lax.optimization_barrier((part, gh[0:320]))
    p2a = y_send(late, 2)
    part = part + lax.ppermute(part, "space", HI_SWAP)
    part, late = lax.optimization_barrier((part, gh[320:640]))
    p2b = y_send(late, 2)
    rows = [
        by_core(gh[576:640], gh[0:64]),
        by_core(p1[576:640], p1[0:64]),
        by_core(p2b[256:320], p2a[0:64]),
        by_core(p3[576:640], p3[0:64]),
        by_core(gh[128:640], gh[0:512]),
    ]
    gh_other = core_swap(jnp.concatenate(rows, 0))
    (gi,) = call(
        input_kernel,
        [out((592, 256), BF)],
        [pltpu.VMEM((11, COLS, CHANS), BF), pltpu.VMEM((3, 9, COLS, 256), F32)],
        gh, p1, p2a, p2b, p3, gh_other, kern, kother, part,
        flops=2 * 576 * 9 * 1024 * 256,
    )

    gi_pieces = y_all(gi)
    rows = []
    for p in gi_pieces:
        low, high = p[0:576, :128], p[0:576, 128:]
        edge = by_core(low[512:576], high[0:64])
        rows.append(jnp.concatenate([by_core(high, low), edge, p[576:592, :128]], 0))
    take, x_edge = lax.optimization_barrier((core_swap(jnp.stack(rows)), core_swap(give_edge)))
    pre, vec = call(
        second_kernel,
        [out((528, 256), BF), out((8, 256), F32)],
        [pltpu.VMEM((10, COLS, CHANS), BF), pltpu.VMEM((3, 8, COLS, 256), F32)],
        *gi_pieces, take, w, hidden, stat, e,
        flops=2 * 512 * 9 * 1024 * 256,
    )
    pre_other = core_swap(pre)

    def correlate(h, pre):
        own_h, m1, m2, m3, evec = call(
            functools.partial(corr_kernel, h),
            [out((1152, 128), F32)] + [out((1168, 128), BF)] * 3 + [out((8, 128), F32)],
            [
                pltpu.VMEM((18 * COLS, 512), BF),
                pltpu.VMEM((18 * COLS, 512), BF),
                pltpu.VMEM((16, COLS, 128), BF),
                pltpu.VMEM((1024, 384), BF),
                pltpu.VMEM((1024, 384), BF),
                pltpu.VMEM((9, 4, 4, 32, 128), F32),
            ],
            x_rows, x_edge, *gi_pieces, take, gh, gh_other, pre, pre_other, vec,
            flops=2 * 1024 * 9 * 512 * 256,
        )
        return own_h, evec, [m1, m2, m3]

    label = labels.reshape(1, 1)
    send_first, send_then = (x_all, z_all), (z_all, x_all)

    def first_sum(h, own_h, evec, got):
        mine_h, c1, c2, c3, evec = call(
            functools.partial(first_sum_kernel, h),
            [out((288, 128), F32)] + [out((304, 128), BF)] * 3 + [out((8, 128), F32)],
            [pltpu.VMEM((36, 4, 8, 128), F32)],
            own_h, evec, label, *got,
        )
        return mine_h, evec, [c1, c2, c3]

    def second_sum(h, mine_h, evec, got):
        (message,) = call(
            functools.partial(second_sum_kernel, h),
            [out((304, 128), BF)],
            [],
            mine_h, evec, label, *got,
        )
        return message

    def pair_sum(message, theirs):
        y0, *rest = call(
            pair_kernel,
            [out((72, 128), F32)] * 4,
            [pltpu.VMEM((9, 4, 8, 128), F32)],
            message, theirs,
        )
        return y0, rest

    def code_of(y0, got):
        (code,) = call(code_kernel, [out((37, 8, 128), BF)], [], y0, *got)
        return code

    def y_all_of(values):
        got = {d: y_send(values[d - 1], d) for d in ORDER}
        return [got[d] for d in (1, 2, 3)]

    def after(values, *others):
        tied = lax.optimization_barrier((*values, *others))
        return list(tied[: len(values)])

    f, g = 1, 0
    own_f, evec_f, sent_f = correlate(f, pre)
    got_f = send_first[f](sent_f)
    own_g, evec_g, sent_g = correlate(g, pre)
    got_g = send_first[g](sent_g)
    own_f, evec_f, sent_f = first_sum(f, own_f, evec_f, got_f)
    got_f = send_then[f](sent_f)
    own_g, evec_g, sent_g = first_sum(g, own_g, evec_g, got_g)
    got_g = send_then[g](sent_g)
    message_f = second_sum(f, own_f, evec_f, after(got_f, evec_g))
    theirs_f = z_send(message_f, 4)
    message_g = second_sum(g, own_g, evec_g, got_g)
    theirs_g = z_send(message_g, 4)
    y_f, sent_f = pair_sum(message_f, *after([theirs_f], message_g))
    got_f = y_all_of(sent_f)
    y_g, sent_g = pair_sum(message_g, theirs_g)
    (egrad,) = call(egrad_kernel, [out((1000, 128), F32)], [], message_g, theirs_g)
    got_g = y_all_of(sent_g)
    code_f = code_of(y_f, after(got_f, y_g))
    got_f = send_then[f]([code_f] * 3)
    code_g = code_of(y_g, got_g)
    got_g = send_then[g]([code_g] * 3)
    code_f = jnp.stack([code_f] + after(got_f, code_g))
    codes_f = [code_f] + send_first[f]([code_f] * 3)
    code_g = jnp.stack([code_g] + got_g)
    codes_g = [code_g] + send_first[g]([code_g] * 3)
    wtotal = ()
    for h, codes in ((f, codes_f), (g, codes_g)):
        wtotal = call(
            functools.partial(final_kernel, h),
            [out((9, 128, CHANS), F32)],
            [pltpu.VMEM((4, 9, 128, 128), F32), pltpu.SemaphoreType.DMA((4,))],
            *codes, *wtotal,
            far=range(4, 5),
            far_out=range(1),
            alias={4: 0} if wtotal else None,
        )
    return (wtotal[0].reshape(3, 3, 128, CHANS), egrad)


def solution(mesh):
    placed = (
        P("dp", ("space", "tensor"), None, None),
        P(None, None, "tensor", None),
        P(None, "tensor"),
        P("dp"),
    )
    return jax.shard_map(
        body,
        mesh=mesh,
        in_specs=placed,
        out_specs=(P(None, None, "tensor", None), P(None, "tensor")),
        check_vma=False,
    )
```
